256 devices in a mesh: seq: 32 (over z, x), head: 8 (over y, core).
Axes of the slice: x: 4, y: 4, z: 8, core: 2. Of those that a mesh axis runs over, the one named last changes fastest.
Arguments:
- queries: bfloat16 [8192, 32, 128], P('seq', 'head'), may hold values from -12 to 12
- keys_in: bfloat16 [8192, 32, 128], P('seq', 'head'), may hold values from -12 to 12
- values: bfloat16 [8192, 32, 128], P('seq', 'head'), may hold values from -6 to 6
- out_proj: bfloat16 [4096, 4096], P(None, 'head'), may hold values from -0.09375 to 0.09375
- out_grad: bfloat16 [8192, 4096], P(('seq', 'head')), may hold values from -24 to 24
- slot_index: int32 [32, 8192], P('head', 'seq'), may hold values from 0 to 12287, as said below
- partner_block: int32 [32, 96], P('head', 'seq'), may hold values from 0 to 95, as said below
Outputs:
- mixed_out: bfloat16 [8192, 4096], P(('seq', 'head'))
- grad_queries: bfloat16 [8192, 32, 128], P('seq', 'head')
- grad_keys: bfloat16 [8192, 32, 128], P('seq', 'head')
- grad_values: bfloat16 [8192, 32, 128], P('seq', 'head')
- grad_proj: bfloat16 [4096, 4096], P('seq', 'head')
The draws below stay inside these ranges and needn't reach their ends.
Inputs may be any that keep to these rules, and one draw needn't show every extreme that they name: `slot_index`: for each head the slots are distinct. The tokens of each index of seq (aligned blocks of 256 tokens) put at most 12 tokens of one head into the blocks of one owner, where owner = slot // 384, and exactly 12 into some owner; every owner receives exactly 256 tokens of each head. `partner_block`: for each head an involution on the blocks: a block is its own partner or is paired with one block of owner o XOR 32 // 2, o being its own owner (owner = block // 3).
All inputs are finite; a program needn't handle non-finite values.
Results may differ from the reference program's by a relative error of at most 0.022.
Values may be sent and summed in bfloat16 or wider, within the bound.
A program may use at most 128 MiB of HBM per device.

```python
import jax
import jax.numpy as jnp
from jax import lax

D = 4096
HD = 128
HEAD_DEV = 4
H = 32
CAP = 128
TOK_DEV = 256
TOKENS = 8192
BLK_DEV = 3
N_HEAD = 8


def draw_queries(key, part):
    key = jax.random.fold_in(key, 31)
    return jnp.clip(jax.random.normal(key, (TOKENS, H, HD), jnp.float32), -4.0, 4.0).astype(jnp.bfloat16)


def draw_keys_in(key, part):
    key = jax.random.fold_in(key, 37)
    return jnp.clip(jax.random.normal(key, (TOKENS, H, HD), jnp.float32), -4.0, 4.0).astype(jnp.bfloat16)


def route_head(head_key):
    peer_total = TOKENS // TOK_DEV
    base_load = TOK_DEV // peer_total
    half_load = base_load // 2
    slot_total = BLK_DEV * CAP
    first_key, second_key, third_key, fourth_key = jax.random.split(head_key, 4)
    lift = jax.random.randint(first_key, (peer_total // 2,), 0, half_load + 1).at[0].set(half_load)
    signed = jnp.concatenate([lift, -lift])
    offsets = signed[jax.random.permutation(second_key, peer_total)]
    source_ids = jnp.arange(peer_total)[:, None]
    target_ids = jnp.arange(peer_total)[None, :]
    counts = base_load + offsets[(target_ids - source_ids) % peer_total]
    upper = jnp.cumsum(counts, axis=1)
    lower = upper - counts
    places = jnp.arange(TOK_DEV)
    owners = jnp.sum((places[None, :, None] >= upper[:, None, :]).astype(jnp.int32), axis=2)
    within = places[None, :] - jnp.take_along_axis(lower, owners, axis=1)
    earlier = jnp.cumsum(counts, axis=0) - counts
    ranking = jnp.take_along_axis(earlier, owners, axis=1) + within
    orders = jax.vmap(lambda sub_key: jax.random.permutation(sub_key, slot_total))(jax.random.split(third_key, peer_total))
    chosen = orders[owners, ranking]
    global_slot = owners * slot_total + chosen
    shuffles = jax.vmap(lambda sub_key: jax.random.permutation(sub_key, TOK_DEV))(jax.random.split(fourth_key, peer_total))
    return jnp.take_along_axis(global_slot, shuffles, axis=1).reshape(TOKENS).astype(jnp.int32)


def draw_slot_index(key, part):
    key = jax.random.fold_in(key, 11)
    return jax.vmap(route_head)(jax.random.split(key, H))


def pair_head(head_key):
    peer_total = TOKENS // TOK_DEV
    half_peers = peer_total // 2
    first_key, second_key, third_key = jax.random.split(head_key, 3)
    levels = jax.random.permutation(first_key, half_peers)
    flags = jax.random.randint(second_key, (half_peers, BLK_DEV), 0, half_peers) <= levels[:, None]
    perms = jax.vmap(lambda sub_key: jax.random.permutation(sub_key, BLK_DEV))(jax.random.split(third_key, half_peers))
    inverse = jnp.argsort(perms, axis=1)
    lower_ids = jnp.arange(half_peers)[:, None]
    block_ids = jnp.arange(BLK_DEV)[None, :]
    lower_pair = jnp.where(flags, (lower_ids + half_peers) * BLK_DEV + perms, lower_ids * BLK_DEV + block_ids)
    upper_flags = jnp.take_along_axis(flags, inverse, axis=1)
    upper_pair = jnp.where(upper_flags, lower_ids * BLK_DEV + inverse, (lower_ids + half_peers) * BLK_DEV + block_ids)
    return jnp.concatenate([lower_pair.reshape(-1), upper_pair.reshape(-1)]).astype(jnp.int32)


def draw_partner_block(key, part):
    key = jax.random.fold_in(key, 23)
    return jax.vmap(pair_head)(jax.random.split(key, H))


def strengthened(drawn, own_key, source, target, shards_of, factor):
    def block_of(dim):
        return (jnp.arange(drawn.shape[dim]) // (drawn.shape[dim] // shards_of)).reshape((-1,) + (1,) * (drawn.ndim - 1 - dim))

    first = jax.random.permutation(own_key, shards_of)[block_of(target)]
    second = (block_of(target) + shards_of // 2) % shards_of
    return jnp.where((block_of(source) == first) | (block_of(source) == second), factor * drawn, drawn)


def shard_levels(rng, shape, cuts, smallest, largest):
    loudness, own = 1.0, jax.random.fold_in(rng, 6)
    for dim, parts in cuts:
        steps = jnp.exp(jax.random.uniform(jax.random.fold_in(own, dim), (parts,), jnp.float32, smallest / len(cuts), largest / len(cuts)))
        loudness = loudness * jnp.repeat(steps, shape[dim] // parts).reshape([-1 if axis == dim else 1 for axis in range(len(shape))])
    return loudness


def centred(own_key, shape, deviation, limit, cuts=(), kind=jnp.bfloat16):
    array = jax.random.normal(own_key, shape, jnp.float32) * deviation
    if len(cuts) > 0:
        array = shard_levels(own_key, shape, cuts, -0.22, 0.18) * array
    return jnp.clip(array, min=-limit, max=limit).astype(kind)


def gaussian_with(rng, dims, width, limit, cuts, heavy, held_as=jnp.bfloat16):
    drawn = width * jax.random.normal(rng, dims, jnp.float32)
    if cuts:
        drawn = drawn * shard_levels(rng, dims, cuts, -0.22, 0.18)
    return jnp.clip(strengthened(drawn, jax.random.fold_in(rng, 3), *heavy), -limit, limit).astype(held_as)


def setup_inputs(seed: int = 0) -> dict:
    streams_of = jax.random.split(jax.random.key(seed), 8)
    return {
        "queries": draw_queries(jax.random.fold_in(streams_of[7], 71), 0),
        "keys_in": draw_keys_in(jax.random.fold_in(streams_of[7], 71), 0),
        "values": centred(streams_of[2], (TOKENS, H, HD), 1.0, 6.0, ((0, 32), (1, 8))),
        "out_proj": centred(streams_of[3], (D, H * HD), (H * HD) ** -0.5, 0.09375, ((1, 8),)),
        "out_grad": gaussian_with(streams_of[4], (TOKENS, D), 1.0, 24.0, ((0, 256),), (0, 1, 256, 6.0)),
        "slot_index": draw_slot_index(jax.random.fold_in(streams_of[7], 71), 0),
        "partner_block": draw_partner_block(jax.random.fold_in(streams_of[7], 71), 0),
    }


def low_copy(source):
    return lax.optimization_barrier(source.astype(jnp.bfloat16))


def head_pass(items):
    query_rows, key_rows, value_rows, grad_rows, slot_of, partner_of = items
    block_total = partner_of.shape[0]
    slot_total = block_total * CAP

    def to_blocks(source):
        slotted = jnp.zeros((slot_total, source.shape[1]), source.dtype).at[slot_of].set(source)
        return slotted.reshape(block_total, CAP, source.shape[1]).astype(jnp.float32)

    query_block_rows = to_blocks(query_rows)
    key_blocks = to_blocks(key_rows)
    value_blocks = to_blocks(value_rows)
    block_gradient = to_blocks(grad_rows)
    fill = jnp.zeros((slot_total,), jnp.float32).at[slot_of].set(1.0).reshape(block_total, CAP)
    own_index = jnp.arange(block_total, dtype=jnp.int32)
    is_split = (partner_of != own_index).astype(jnp.float32)
    bucket_keys = jnp.concatenate([key_blocks, key_blocks[partner_of]], axis=1)
    bucket_values = jnp.concatenate([value_blocks, value_blocks[partner_of]], axis=1)
    live_mask = jnp.concatenate([fill, fill[partner_of] * is_split[:, None]], axis=1)
    scale_factor = HD ** -0.5
    attention_scores = jnp.einsum("jxp,jwp->jxw", query_block_rows, bucket_keys) * scale_factor
    live = live_mask[:, None, :]
    attention_scores = jnp.where(live > 0, attention_scores, -1e30)
    row_top = jnp.max(attention_scores, axis=-1, keepdims=True)
    weights = jnp.exp(attention_scores - row_top) * live
    row_sum = jnp.sum(weights, axis=-1, keepdims=True) + (1.0 - fill[:, :, None])
    attn_probs = weights / row_sum * fill[:, :, None]
    lower_probabilities = low_copy(attn_probs).astype(jnp.float32)
    attended_output = jnp.einsum("fzu,fua->fza", lower_probabilities, bucket_values).astype(jnp.bfloat16)
    probability_gradient = jnp.einsum("jxp,jwp->jxw", block_gradient, bucket_values)
    row_inner = jnp.sum(attn_probs * probability_gradient, axis=-1, keepdims=True)
    score_gradient = low_copy(attn_probs * (probability_gradient - row_inner)).astype(jnp.float32)
    query_gradient = (jnp.einsum("fzu,fua->fza", score_gradient, bucket_keys) * scale_factor).astype(jnp.bfloat16)
    key_gradient = jnp.einsum("wtr,wtj->wrj", score_gradient, query_block_rows) * scale_factor
    value_gradient = jnp.einsum("wtr,wtj->wrj", lower_probabilities, block_gradient)

    def settle(term):
        far_part = low_copy(term[:, CAP:]).astype(jnp.float32)
        arrived = jnp.zeros((block_total, CAP, term.shape[2]), jnp.float32).at[partner_of].add(far_part)
        return (term[:, :CAP] + arrived).astype(jnp.bfloat16)

    def at_tokens(blocked):
        return blocked.reshape(slot_total, blocked.shape[-1])[slot_of]

    return at_tokens(attended_output), at_tokens(query_gradient), at_tokens(settle(key_gradient)), at_tokens(settle(value_gradient))


def reference(queries, keys_in, values, out_proj, out_grad, slot_index, partner_block):
    token_total, head_total, head_width = queries.shape
    grad_attn = low_copy(jnp.dot(out_grad, out_proj, preferred_element_type=jnp.float32))
    grad_attn = grad_attn.reshape(token_total, head_total, head_width)
    per_head = lax.map(head_pass, (jnp.swapaxes(queries, 0, 1), jnp.swapaxes(keys_in, 0, 1),
                                   jnp.swapaxes(values, 0, 1), jnp.swapaxes(grad_attn, 0, 1),
                                   slot_index, partner_block))
    attended_output = jnp.swapaxes(per_head[0], 0, 1)
    grad_queries = jnp.swapaxes(per_head[1], 0, 1)
    grad_keys = jnp.swapaxes(per_head[2], 0, 1)
    grad_values = jnp.swapaxes(per_head[3], 0, 1)
    attn_flat = attended_output.reshape(token_total, head_total * head_width)
    group_width = HEAD_DEV * head_width
    mixed_sum = jnp.zeros((token_total, out_proj.shape[0]), jnp.float32)
    for group_index in range(N_HEAD):
        first_col = group_index * group_width
        attn_group = attn_flat[:, first_col:first_col + group_width]
        proj_group = out_proj[:, first_col:first_col + group_width]
        partial_sum = jnp.dot(attn_group, proj_group.T, preferred_element_type=jnp.float32)
        mixed_sum = mixed_sum + low_copy(partial_sum).astype(jnp.float32)
    mixed_out = mixed_sum.astype(jnp.bfloat16)
    grad_proj = jnp.dot(out_grad.T, attn_flat, preferred_element_type=jnp.float32).astype(jnp.bfloat16)
    return mixed_out, grad_queries, grad_keys, grad_values, grad_proj
```

```python
import functools

import jax
import jax.numpy as jnp
from jax import lax
from jax.experimental import pallas as pl
from jax.experimental.pallas import tpu as pltpu
from jax.sharding import PartitionSpec as P

MESH = pl.DeviceIdType.MESH
CAP = 128
HD = 128
HEADS = 4
TOK = 256
SEQ = 32
N_HEAD = 8
OWNED = 384
PER = 12
MSG = HEADS * PER
QUADS = 8
ROWS = SEQ * MSG
BLOCKS = ROWS // CAP
D = 4096
XN = 4
ZN = 8
VMEM_LIMIT = 56 * 1024 * 1024
F32 = jnp.float32
BF16 = jnp.bfloat16


def iota(shape, dim):
    return lax.broadcasted_iota(jnp.int32, shape, dim)


def greet(peers):
    barrier = pltpu.get_barrier_semaphore()
    for peer in peers:
        pl.semaphore_signal(barrier, inc=1, device_id=peer, device_id_type=MESH)
    pl.semaphore_wait(barrier, len(peers))


def remote(src, dst, send_sem, recv_sem, peer):
    return pltpu.make_async_remote_copy(
        src_ref=src,
        dst_ref=dst,
        send_sem=send_sem,
        recv_sem=recv_sem,
        device_id=peer,
        device_id_type=MESH,
    )


def dispatch_kernel(
    x_ref, slot_ref, partner_ref, grad_ref, proj_hbm,
    rx_ref, rid_ref, rga_ref, up_ref, pack_ref,
    sx, sid, sga, proj, ga_scr,
    x_send, x_recv, id_send, id_recv, ga_send, ga_recv, up_send, up_recv, proj_sem,
):
    me = lax.axis_index("seq")
    hm = lax.axis_index("head")
    fetch = pltpu.make_async_copy(proj_hbm, proj, proj_sem)
    fetch.start()
    greet(
        [{"seq": lax.rem(me + k, SEQ)} for k in range(1, SEQ)]
        + [{"head": lax.rem(hm + k, N_HEAD)} for k in range(1, N_HEAD)]
    )
    for k in range(1, N_HEAD):
        peer = lax.rem(hm + k, N_HEAD)
        remote(grad_ref, up_ref.at[hm], up_send.at[peer], up_recv.at[hm], {"head": peer}).start()
    up_ref[hm] = grad_ref[...]

    first = me // QUADS
    spot_in = lax.rem(me, QUADS)
    owner_col = iota((SEQ, TOK), 0)
    before_mask = (iota((TOK, TOK), 0) < iota((TOK, TOK), 1)).astype(BF16)
    lane = iota((QUADS, 128), 1)
    half = lane // PER
    quad_col = iota((QUADS, TOK), 0).astype(F32)
    row_col = iota((128, TOK), 0).astype(F32)
    base = ((owner_col % QUADS) * MSG + (owner_col // QUADS) * PER).astype(F32)
    for i in range(HEADS):
        h = lax.rem(first + i, HEADS)
        slots = slot_ref[h]
        member = (slots >= owner_col * OWNED) & (slots < (owner_col + 1) * OWNED)
        one = jnp.where(member, 1.0, 0.0).astype(F32)
        before = jnp.dot(one.astype(BF16), before_mask, preferred_element_type=F32)
        rank = jnp.sum(one * before, axis=0, keepdims=True)
        owner = jnp.sum(jnp.where(member, owner_col.astype(F32), 0.0), axis=0, keepdims=True)
        spot = jnp.sum(jnp.where(member, base, 0.0), axis=0, keepdims=True) + rank
        within = slots.astype(F32) - owner * OWNED
        block = jnp.where(within >= CAP, 1.0, 0.0) + jnp.where(within >= 2 * CAP, 1.0, 0.0)
        place = within - block * CAP
        part = jnp.floor(owner / QUADS)
        quad = owner - part * QUADS
        row = part * PER + rank
        pack = jnp.where(iota((QUADS * MSG, TOK), 0).astype(F32) == spot, 1.0, 0.0).astype(BF16)
        pack_ref[h] = pack
        packed = jnp.dot(pack, x_ref[h], preferred_element_type=F32).astype(BF16)
        sx[pl.ds(h * QUADS, QUADS)] = packed.reshape(QUADS, MSG, 3 * HD)
        here = quad_col == quad
        at_row = jnp.where(row_col == row, 1.0, 0.0).astype(BF16)
        contract = (((1,), (1,)), ((), ()))
        high = lax.dot_general(
            jnp.where(here, block + 1.0, 0.0).astype(BF16), at_row, contract,
            preferred_element_type=F32,
        )
        low = lax.dot_general(
            jnp.where(here, place, 0.0).astype(BF16), at_row, contract,
            preferred_element_type=F32,
        )
        ids = half * OWNED + ((high - 1.0) * CAP + low).astype(jnp.int32)
        ids = jnp.where(high > 0.5, ids, -1)
        ids = jnp.where(lane >= 64, partner_ref[h], ids)
        for d in range(QUADS):
            sid[h * QUADS + d] = ids[d : d + 1]
        for k in range(QUADS):
            dst = h * QUADS + lax.rem(spot_in + k, QUADS)
            if i == 0 and k == 0:
                rx_ref[me] = sx[me]
                rid_ref[me] = sid[me]
                continue
            remote(sid.at[dst], rid_ref.at[me], id_send.at[dst], id_recv.at[me], {"seq": dst}).start()
            remote(sx.at[dst], rx_ref.at[me], x_send.at[dst], x_recv.at[me], {"seq": dst}).start()

    for k in range(1, N_HEAD):
        peer = lax.rem(hm + k, N_HEAD)
        remote(grad_ref, up_ref.at[peer], up_send.at[peer], up_recv.at[peer], {"head": peer}).wait()
    fetch.wait()
    step = 512
    for n in range(D // step):
        term = jnp.dot(
            up_ref[:, :, n * step : (n + 1) * step].reshape(TOK, step),
            proj[n * step : (n + 1) * step, :],
            preferred_element_type=F32,
        )
        if n == 0:
            ga_scr[...] = term
        else:
            ga_scr[...] += term
    for i in range(HEADS):
        h = lax.rem(first + i, HEADS)
        mine = ga_scr[:, pl.ds(pl.multiple_of(h * HD, HD), HD)].astype(BF16)
        packed = jnp.dot(pack_ref[h], mine, preferred_element_type=F32).astype(BF16)
        sga[pl.ds(h * QUADS, QUADS)] = packed.reshape(QUADS, MSG, HD)
        for k in range(QUADS):
            dst = h * QUADS + lax.rem(spot_in + k, QUADS)
            if i == 0 and k == 0:
                rga_ref[me] = sga[me]
                continue
            remote(sga.at[dst], rga_ref.at[me], ga_send.at[dst], ga_recv.at[me], {"seq": dst}).start()

    @pl.loop(1, SEQ)
    def _(k):
        peer = lax.rem(me + k, SEQ)
        who = {"seq": peer}
        remote(sid.at[peer], rid_ref.at[peer], id_send.at[peer], id_recv.at[peer], who).wait()
        remote(sx.at[peer], rx_ref.at[peer], x_send.at[peer], x_recv.at[peer], who).wait()
        remote(sga.at[peer], rga_ref.at[peer], ga_send.at[peer], ga_recv.at[peer], who).wait()


def dispatch(x, slots, partner, grad, proj):
    vmem = pl.BlockSpec(memory_space=pltpu.VMEM)
    dma = pltpu.SemaphoreType.DMA
    return pl.pallas_call(
        dispatch_kernel,
        out_shape=(
            jax.ShapeDtypeStruct((SEQ, MSG, 3 * HD), BF16),
            jax.ShapeDtypeStruct((SEQ, 1, 128), jnp.int32),
            jax.ShapeDtypeStruct((SEQ, MSG, HD), BF16),
            jax.ShapeDtypeStruct((N_HEAD, TOK // N_HEAD, D), BF16),
            jax.ShapeDtypeStruct((HEADS, QUADS * MSG, TOK), BF16),
        ),
        in_specs=[vmem] * 4 + [pl.BlockSpec(memory_space=pl.ANY)],
        out_specs=(vmem,) * 5,
        scratch_shapes=[
            pltpu.VMEM((SEQ, MSG, 3 * HD), BF16),
            pltpu.VMEM((SEQ, 1, 128), jnp.int32),
            pltpu.VMEM((SEQ, MSG, HD), BF16),
            pltpu.VMEM((D, HEADS * HD), BF16),
            pltpu.VMEM((TOK, HEADS * HD), F32),
            dma((SEQ,)), dma((SEQ,)), dma((SEQ,)), dma((SEQ,)), dma((SEQ,)), dma((SEQ,)),
            dma((N_HEAD,)), dma((N_HEAD,)), dma,
        ],
        compiler_params=pltpu.CompilerParams(
            collective_id=0, has_side_effects=True, vmem_limit_bytes=VMEM_LIMIT
        ),
        name="dispatch",
    )(x, slots, partner, grad, proj)


def attend_kernel(ids_smem, ids_ref, x_ref, ga_ref, out_ref, placed, fill_col, fill_row, own, far, res):
    me = lax.axis_index("seq")
    quad = lax.rem(me, QUADS)
    ids = ids_ref[...]
    high = (ids >> 7).astype(F32).astype(BF16)
    low = (ids & 127).astype(F32).astype(BF16)
    spread = (iota((128, ROWS), 0) == iota((128, ROWS), 1) % MSG).astype(BF16)
    src_row = iota((SEQ, ROWS), 0) == iota((SEQ, ROWS), 1) // MSG
    wide = jnp.dot(high, spread, preferred_element_type=F32) * CAP + jnp.dot(
        low, spread, preferred_element_type=F32
    )
    ids_row = jnp.sum(jnp.where(src_row, wide, 0.0), axis=0, keepdims=True)
    chunk = 256
    for n in range(ROWS // chunk):
        rows = pl.ds(n * chunk, chunk)
        slot = (iota((chunk, ROWS), 0) + n * chunk).astype(F32)
        put = jnp.where(slot == ids_row, 1.0, 0.0)
        fill_col[rows] = jnp.broadcast_to(jnp.sum(put, axis=1, keepdims=True), (chunk, 128))
        put = put.astype(BF16)
        fill = lax.dot_general(
            jnp.ones((8, ROWS), BF16), put, (((1,), (1,)), ((), ())), preferred_element_type=F32
        )
        for m in range(chunk // CAP):
            fill_row[n * (chunk // CAP) + m] = fill[:, m * CAP : (m + 1) * CAP]
        placed[rows, : 3 * HD] = jnp.dot(put, x_ref[...], preferred_element_type=F32).astype(BF16)
        placed[rows, 3 * HD :] = jnp.dot(put, ga_ref[...], preferred_element_type=F32).astype(BF16)

    scale = HD**-0.5
    nt = (((1,), (1,)), ((), ()))
    tn = (((0,), (0,)), ((), ()))

    def other_of(b):
        j = b // 3
        owner = quad + QUADS * j
        partner = ids_smem[owner, 64 + b % 3]
        same = partner == owner * 3 + b % 3
        return same, (partner // (3 * QUADS)) * 3 + partner % 3

    def block(b, _):
        same, other = other_of(b)
        near = pl.ds(pl.multiple_of(b * CAP, CAP), CAP)
        away = pl.ds(pl.multiple_of(other * CAP, CAP), CAP)
        query = placed[near, :HD]
        grad = placed[near, 3 * HD :]
        keys = jnp.concatenate([placed[near, HD : 2 * HD], placed[away, HD : 2 * HD]], axis=0)
        vals = jnp.concatenate(
            [placed[near, 2 * HD : 3 * HD], placed[away, 2 * HD : 3 * HD]], axis=0
        )
        apart = jnp.where(same, 0.0, 1.0)
        live = jnp.concatenate([fill_row[b][:1], fill_row[other][:1] * apart], axis=1)
        filled = fill_col[near, :1]
        scores = lax.dot_general(query, keys, nt, preferred_element_type=F32) * scale
        scores = jnp.where(live > 0, scores, -1e30)
        top = jnp.max(scores, axis=1, keepdims=True)
        weights = jnp.exp(scores - top) * live
        total = jnp.sum(weights, axis=1, keepdims=True) + (1.0 - filled)
        probs = weights * (filled / total)
        low_probs = probs.astype(BF16)
        attended = jnp.dot(low_probs, vals, preferred_element_type=F32)
        prob_grad = lax.dot_general(grad, vals, nt, preferred_element_type=F32)
        inner = jnp.sum(probs * prob_grad, axis=1, keepdims=True)
        score_grad = (probs * (prob_grad - inner)).astype(BF16)
        query_grad = jnp.dot(score_grad, keys, preferred_element_type=F32) * scale
        key_grad = lax.dot_general(score_grad, query, tn, preferred_element_type=F32) * scale
        val_grad = lax.dot_general(low_probs, grad, tn, preferred_element_type=F32)
        res[near, :HD] = attended.astype(BF16)
        res[near, HD : 2 * HD] = query_grad.astype(BF16)
        own[near, :HD] = key_grad[:CAP]
        own[near, HD:] = val_grad[:CAP]
        far[near, :HD] = key_grad[CAP:].astype(BF16)
        far[near, HD:] = val_grad[CAP:].astype(BF16)
        return 0

    lax.fori_loop(0, BLOCKS, block, 0, unroll=4)

    def settle(b, _):
        _, other = other_of(b)
        near = pl.ds(pl.multiple_of(b * CAP, CAP), CAP)
        away = pl.ds(pl.multiple_of(other * CAP, CAP), CAP)
        res[near, 2 * HD :] = (own[near] + far[away].astype(F32)).astype(BF16)
        return 0

    lax.fori_loop(0, BLOCKS, settle, 0, unroll=4)

    for n in range(ROWS // chunk):
        lane = iota((chunk, 128), 1)
        row = iota((chunk, 1), 0) + n * chunk
        pick = (iota((chunk, SEQ), 1) == (iota((chunk, SEQ), 0) + n * chunk) // MSG).astype(BF16)
        tall = jnp.dot(pick, high, preferred_element_type=F32) * CAP + jnp.dot(
            pick, low, preferred_element_type=F32
        )
        ids_col = jnp.sum(jnp.where(lane == row % MSG, tall, 0.0), axis=1, keepdims=True)
        take = jnp.where(iota((chunk, ROWS), 1).astype(F32) == ids_col, 1.0, 0.0).astype(BF16)
        out_ref[pl.ds(n * chunk, chunk)] = jnp.dot(
            take, res[...], preferred_element_type=F32
        ).astype(BF16)


def attend(ids, x, ga):
    vmem = pl.BlockSpec(memory_space=pltpu.VMEM)
    return pl.pallas_call(
        attend_kernel,
        out_shape=jax.ShapeDtypeStruct((ROWS, 4 * HD), BF16),
        in_specs=[pl.BlockSpec(memory_space=pltpu.SMEM), vmem, vmem, vmem],
        out_specs=vmem,
        scratch_shapes=[
            pltpu.VMEM((ROWS, 4 * HD), BF16),
            pltpu.VMEM((ROWS, 128), F32),
            pltpu.VMEM((BLOCKS, 8, CAP), F32),
            pltpu.VMEM((ROWS, 2 * HD), F32),
            pltpu.VMEM((ROWS, 2 * HD), BF16),
            pltpu.VMEM((ROWS, 4 * HD), BF16),
        ],
        compiler_params=pltpu.CompilerParams(vmem_limit_bytes=VMEM_LIMIT),
        name="attend",
    )(ids, ids, x, ga)


def back_kernel(send_ref, up_ref, recv_ref, g_ref, b_send, b_recv, g_send, g_recv, g_local):
    me = lax.axis_index("seq")
    mx = lax.rem(me, XN)
    row = me - mx
    greet([{"seq": lax.rem(me + k, SEQ)} for k in range(1, SEQ)])

    @pl.loop(1, SEQ)
    def _(k):
        peer = lax.rem(me + k, SEQ)
        remote(
            send_ref.at[peer], recv_ref.at[me], b_send.at[peer], b_recv.at[me], {"seq": peer}
        ).start()

    recv_ref[me] = send_ref[me]

    def piece(z, x):
        return up_ref.at[:, :, pl.ds(pl.multiple_of((z * XN + x) * 128, 128), 128)]

    def outgoing(k, z):
        x = lax.rem(mx + k, XN)
        return remote(
            piece(z, x), g_ref.at[mx, z], g_send.at[x, z], g_recv.at[mx, z], {"seq": row + x}
        )

    def arriving(k, z):
        x = lax.rem(mx + k, XN)
        return remote(
            piece(z, x), g_ref.at[x, z], g_send.at[x, z], g_recv.at[x, z], {"seq": row + x}
        )

    for k in range(1, XN):
        for z in range(ZN):
            outgoing(k, z).start()
    for z in range(ZN):
        pltpu.make_async_copy(piece(z, mx), g_ref.at[mx, z], g_local.at[z]).start()
    for z in range(ZN):
        pltpu.make_async_copy(piece(z, mx), g_ref.at[mx, z], g_local.at[z]).wait()

    @pl.loop(1, SEQ)
    def _(k):
        peer = lax.rem(me + k, SEQ)
        remote(
            send_ref.at[peer], recv_ref.at[peer], b_send.at[peer], b_recv.at[peer], {"seq": peer}
        ).wait()

    for k in range(1, XN):
        for z in range(ZN):
            arriving(k, z).wait()


def back(rows, up):
    vmem = pl.BlockSpec(memory_space=pltpu.VMEM)
    dma = pltpu.SemaphoreType.DMA
    return pl.pallas_call(
        back_kernel,
        out_shape=(
            jax.ShapeDtypeStruct((SEQ, MSG, 4 * HD), BF16),
            jax.ShapeDtypeStruct((XN, ZN, N_HEAD, TOK // N_HEAD, 128), BF16),
        ),
        in_specs=[vmem, vmem],
        out_specs=(vmem, vmem),
        scratch_shapes=[dma((SEQ,)), dma((SEQ,)), dma((XN, ZN)), dma((XN, ZN)), dma((ZN,))],
        compiler_params=pltpu.CompilerParams(
            collective_id=1, has_side_effects=True, vmem_limit_bytes=VMEM_LIMIT
        ),
        name="back",
    )(rows, up)


def finish_kernel(
    back_ref, pack_ref, g_ref, proj_hbm,
    mixed_ref, dq_ref, dk_ref, dv_ref, gp_ref,
    proj, attn, attn_all, attn_t, part, mixed_in, gp_part, gp_in,
    proj_sem, a_send, a_recv, m_send, m_recv, p_send, p_recv,
):
    me = lax.axis_index("seq")
    hm = lax.axis_index("head")
    mx = lax.rem(me, XN)
    mz = me // XN
    fetch = pltpu.make_async_copy(proj_hbm, proj, proj_sem)
    fetch.start()

    def x_peer(k):
        x = lax.rem(mx + k, XN)
        return x, {"seq": mz * XN + x}

    def z_peer(k):
        z = lax.rem(mz + k, ZN)
        return z, {"seq": z * XN + mx}

    def h_peer(k):
        h = lax.rem(hm + k, N_HEAD)
        return h, {"head": h}

    greet(
        [x_peer(k)[1] for k in range(1, XN)]
        + [z_peer(k)[1] for k in range(1, ZN)]
        + [h_peer(k)[1] for k in range(1, N_HEAD)]
    )
    tn = (((0,), (0,)), ((), ()))
    for h in range(HEADS):
        rows = back_ref[h * QUADS : (h + 1) * QUADS].reshape(QUADS * MSG, 4 * HD)
        home = lax.dot_general(pack_ref[h], rows, tn, preferred_element_type=F32).astype(BF16)
        lanes = slice(h * HD, (h + 1) * HD)
        attn[:, lanes] = home[:, :HD]
        dq_ref[:, lanes] = home[:, HD : 2 * HD]
        dk_ref[:, lanes] = home[:, 2 * HD : 3 * HD]
        dv_ref[:, lanes] = home[:, 3 * HD :]
    for k in range(1, XN):
        x, who = x_peer(k)
        remote(attn, attn_all.at[mx], a_send.at[x], a_recv.at[mx], who).start()
    attn_all[mx] = attn[...]
    fetch.wait()
    step = 512
    for n in range(D // step):
        term = lax.dot_general(
            attn[...], proj[n * step : (n + 1) * step, :], (((1,), (1,)), ((), ())),
            preferred_element_type=F32,
        )
        part[:, :, n * step : (n + 1) * step] = term.astype(BF16).reshape(
            N_HEAD, TOK // N_HEAD, step
        )
    for k in range(1, N_HEAD):
        h, who = h_peer(k)
        remote(part.at[h], mixed_in.at[hm], m_send.at[h], m_recv.at[hm], who).start()
    mixed_in[hm] = part[hm]
    for k in range(1, XN):
        x, who = x_peer(k)
        remote(attn, attn_all.at[x], a_send.at[x], a_recv.at[x], who).wait()
    for x in range(XN):
        attn_t[:, x * TOK : (x + 1) * TOK] = attn_all[x].T
    for k in range(1, ZN + 1):
        z, who = z_peer(k)
        grads = g_ref[:, pl.ds(z, 1)].reshape(XN * TOK, 128)
        gp_part[z] = jnp.dot(attn_t[...], grads, preferred_element_type=F32).astype(BF16)
        if k < ZN:
            remote(gp_part.at[z], gp_in.at[mz], p_send.at[z], p_recv.at[mz], who).start()
    gp_in[mz] = gp_part[mz]
    for k in range(1, N_HEAD):
        h, who = h_peer(k)
        remote(part.at[h], mixed_in.at[h], m_send.at[h], m_recv.at[h], who).wait()
    total = mixed_in[0].astype(F32)
    for h in range(1, N_HEAD):
        total += mixed_in[h].astype(F32)
    mixed_ref[...] = total.astype(BF16)
    for k in range(1, ZN):
        z, who = z_peer(k)
        remote(gp_part.at[z], gp_in.at[z], p_send.at[z], p_recv.at[z], who).wait()
    total = gp_in[0].astype(F32)
    for z in range(1, ZN):
        total += gp_in[z].astype(F32)
    gp_ref[...] = total.T.astype(BF16)


def finish(rows, pack, grads, proj):
    vmem = pl.BlockSpec(memory_space=pltpu.VMEM)
    dma = pltpu.SemaphoreType.DMA
    wide = HEADS * HD
    return pl.pallas_call(
        finish_kernel,
        out_shape=(
            jax.ShapeDtypeStruct((TOK // N_HEAD, D), BF16),
            jax.ShapeDtypeStruct((TOK, wide), BF16),
            jax.ShapeDtypeStruct((TOK, wide), BF16),
            jax.ShapeDtypeStruct((TOK, wide), BF16),
            jax.ShapeDtypeStruct((128, wide), BF16),
        ),
        in_specs=[vmem, vmem, vmem, pl.BlockSpec(memory_space=pl.ANY)],
        out_specs=(vmem,) * 5,
        scratch_shapes=[
            pltpu.VMEM((D, wide), BF16),
            pltpu.VMEM((TOK, wide), BF16),
            pltpu.VMEM((XN, TOK, wide), BF16),
            pltpu.VMEM((wide, XN * TOK), BF16),
            pltpu.VMEM((N_HEAD, TOK // N_HEAD, D), BF16),
            pltpu.VMEM((N_HEAD, TOK // N_HEAD, D), BF16),
            pltpu.VMEM((ZN, wide, 128), BF16),
            pltpu.VMEM((ZN, wide, 128), BF16),
            dma,
            dma((XN,)), dma((XN,)), dma((N_HEAD,)), dma((N_HEAD,)), dma((ZN,)), dma((ZN,)),
        ],
        compiler_params=pltpu.CompilerParams(
            collective_id=2, has_side_effects=True, vmem_limit_bytes=VMEM_LIMIT
        ),
        name="finish",
    )(rows, pack, grads, proj)


def shards(queries, keys_in, values, out_proj, out_grad, slot_index, partner_block):
    x = jnp.swapaxes(jnp.concatenate([queries, keys_in, values], axis=2), 0, 1)
    slots = slot_index.reshape(HEADS, 1, TOK)
    partner = jnp.pad(partner_block, ((0, 0), (64, 128 - 64 - 3))).reshape(HEADS, 1, 128)
    rx, rid, rga, up, pack = dispatch(x, slots, partner, out_grad, out_proj)
    rows = attend(
        rid.reshape(SEQ, 128), rx.reshape(ROWS, 3 * HD), rga.reshape(ROWS, HD)
    )
    returned, grads = back(rows.reshape(SEQ, MSG, 4 * HD), up)
    mixed, dq, dk, dv, gp = finish(returned, pack, grads, out_proj)
    shape = (TOK, HEADS, HD)
    return mixed, dq.reshape(shape), dk.reshape(shape), dv.reshape(shape), gp


def solution(mesh):
    placed = (
        P("seq", "head", None),
        P("seq", "head", None),
        P("seq", "head", None),
        P(None, "head"),
        P(("seq", "head"), None),
        P("head", "seq"),
        P("head", "seq"),
    )
    return jax.shard_map(
        shards,
        mesh=mesh,
        in_specs=placed,
        out_specs=(
            P(("seq", "head"), None),
            P("seq", "head", None),
            P("seq", "head", None),
            P("seq", "head", None),
            P("seq", "head"),
        ),
        check_vma=False,
    )
```

```python
import functools

import jax
import jax.numpy as jnp
from jax import lax
from jax.experimental import pallas as pl
from jax.experimental.pallas import tpu as pltpu
from jax.sharding import PartitionSpec as P

MESH = pl.DeviceIdType.MESH
CAP = 128
HD = 128
HEADS = 4
TOK = 256
SEQ = 32
N_HEAD = 8
OWNED = 384
PER = 12
MSG = HEADS * PER
QUADS = 8
ROWS = SEQ * MSG
BLOCKS = ROWS // CAP
D = 4096
XN = 4
ZN = 8
VMEM_LIMIT = 56 * 1024 * 1024
F32 = jnp.float32
BF16 = jnp.bfloat16


def iota(shape, dim):
    return lax.broadcasted_iota(jnp.int32, shape, dim)


def greet(peers):
    barrier = pltpu.get_barrier_semaphore()
    for peer in peers:
        pl.semaphore_signal(barrier, inc=1, device_id=peer, device_id_type=MESH)
    pl.semaphore_wait(barrier, len(peers))


def remote(src, dst, send_sem, recv_sem, peer):
    return pltpu.make_async_remote_copy(
        src_ref=src,
        dst_ref=dst,
        send_sem=send_sem,
        recv_sem=recv_sem,
        device_id=peer,
        device_id_type=MESH,
    )

NT = (((1,), (1,)), ((), ()))
TN = (((0,), (0,)), ((), ()))
ID, QKV, GA, ATT, BACK = range(5)
ROW = TOK // N_HEAD
GROUP = QUADS * MSG


def dot(a, b):
    return jnp.dot(a, b, preferred_element_type=F32)


def dot_general(a, b, dims):
    return lax.dot_general(a, b, dims, preferred_element_type=F32)


def hot(condition):
    return jnp.where(condition, 1.0, 0.0).astype(BF16)


def layer_kernel(
    q_ref, k_ref, v_ref, slot_ref, partner_ref, grad_ref, proj_hbm,
    mixed_ref, dq_ref, dk_ref, dv_ref, gp_ref,
    proj, xf, x, pack, pack_t, sx, sid, sga, satt, sback, rx, rid, rga, ratt, rback,
    ga_scr, up, gs, gx, gall, put, take, acc, acc_g, fill_col, fill_row,
    placed, placed_g, key_set, probs_scr, own, far, res, res_g,
    attn, attn_all, attn_t, part, mixed_in, gp_part, gp_acc,
    proj_sem, t_send, t_recv, up_send, up_recv, core_send, core_recv,
    gx_send, gx_recv, a_send, a_recv, m_send, m_recv, p_send, p_recv,
):
    me = lax.axis_index("seq")
    hm = lax.axis_index("head")
    mx = lax.rem(me, XN)
    mz = me // XN
    first = me // QUADS
    quad = lax.rem(me, QUADS)
    core = lax.rem(hm, 2)
    my = hm // 2
    sibling = {"head": my * 2 + 1 - core}
    fetch = pltpu.make_async_copy(proj_hbm, proj, proj_sem)
    fetch.start()

    def x_peer(k):
        to = lax.rem(mx + k, XN)
        return to, {"seq": mz * XN + to}

    def y_peer(k):
        to = lax.rem(my + k, 4)
        return to, {"head": to * 2 + core}

    def h_peer(k):
        to = lax.rem(hm + k, N_HEAD)
        return to, {"head": to}

    greet(
        [{"seq": lax.rem(me + k, SEQ)} for k in range(1, SEQ)]
        + [h_peer(k)[1] for k in range(1, N_HEAD)]
    )

    def gather_start(kind, src, out):
        for k in (1, 3, 2):
            _, who = y_peer(k)
            remote(src, out.at[hm], up_send.at[kind, k], up_recv.at[kind, my], who).start()
        remote(src, out.at[hm], core_send.at[kind, 0], core_recv.at[kind, my], sibling).start()
        out[hm] = src[...]

    def gather_forward(kind, src, out):
        for k in (1, 3, 2):
            y, who = y_peer(k)
            block = out.at[y * 2 + core]
            remote(src, block, up_send.at[kind, k], up_recv.at[kind, y], who).wait_recv()
            remote(block, block, core_send.at[kind, k], core_recv.at[kind, y], sibling).start()

    def gather_end(kind, src, out):
        for k in range(4):
            y, who = y_peer(k)
            block = out.at[y * 2 + 1 - core]
            remote(src, block, core_send.at[kind, k], core_recv.at[kind, y], sibling).wait()
            if k:
                remote(src, block, up_send.at[kind, k], up_recv.at[kind, y], who).wait_send()

    def send(kind, src, out, to):
        remote(src.at[to], out.at[me], t_send.at[kind, to], t_recv.at[kind, me], {"seq": to}).start()

    def message(kind, src, out, peer):
        return remote(
            src.at[peer], out.at[peer], t_send.at[kind, peer], t_recv.at[kind, peer], {"seq": peer}
        )

    def members(group, i):
        for k in range(QUADS):
            yield group * QUADS + lax.rem(quad + k, QUADS), i == 0 and k == 0

    def send_group(kind, src, out, group, i):
        for to, mine in members(group, i):
            if mine:
                out[me] = src[me]
            else:
                send(kind, src, out, to)

    def wait_group(kind, src, out, group, i):
        for peer, mine in members(group, i):
            if not mine:
                message(kind, src, out, peer).wait_recv()

    gather_start(0, grad_ref, up)
    for xx in range(XN):
        for zz in range(ZN):
            chunk = zz * XN + xx
            gs[xx, zz] = grad_ref[:, chunk * 128 : (chunk + 1) * 128]
    for k in range(1, XN):
        to, who = x_peer(k)
        remote(gs.at[to], gx.at[mx], gx_send.at[k], gx_recv.at[mx], who).start()
    gx[mx] = gs[mx]

    for n, ref in enumerate((q_ref, k_ref, v_ref)):
        xf[n] = ref[...].astype(F32)
    for h in range(HEADS):
        for n in range(3):
            x[h, :, n * HD : (n + 1) * HD] = xf[n, pl.ds(h, TOK, stride=HEADS), :].astype(BF16)

    owner_col = iota((SEQ, TOK), 0)
    before_mask = hot(iota((TOK, TOK), 0) < iota((TOK, TOK), 1))
    lane = iota((QUADS, 128), 1)
    lane_row = iota((1, 128), 1)
    quad_col = iota((QUADS, TOK), 0).astype(F32)
    row_col = iota((128, TOK), 0).astype(F32)
    base = ((owner_col % QUADS) * MSG + (owner_col // QUADS) * PER).astype(F32)
    for i in range(HEADS):
        h = lax.rem(first + i, HEADS)
        slots = slot_ref[pl.ds(h, 1), :]
        member = (slots >= owner_col * OWNED) & (slots < (owner_col + 1) * OWNED)
        one = jnp.where(member, 1.0, 0.0)
        before = dot(one.astype(BF16), before_mask)
        rank = jnp.sum(one * before, axis=0, keepdims=True)
        owner = jnp.sum(jnp.where(member, owner_col.astype(F32), 0.0), axis=0, keepdims=True)
        spot = jnp.sum(jnp.where(member, base, 0.0), axis=0, keepdims=True) + rank
        within = slots.astype(F32) - owner * OWNED
        block = jnp.where(within >= CAP, 1.0, 0.0) + jnp.where(within >= 2 * CAP, 1.0, 0.0)
        place = within - block * CAP
        row_part = jnp.floor(owner / QUADS)
        row = row_part * PER + rank
        here = quad_col == owner - row_part * QUADS
        at_row = hot(row_col == row)
        high = dot_general(jnp.where(here, block + 1.0, 0.0).astype(BF16), at_row, NT)
        low = dot_general(jnp.where(here, place, 0.0).astype(BF16), at_row, NT)
        ids = (lane // PER) * OWNED + ((high - 1.0) * CAP + low).astype(jnp.int32)
        ids = jnp.where(high > 0.5, ids, -1)
        pairs = partner_ref[pl.ds(h, 1), :]
        for b in range(3):
            ids = jnp.where(lane == 64 + b, pairs[:, b : b + 1], ids)
        for d in range(QUADS):
            sid[h * QUADS + d] = ids[d : d + 1]
        send_group(ID, sid, rid, h, i)
        packing = hot(iota((GROUP, TOK), 0).astype(F32) == spot)
        pack[h] = packing
        sx[pl.ds(h * QUADS, QUADS)] = dot(packing, x[h]).astype(BF16).reshape(QUADS, MSG, 3 * HD)
        send_group(QKV, sx, rx, h, i)

    gather_forward(0, grad_ref, up)
    for k in range(1, XN):
        xx, who = x_peer(k)
        remote(gs.at[xx], gx.at[xx], gx_send.at[k], gx_recv.at[xx], who).wait()
    gather_start(1, gx, gall)
    gather_end(0, grad_ref, up)
    fetch.wait()
    step = 512
    for n in range(D // step):
        cols = slice(n * step, (n + 1) * step)
        term = dot(up[:, :, cols].reshape(TOK, step), proj[cols, :])
        if n == 0:
            ga_scr[...] = term
        else:
            ga_scr[...] += term
    for i in range(HEADS):
        h = lax.rem(first + i, HEADS)
        mine = ga_scr[:, pl.ds(pl.multiple_of(h * HD, HD), HD)].astype(BF16)
        sga[pl.ds(h * QUADS, QUADS)] = dot(pack[h], mine).astype(BF16).reshape(QUADS, MSG, HD)
        send_group(GA, sga, rga, h, i)
    gather_forward(1, gx, gall)

    spread = hot(iota((128, GROUP), 0) == iota((128, GROUP), 1) % MSG)
    src_row = iota((QUADS, GROUP), 0) == iota((QUADS, GROUP), 1) // MSG
    pick = hot(iota((GROUP, QUADS), 0) // MSG == iota((GROUP, QUADS), 1))
    own_lane = iota((GROUP, 128), 1) == iota((GROUP, 128), 0) % MSG
    sub = iota((QUADS, 128), 0)
    for i in range(HEADS):
        c = lax.rem(first + HEADS - i, HEADS)
        wait_group(ID, sid, rid, c, i)
        ids = jnp.zeros((QUADS, 128), jnp.int32)
        for d in range(QUADS):
            ids = jnp.where(sub == d, rid[c * QUADS + d], ids)
        high = (ids >> 7).astype(F32).astype(BF16)
        low = (ids & 127).astype(F32).astype(BF16)
        wide = dot(high, spread) * CAP + dot(low, spread)
        ids_row = jnp.sum(jnp.where(src_row, wide, 0.0), axis=0, keepdims=True)
        tall = dot(pick, high) * CAP + dot(pick, low)
        ids_col = jnp.sum(jnp.where(own_lane, tall, 0.0), axis=1, keepdims=True)
        put[c] = hot(iota((ROWS, GROUP), 0).astype(F32) == ids_row)
        take[c] = hot(iota((GROUP, ROWS), 1).astype(F32) == ids_col)
        col = dot(put[c], jnp.ones((GROUP, 128), BF16))
        row = dot(jnp.ones((8, GROUP), BF16), take[c])
        if i == 0:
            fill_col[...] = col
        else:
            fill_col[...] += col
        for b in range(BLOCKS):
            piece = row[:, b * CAP : (b + 1) * CAP]
            if i == 0:
                fill_row[b] = piece
            else:
                fill_row[b] += piece
    for h in range(HEADS):
        pack_t[h] = pack[h].T
    for i in range(HEADS):
        c = lax.rem(first + HEADS - i, HEADS)
        wait_group(QKV, sx, rx, c, i)
        term = dot(put[c], rx[pl.ds(c * QUADS, QUADS)].reshape(GROUP, 3 * HD))
        if i == 0:
            acc[...] = term
        elif i < HEADS - 1:
            acc[...] += term
        else:
            placed[...] = (acc[...] + term).astype(BF16)

    scale = HD**-0.5

    def rows_of(b):
        return pl.ds(pl.multiple_of(b * CAP, CAP), CAP)

    def pairing(j, b):
        owner = quad + QUADS * j
        partner = rid[owner][:, 64 + b : 65 + b]
        away = lax.rem(j + 2, 4)
        chosen = [
            jnp.where(partner == (quad + QUADS * away) * 3 + m, 1.0, 0.0) for m in range(3)
        ]
        return away, chosen

    @pl.loop(0, HEADS)
    def _(j):
        for b in range(3):
            near = rows_of(j * 3 + b)
            away, chosen = pairing(j, b)
            other = jnp.zeros((CAP, 2 * HD), F32)
            other_fill = jnp.zeros((1, CAP), F32)
            for m in range(3):
                other += placed[rows_of(away * 3 + m), HD:].astype(F32) * chosen[m]
                other_fill += fill_row[away * 3 + m][:1] * chosen[m]
            both = jnp.concatenate([placed[near, HD:], other.astype(BF16)], axis=0)
            key_set[j * 3 + b] = both
            live = jnp.concatenate([fill_row[j * 3 + b][:1], other_fill], axis=1)
            filled = fill_col[near, :1]
            scores = dot_general(placed[near, :HD], both[:, :HD], NT) * scale
            scores = jnp.where(live > 0, scores, -1e30)
            top = jnp.max(scores, axis=1, keepdims=True)
            weights = jnp.exp(scores - top) * live
            total = jnp.sum(weights, axis=1, keepdims=True) + (1.0 - filled)
            probs = weights * (filled / total)
            probs_scr[j * 3 + b] = probs
            res[near, :] = dot(probs.astype(BF16), both[:, HD:]).astype(BF16)

    for i in range(HEADS):
        c = lax.rem(first + i, HEADS)
        rows = dot(take[c], res[...]).astype(BF16)
        satt[pl.ds(c * QUADS, QUADS)] = rows.reshape(QUADS, MSG, HD)
        send_group(ATT, satt, ratt, c, i)

    for i in range(HEADS):
        c = lax.rem(first + HEADS - i, HEADS)
        wait_group(GA, sga, rga, c, i)
        term = dot(put[c], rga[pl.ds(c * QUADS, QUADS)].reshape(GROUP, HD))
        if i == 0:
            acc_g[...] = term
        elif i < HEADS - 1:
            acc_g[...] += term
        else:
            placed_g[...] = (acc_g[...] + term).astype(BF16)

    @pl.loop(0, HEADS)
    def _(j):
        for b in range(3):
            near = rows_of(j * 3 + b)
            both = key_set[j * 3 + b]
            probs = probs_scr[j * 3 + b]
            grad = placed_g[near, :]
            prob_grad = dot_general(grad, both[:, HD:], NT)
            inner = jnp.sum(probs * prob_grad, axis=1, keepdims=True)
            score_grad = (probs * (prob_grad - inner)).astype(BF16)
            res_g[near, :HD] = (dot(score_grad, both[:, :HD]) * scale).astype(BF16)
            key_grad = dot_general(score_grad, placed[near, :HD], TN) * scale
            val_grad = dot_general(probs.astype(BF16), grad, TN)
            own[near, :HD] = key_grad[:CAP]
            own[near, HD:] = val_grad[:CAP]
            far[near, :HD] = key_grad[CAP:].astype(BF16)
            far[near, HD:] = val_grad[CAP:].astype(BF16)

    @pl.loop(0, HEADS)
    def _(j):
        for b in range(3):
            near = rows_of(j * 3 + b)
            away, chosen = pairing(j, b)
            total = own[near, :]
            for m in range(3):
                total += far[rows_of(away * 3 + m), :].astype(F32) * chosen[m]
            res_g[near, HD:] = total.astype(BF16)

    for i in range(HEADS):
        c = lax.rem(first + i, HEADS)
        rows = dot(take[c], res_g[...]).astype(BF16)
        sback[pl.ds(c * QUADS, QUADS)] = rows.reshape(QUADS, MSG, 3 * HD)
        send_group(BACK, sback, rback, c, i)

    for i in range(HEADS):
        wait_group(ATT, satt, ratt, lax.rem(first + HEADS - i, HEADS), i)
    for h in range(HEADS):
        rows = ratt[h * QUADS : (h + 1) * QUADS].reshape(GROUP, HD)
        home = dot(pack_t[h], rows).astype(BF16)
        attn[:, :, h * HD : (h + 1) * HD] = home.reshape(N_HEAD, ROW, HD)

    def attn_half(n):
        return pl.ds(n * (N_HEAD // 2), N_HEAD // 2)

    def attn_copy(k, n, slot, source):
        _, who = x_peer(k)
        half = attn_half(n)
        block = attn_all.at[half, source]
        mine = attn.at[half] if slot < 2 else block
        return remote(mine, block, a_send.at[k // 2, slot], a_recv.at[k // 2, slot], who)

    right, left = 1, XN - 1
    attn_copy(right, 0, 0, mx).start()
    attn_copy(left, 1, 0, mx).start()
    attn_copy(right, 1, 1, mx).start()
    attn_copy(left, 0, 1, mx).start()
    attn_all[:, mx] = attn[...]
    before_x = lax.rem(mx + XN - 1, XN)
    after_x = lax.rem(mx + 1, XN)
    across_x = lax.rem(mx + 2, XN)
    mixed_rows = attn[...].reshape(TOK, HEADS * HD)
    for n in range(D // step):
        cols = slice(n * step, (n + 1) * step)
        term = dot_general(mixed_rows, proj[cols, :], NT)
        part[:, :, cols] = term.astype(BF16).reshape(N_HEAD, ROW, step)
    for k in range(1, N_HEAD):
        h, who = h_peer(k)
        remote(part.at[h], mixed_in.at[hm], m_send.at[h], m_recv.at[hm], who).start()
    mixed_in[hm] = part[hm]
    attn_copy(right, 0, 0, before_x).wait_recv()
    attn_copy(right, 0, 2, before_x).start()
    attn_copy(left, 1, 0, after_x).wait_recv()
    attn_copy(left, 1, 2, after_x).start()
    gather_end(1, gx, gall)
    attn_copy(right, 1, 1, before_x).wait_recv()
    attn_copy(left, 0, 1, after_x).wait_recv()
    attn_copy(right, 0, 2, across_x).wait_recv()
    attn_copy(left, 1, 2, across_x).wait_recv()
    for n in range(XN):
        group = attn_all[2 * n : 2 * n + 2].reshape(TOK, HEADS * HD)
        attn_t[:, n * TOK : (n + 1) * TOK] = group.T

    up_z = {"seq": lax.rem(mz + 1, ZN) * XN + mx}
    down_z = {"seq": lax.rem(mz + ZN - 1, ZN) * XN + mx}
    ring = ((up_z, ZN - 1), (down_z, 1))
    tall_half = HEADS * HD // 2

    def partial_of(z, d):
        grads = gall[:, :, pl.ds(z, 1)].reshape(XN * TOK, 128)
        return dot(attn_t[d * tall_half : (d + 1) * tall_half, :], grads).astype(BF16)

    def ring_copy(d, t):
        source = gp_part.at[d] if t == 0 else gp_acc.at[d, t - 1]
        return remote(source, gp_acc.at[d, t], p_send.at[d, t], p_recv.at[d, t], ring[d][0])

    for d in range(2):
        gp_part[d] = partial_of(lax.rem(mz + ring[d][1], ZN), d)
        ring_copy(d, 0).start()
    for t in range(1, ZN):
        terms = [
            partial_of(lax.rem(mz + ring[d][1] * (t + 1), ZN), d).astype(F32) for d in range(2)
        ]
        for d in range(2):
            ring_copy(d, t - 1).wait_recv()
            total = gp_acc[d, t - 1].astype(F32) + terms[d]
            if t < ZN - 1:
                gp_acc[d, t - 1] = total.astype(BF16)
                ring_copy(d, t).start()
            else:
                gp_ref[:, d * tall_half : (d + 1) * tall_half] = total.T.astype(BF16)

    for i in range(HEADS):
        wait_group(BACK, sback, rback, lax.rem(first + HEADS - i, HEADS), i)
    for h in range(HEADS):
        rows = rback[h * QUADS : (h + 1) * QUADS].reshape(GROUP, 3 * HD)
        home = dot(pack_t[h], rows)
        for n in range(3):
            xf[n, pl.ds(h, TOK, stride=HEADS), :] = home[:, n * HD : (n + 1) * HD]
    for n, ref in enumerate((dq_ref, dk_ref, dv_ref)):
        ref[...] = xf[n].astype(BF16)

    for k in range(1, N_HEAD):
        h, who = h_peer(k)
        remote(part.at[h], mixed_in.at[h], m_send.at[h], m_recv.at[h], who).wait()
    total = mixed_in[0].astype(F32)
    for h in range(1, N_HEAD):
        total += mixed_in[h].astype(F32)
    mixed_ref[...] = total.astype(BF16)

    @pl.loop(1, SEQ)
    def _(k):
        peer = lax.rem(me + k, SEQ)
        message(ID, sid, rid, peer).wait_send()
        message(QKV, sx, rx, peer).wait_send()
        message(GA, sga, rga, peer).wait_send()
        message(ATT, satt, ratt, peer).wait_send()
        message(BACK, sback, rback, peer).wait_send()

    attn_copy(right, 0, 0, mx).wait_send()
    attn_copy(right, 1, 1, mx).wait_send()
    attn_copy(right, 0, 2, before_x).wait_send()
    attn_copy(left, 1, 0, mx).wait_send()
    attn_copy(left, 0, 1, mx).wait_send()
    attn_copy(left, 1, 2, after_x).wait_send()
    for d in range(2):
        for t in range(ZN - 1):
            ring_copy(d, t).wait_send()


def layer(*args):
    vmem = pl.BlockSpec(memory_space=pltpu.VMEM)
    dma = pltpu.SemaphoreType.DMA
    wide = HEADS * HD
    flat = jax.ShapeDtypeStruct((TOK * HEADS, HD), BF16)

    def half(*shape):
        return pltpu.VMEM(shape, BF16)

    def full(*shape):
        return pltpu.VMEM(shape, F32)

    return pl.pallas_call(
        layer_kernel,
        out_shape=(
            jax.ShapeDtypeStruct((ROW, D), BF16), flat, flat, flat,
            jax.ShapeDtypeStruct((128, wide), BF16),
        ),
        in_specs=[vmem] * 6 + [pl.BlockSpec(memory_space=pl.ANY)],
        out_specs=(vmem,) * 5,
        scratch_shapes=[
            half(D, wide), full(3, TOK * HEADS, HD), half(HEADS, TOK, 3 * HD),
            half(HEADS, GROUP, TOK), half(HEADS, TOK, GROUP),
            half(SEQ, MSG, 3 * HD), pltpu.VMEM((SEQ, 1, 128), jnp.int32),
            half(SEQ, MSG, HD), half(SEQ, MSG, HD), half(SEQ, MSG, 3 * HD),
            half(SEQ, MSG, 3 * HD), pltpu.VMEM((SEQ, 1, 128), jnp.int32),
            half(SEQ, MSG, HD), half(SEQ, MSG, HD), half(SEQ, MSG, 3 * HD),
            full(TOK, wide), half(N_HEAD, ROW, D),
            half(XN, ZN, ROW, 128), half(XN, ZN, ROW, 128), half(N_HEAD, XN, ZN, ROW, 128),
            half(HEADS, ROWS, GROUP), half(HEADS, GROUP, ROWS),
            full(ROWS, 3 * HD), full(ROWS, HD), full(ROWS, 128), full(BLOCKS, 8, CAP),
            half(ROWS, 3 * HD), half(ROWS, HD), half(BLOCKS, 2 * CAP, 2 * HD),
            full(BLOCKS, CAP, 2 * CAP), full(ROWS, 2 * HD), half(ROWS, 2 * HD),
            half(ROWS, HD), half(ROWS, 3 * HD),
            half(N_HEAD, ROW, wide), half(N_HEAD, XN, ROW, wide), half(wide, XN * TOK),
            half(N_HEAD, ROW, D), half(N_HEAD, ROW, D),
            half(2, wide // 2, 128), half(2, ZN - 1, wide // 2, 128),
            dma, dma((5, SEQ)), dma((5, SEQ)), dma((2, 4)), dma((2, 4)), dma((2, 4)), dma((2, 4)),
            dma((XN,)), dma((XN,)), dma((2, 3)), dma((2, 3)),
            dma((N_HEAD,)), dma((N_HEAD,)), dma((2, ZN - 1)), dma((2, ZN - 1)),
        ],
        compiler_params=pltpu.CompilerParams(
            collective_id=0, has_side_effects=True, vmem_limit_bytes=VMEM_LIMIT
        ),
        name="layer",
    )(*args)


def shards(queries, keys_in, values, out_proj, out_grad, slot_index, partner_block):
    flat = (TOK * HEADS, HD)
    mixed, dq, dk, dv, gp = layer(
        queries.reshape(flat), keys_in.reshape(flat), values.reshape(flat),
        slot_index, partner_block, out_grad, out_proj,
    )
    shape = (TOK, HEADS, HD)
    return mixed, dq.reshape(shape), dk.reshape(shape), dv.reshape(shape), gp


def solution(mesh):
    placed = (
        P("seq", "head", None),
        P("seq", "head", None),
        P("seq", "head", None),
        P(None, "head"),
        P(("seq", "head"), None),
        P("head", "seq"),
        P("head", "seq"),
    )
    return jax.shard_map(
        shards,
        mesh=mesh,
        in_specs=placed,
        out_specs=(
            P(("seq", "head"), None),
            P("seq", "head", None),
            P("seq", "head", None),
            P("seq", "head", None),
            P("seq", "head"),
        ),
        check_vma=False,
    )
```

```python
import functools

import jax
import jax.numpy as jnp
from jax import lax
from jax.experimental import pallas as pl
from jax.experimental.pallas import tpu as pltpu
from jax.sharding import PartitionSpec as P

MESH = pl.DeviceIdType.MESH
CAP = 128
HD = 128
HEADS = 4
TOK = 256
SEQ = 32
N_HEAD = 8
OWNED = 384
PER = 12
MSG = HEADS * PER
QUADS = 8
ROWS = SEQ * MSG
BLOCKS = ROWS // CAP
D = 4096
XN = 4
ZN = 8
VMEM_LIMIT = 56 * 1024 * 1024
F32 = jnp.float32
BF16 = jnp.bfloat16


def iota(shape, dim):
    return lax.broadcasted_iota(jnp.int32, shape, dim)


def greet(peers):
    barrier = pltpu.get_barrier_semaphore()
    for peer in peers:
        pl.semaphore_signal(barrier, inc=1, device_id=peer, device_id_type=MESH)


def greeted(count):
    pl.semaphore_wait(pltpu.get_barrier_semaphore(), count)


def remote(src, dst, send_sem, recv_sem, peer):
    return pltpu.make_async_remote_copy(
        src_ref=src,
        dst_ref=dst,
        send_sem=send_sem,
        recv_sem=recv_sem,
        device_id=peer,
        device_id_type=MESH,
    )

NT = (((1,), (1,)), ((), ()))
TN = (((0,), (0,)), ((), ()))
ID, QKV, GA, ATT, BACK = range(5)
ROW = TOK // N_HEAD
GROUP = QUADS * MSG


def dot(a, b):
    return jnp.dot(a, b, preferred_element_type=F32)


def dot_general(a, b, dims):
    return lax.dot_general(a, b, dims, preferred_element_type=F32)


def hot(condition):
    return jnp.where(condition, 1.0, 0.0).astype(BF16)


def layer_kernel(
    slot_ref, partner_ref, q_hbm, k_hbm, v_hbm, grad_hbm, proj_hbm,
    mixed_ref, dq_ref, dk_ref, dv_ref, gp_ref,
    proj, raw, xf, x, pack, pack_t, sx, sid, sga, satt, sback, rx, rid, rga, ratt, rback,
    ga_scr, up, gs, gx, gall, put, take, acc, acc_g, fill_col, fill_row,
    placed, placed_g, key_set, probs_scr, own, far, res, res_g,
    attn, attn_all, attn_t, part, mixed_in, gp_part, gp_acc,
    in_sem, t_send, t_recv, up_send, up_recv, core_send, core_recv,
    gx_send, gx_recv, a_send, a_recv, m_send, m_recv, p_send, p_recv,
):
    me = lax.axis_index("seq")
    hm = lax.axis_index("head")
    mx = lax.rem(me, XN)
    mz = me // XN
    first = me // QUADS
    quad = lax.rem(me, QUADS)
    core = lax.rem(hm, 2)
    my = hm // 2
    sibling = {"head": my * 2 + 1 - core}
    loads = [
        pltpu.make_async_copy(source, target, in_sem.at[n])
        for n, (source, target) in enumerate(
            (
                (q_hbm, raw.at[0]), (k_hbm, raw.at[1]), (v_hbm, raw.at[2]),
                (grad_hbm, up.at[hm]), (proj_hbm, proj),
            )
        )
    ]
    for load in loads:
        load.start()

    def x_peer(k):
        to = lax.rem(mx + k, XN)
        return to, {"seq": mz * XN + to}

    def y_peer(k):
        to = lax.rem(my + k, 4)
        return to, {"head": to * 2 + core}

    def h_peer(k):
        to = lax.rem(hm + k, N_HEAD)
        return to, {"head": to}

    greet(
        [{"seq": lax.rem(me + k, SEQ)} for k in range(1, SEQ)]
        + [h_peer(k)[1] for k in range(1, N_HEAD)]
    )

    def gather_start(kind, src, out):
        for k in (1, 3, 2):
            _, who = y_peer(k)
            remote(src, out.at[hm], up_send.at[kind, k], up_recv.at[kind, my], who).start()
        remote(src, out.at[hm], core_send.at[kind, 0], core_recv.at[kind, my], sibling).start()

    def gather_forward(kind, src, out):
        for k in (1, 3, 2):
            y, who = y_peer(k)
            block = out.at[y * 2 + core]
            remote(src, block, up_send.at[kind, k], up_recv.at[kind, y], who).wait_recv()
            remote(block, block, core_send.at[kind, k], core_recv.at[kind, y], sibling).start()

    def gather_end(kind, src, out):
        for k in range(4):
            y, who = y_peer(k)
            block = out.at[y * 2 + 1 - core]
            remote(src, block, core_send.at[kind, k], core_recv.at[kind, y], sibling).wait()
            if k:
                remote(src, block, up_send.at[kind, k], up_recv.at[kind, y], who).wait_send()

    def send(kind, src, out, to):
        remote(src.at[to], out.at[me], t_send.at[kind, to], t_recv.at[kind, me], {"seq": to}).start()

    def message(kind, src, out, peer):
        return remote(
            src.at[peer], out.at[peer], t_send.at[kind, peer], t_recv.at[kind, peer], {"seq": peer}
        )

    def members(group, i):
        for k in range(QUADS):
            yield group * QUADS + lax.rem(quad + k, QUADS), i == 0 and k == 0

    def send_group(kind, src, out, group, i):
        for to, mine in members(group, i):
            if mine:
                out[me] = src[me]
            else:
                send(kind, src, out, to)

    def wait_group(kind, src, out, group, i):
        for peer, mine in members(group, i):
            if not mine:
                message(kind, src, out, peer).wait_recv()

    for n in range(3):
        loads[n].wait()
        xf[n] = raw[n].astype(F32)
    for h in range(HEADS):
        for n in range(3):
            x[h, :, n * HD : (n + 1) * HD] = xf[n, pl.ds(h, TOK, stride=HEADS), :].astype(BF16)

    owner_col = iota((SEQ, TOK), 0)
    before_mask = hot(iota((TOK, TOK), 0) < iota((TOK, TOK), 1))
    lane = iota((QUADS, 128), 1)
    lane_row = iota((1, 128), 1)
    quad_col = iota((QUADS, TOK), 0).astype(F32)
    row_col = iota((128, TOK), 0).astype(F32)
    base = ((owner_col % QUADS) * MSG + (owner_col // QUADS) * PER).astype(F32)
    for i in range(HEADS):
        h = lax.rem(first + i, HEADS)
        slots = slot_ref[pl.ds(h, 1), :]
        member = (slots >= owner_col * OWNED) & (slots < (owner_col + 1) * OWNED)
        one = jnp.where(member, 1.0, 0.0)
        before = dot(one.astype(BF16), before_mask)
        rank = jnp.sum(one * before, axis=0, keepdims=True)
        owner = jnp.sum(jnp.where(member, owner_col.astype(F32), 0.0), axis=0, keepdims=True)
        spot = jnp.sum(jnp.where(member, base, 0.0), axis=0, keepdims=True) + rank
        within = slots.astype(F32) - owner * OWNED
        block = jnp.where(within >= CAP, 1.0, 0.0) + jnp.where(within >= 2 * CAP, 1.0, 0.0)
        place = within - block * CAP
        row_part = jnp.floor(owner / QUADS)
        row = row_part * PER + rank
        here = quad_col == owner - row_part * QUADS
        at_row = hot(row_col == row)
        high = dot_general(jnp.where(here, block + 1.0, 0.0).astype(BF16), at_row, NT)
        low = dot_general(jnp.where(here, place, 0.0).astype(BF16), at_row, NT)
        ids = (lane // PER) * OWNED + ((high - 1.0) * CAP + low).astype(jnp.int32)
        ids = jnp.where(high > 0.5, ids, -1)
        pairs = partner_ref[pl.ds(h, 1), :]
        for b in range(3):
            ids = jnp.where(lane == 64 + b, pairs[:, b : b + 1], ids)
        for d in range(QUADS):
            sid[h * QUADS + d] = ids[d : d + 1]
        packing = hot(iota((GROUP, TOK), 0).astype(F32) == spot)
        pack[h] = packing
        sx[pl.ds(h * QUADS, QUADS)] = dot(packing, x[h]).astype(BF16).reshape(QUADS, MSG, 3 * HD)

    loads[3].wait()
    for xx in range(XN):
        for zz in range(ZN):
            chunk = zz * XN + xx
            gs[xx, zz] = up[hm, :, chunk * 128 : (chunk + 1) * 128]
    greeted(SEQ + N_HEAD - 2)
    for i in range(HEADS):
        h = lax.rem(first + i, HEADS)
        send_group(ID, sid, rid, h, i)
        send_group(QKV, sx, rx, h, i)
        if i == 0:
            gather_start(0, up.at[hm], up)
            for k in range(1, XN):
                to, who = x_peer(k)
                remote(gs.at[to], gx.at[mx], gx_send.at[k], gx_recv.at[mx], who).start()
            gx[mx] = gs[mx]

    gather_forward(0, up.at[hm], up)
    for k in range(1, XN):
        xx, who = x_peer(k)
        remote(gs.at[xx], gx.at[xx], gx_send.at[k], gx_recv.at[xx], who).wait()
    gather_start(1, gx, gall)
    gall[hm] = gx[...]
    gather_end(0, up.at[hm], up)
    loads[4].wait()
    step = 512
    for n in range(D // step):
        cols = slice(n * step, (n + 1) * step)
        term = dot(up[:, :, cols].reshape(TOK, step), proj[cols, :])
        if n == 0:
            ga_scr[...] = term
        else:
            ga_scr[...] += term
    for i in range(HEADS):
        h = lax.rem(first + i, HEADS)
        mine = ga_scr[:, pl.ds(pl.multiple_of(h * HD, HD), HD)].astype(BF16)
        sga[pl.ds(h * QUADS, QUADS)] = dot(pack[h], mine).astype(BF16).reshape(QUADS, MSG, HD)
    gather_forward(1, gx, gall)

    spread = hot(iota((128, GROUP), 0) == iota((128, GROUP), 1) % MSG)
    src_row = iota((QUADS, GROUP), 0) == iota((QUADS, GROUP), 1) // MSG
    pick = hot(iota((GROUP, QUADS), 0) // MSG == iota((GROUP, QUADS), 1))
    own_lane = iota((GROUP, 128), 1) == iota((GROUP, 128), 0) % MSG
    sub = iota((QUADS, 128), 0)
    for i in range(HEADS):
        c = lax.rem(first + HEADS - i, HEADS)
        wait_group(ID, sid, rid, c, i)
        ids = jnp.zeros((QUADS, 128), jnp.int32)
        for d in range(QUADS):
            ids = jnp.where(sub == d, rid[c * QUADS + d], ids)
        high = (ids >> 7).astype(F32).astype(BF16)
        low = (ids & 127).astype(F32).astype(BF16)
        wide = dot(high, spread) * CAP + dot(low, spread)
        ids_row = jnp.sum(jnp.where(src_row, wide, 0.0), axis=0, keepdims=True)
        tall = dot(pick, high) * CAP + dot(pick, low)
        ids_col = jnp.sum(jnp.where(own_lane, tall, 0.0), axis=1, keepdims=True)
        put[c] = hot(iota((ROWS, GROUP), 0).astype(F32) == ids_row)
        take[c] = hot(iota((GROUP, ROWS), 1).astype(F32) == ids_col)
        col = dot(put[c], jnp.ones((GROUP, 128), BF16))
        row = dot(jnp.ones((8, GROUP), BF16), take[c])
        if i == 0:
            fill_col[...] = col
        else:
            fill_col[...] += col
        for b in range(BLOCKS):
            piece = row[:, b * CAP : (b + 1) * CAP]
            if i == 0:
                fill_row[b] = piece
            else:
                fill_row[b] += piece
    for h in range(HEADS):
        pack_t[h] = pack[h].T
    for i in range(HEADS):
        c = lax.rem(first + HEADS - i, HEADS)
        wait_group(QKV, sx, rx, c, i)
        term = dot(put[c], rx[pl.ds(c * QUADS, QUADS)].reshape(GROUP, 3 * HD))
        if i == 0:
            acc[...] = term
        elif i < HEADS - 1:
            acc[...] += term
        else:
            for n in range(HEADS):
                send_group(GA, sga, rga, lax.rem(first + n, HEADS), n)
            placed[...] = (acc[...] + term).astype(BF16)

    scale = HD**-0.5

    def rows_of(b):
        return pl.ds(pl.multiple_of(b * CAP, CAP), CAP)

    def pairing(j, b):
        owner = quad + QUADS * j
        partner = rid[owner][:, 64 + b : 65 + b]
        away = lax.rem(j + 2, 4)
        chosen = [
            jnp.where(partner == (quad + QUADS * away) * 3 + m, 1.0, 0.0) for m in range(3)
        ]
        return away, chosen

    @pl.loop(0, HEADS)
    def _(j):
        for b in range(3):
            near = rows_of(j * 3 + b)
            away, chosen = pairing(j, b)
            other = jnp.zeros((CAP, 2 * HD), F32)
            other_fill = jnp.zeros((1, CAP), F32)
            for m in range(3):
                other += placed[rows_of(away * 3 + m), HD:].astype(F32) * chosen[m]
                other_fill += fill_row[away * 3 + m][:1] * chosen[m]
            both = jnp.concatenate([placed[near, HD:], other.astype(BF16)], axis=0)
            key_set[j * 3 + b] = both
            live = jnp.concatenate([fill_row[j * 3 + b][:1], other_fill], axis=1)
            filled = fill_col[near, :1]
            scores = dot_general(placed[near, :HD], both[:, :HD], NT) * scale
            scores = jnp.where(live > 0, scores, -1e30)
            top = jnp.max(scores, axis=1, keepdims=True)
            weights = jnp.exp(scores - top) * live
            total = jnp.sum(weights, axis=1, keepdims=True) + (1.0 - filled)
            probs = weights * (filled / total)
            probs_scr[j * 3 + b] = probs
            res[near, :] = dot(probs.astype(BF16), both[:, HD:]).astype(BF16)

    for i in range(HEADS):
        c = lax.rem(first + i, HEADS)
        rows = dot(take[c], res[...]).astype(BF16)
        satt[pl.ds(c * QUADS, QUADS)] = rows.reshape(QUADS, MSG, HD)
        send_group(ATT, satt, ratt, c, i)

    for i in range(HEADS):
        c = lax.rem(first + HEADS - i, HEADS)
        wait_group(GA, sga, rga, c, i)
        term = dot(put[c], rga[pl.ds(c * QUADS, QUADS)].reshape(GROUP, HD))
        if i == 0:
            acc_g[...] = term
        elif i < HEADS - 1:
            acc_g[...] += term
        else:
            placed_g[...] = (acc_g[...] + term).astype(BF16)

    @pl.loop(0, HEADS)
    def _(j):
        for b in range(3):
            near = rows_of(j * 3 + b)
            both = key_set[j * 3 + b]
            probs = probs_scr[j * 3 + b]
            grad = placed_g[near, :]
            prob_grad = dot_general(grad, both[:, HD:], NT)
            inner = jnp.sum(probs * prob_grad, axis=1, keepdims=True)
            score_grad = (probs * (prob_grad - inner)).astype(BF16)
            res_g[near, :HD] = (dot(score_grad, both[:, :HD]) * scale).astype(BF16)
            key_grad = dot_general(score_grad, placed[near, :HD], TN) * scale
            val_grad = dot_general(probs.astype(BF16), grad, TN)
            own[near, :HD] = key_grad[:CAP]
            own[near, HD:] = val_grad[:CAP]
            far[near, :HD] = key_grad[CAP:].astype(BF16)
            far[near, HD:] = val_grad[CAP:].astype(BF16)

    @pl.loop(0, HEADS)
    def _(j):
        for b in range(3):
            near = rows_of(j * 3 + b)
            away, chosen = pairing(j, b)
            total = own[near, :]
            for m in range(3):
                total += far[rows_of(away * 3 + m), :].astype(F32) * chosen[m]
            res_g[near, HD:] = total.astype(BF16)

    for i in range(HEADS):
        c = lax.rem(first + i, HEADS)
        rows = dot(take[c], res_g[...]).astype(BF16)
        sback[pl.ds(c * QUADS, QUADS)] = rows.reshape(QUADS, MSG, 3 * HD)

    for i in range(HEADS):
        wait_group(ATT, satt, ratt, lax.rem(first + HEADS - i, HEADS), i)
    for h in range(HEADS):
        rows = ratt[h * QUADS : (h + 1) * QUADS].reshape(GROUP, HD)
        home = dot(pack_t[h], rows).astype(BF16)
        attn[:, :, h * HD : (h + 1) * HD] = home.reshape(N_HEAD, ROW, HD)

    def back_batch(begin, end):
        for n in range(begin, end):
            i, k = n // QUADS, n % QUADS
            if n == 0:
                rback[me] = sback[me]
            else:
                group = lax.rem(first + i, HEADS)
                send(BACK, sback, rback, group * QUADS + lax.rem(quad + k, QUADS))

    def attn_half(n):
        return pl.ds(n * (N_HEAD // 2), N_HEAD // 2)

    def attn_copy(k, n, slot, source):
        _, who = x_peer(k)
        half = attn_half(n)
        block = attn_all.at[half, source]
        mine = attn.at[half] if slot < 2 else block
        return remote(mine, block, a_send.at[k // 2, slot], a_recv.at[k // 2, slot], who)

    right, left = 1, XN - 1
    attn_copy(right, 0, 0, mx).start()
    attn_copy(left, 1, 0, mx).start()
    attn_copy(right, 1, 1, mx).start()
    attn_copy(left, 0, 1, mx).start()
    back_batch(0, QUADS)
    attn_all[:, mx] = attn[...]
    before_x = lax.rem(mx + XN - 1, XN)
    after_x = lax.rem(mx + 1, XN)
    across_x = lax.rem(mx + 2, XN)
    mixed_rows = attn[...].reshape(TOK, HEADS * HD)
    for n in range(D // step):
        cols = slice(n * step, (n + 1) * step)
        term = dot_general(mixed_rows, proj[cols, :], NT)
        part[:, :, cols] = term.astype(BF16).reshape(N_HEAD, ROW, step)
    for k in range(1, N_HEAD):
        h, who = h_peer(k)
        remote(part.at[h], mixed_in.at[hm], m_send.at[h], m_recv.at[hm], who).start()
    mixed_in[hm] = part[hm]
    attn_copy(right, 0, 0, before_x).wait_recv()
    attn_copy(right, 0, 2, before_x).start()
    attn_copy(left, 1, 0, after_x).wait_recv()
    attn_copy(left, 1, 2, after_x).start()
    gather_end(1, gx, gall)
    attn_copy(right, 1, 1, before_x).wait_recv()
    attn_copy(left, 0, 1, after_x).wait_recv()
    attn_copy(right, 0, 2, across_x).wait_recv()
    attn_copy(left, 1, 2, across_x).wait_recv()
    for n in range(XN):
        group = attn_all[2 * n : 2 * n + 2].reshape(TOK, HEADS * HD)
        attn_t[:, n * TOK : (n + 1) * TOK] = group.T

    up_z = {"seq": lax.rem(mz + 1, ZN) * XN + mx}
    down_z = {"seq": lax.rem(mz + ZN - 1, ZN) * XN + mx}
    ring = ((up_z, ZN - 1), (down_z, 1))
    tall_half = HEADS * HD // 2

    def partial_of(z, d):
        grads = gall[:, :, pl.ds(z, 1)].reshape(XN * TOK, 128)
        return dot(attn_t[d * tall_half : (d + 1) * tall_half, :], grads).astype(BF16)

    def ring_copy(d, t):
        source = gp_part.at[d] if t == 0 else gp_acc.at[d, t - 1]
        return remote(source, gp_acc.at[d, t], p_send.at[d, t], p_recv.at[d, t], ring[d][0])

    def ring_term(d, t):
        return partial_of(lax.rem(mz + ring[d][1] * (t + 1), ZN), d)

    for d in range(2):
        gp_part[d] = ring_term(d, 0)
        ring_copy(d, 0).start()
    back_batch(QUADS, QUADS + 4)
    for t in range(1, ZN - 1):
        terms = [ring_term(d, t).astype(F32) for d in range(2)]
        for d in range(2):
            ring_copy(d, t - 1).wait_recv()
            gp_acc[d, t - 1] = (gp_acc[d, t - 1].astype(F32) + terms[d]).astype(BF16)
            ring_copy(d, t).start()
        if t < 6:
            back_batch(QUADS + 4 * t, QUADS + 4 * t + 4)
    terms = [ring_term(d, ZN - 1).astype(F32) for d in range(2)]

    for k in range(1, N_HEAD):
        h, who = h_peer(k)
        remote(part.at[h], mixed_in.at[h], m_send.at[h], m_recv.at[h], who).wait()
    total = mixed_in[0].astype(F32)
    for h in range(1, N_HEAD):
        total += mixed_in[h].astype(F32)
    mixed_ref[...] = total.astype(BF16)

    for d in range(2):
        ring_copy(d, ZN - 2).wait_recv()
        total = gp_acc[d, ZN - 2].astype(F32) + terms[d]
        gp_ref[:, d * tall_half : (d + 1) * tall_half] = total.T.astype(BF16)

    for i in range(HEADS):
        wait_group(BACK, sback, rback, lax.rem(first + HEADS - i, HEADS), i)
    for h in range(HEADS):
        rows = rback[h * QUADS : (h + 1) * QUADS].reshape(GROUP, 3 * HD)
        home = dot(pack_t[h], rows)
        for n in range(3):
            xf[n, pl.ds(h, TOK, stride=HEADS), :] = home[:, n * HD : (n + 1) * HD]
    for n, ref in enumerate((dq_ref, dk_ref, dv_ref)):
        ref[...] = xf[n].astype(BF16)

    @pl.loop(1, SEQ)
    def _(k):
        peer = lax.rem(me + k, SEQ)
        message(ID, sid, rid, peer).wait_send()
        message(QKV, sx, rx, peer).wait_send()
        message(GA, sga, rga, peer).wait_send()
        message(ATT, satt, ratt, peer).wait_send()
        message(BACK, sback, rback, peer).wait_send()

    attn_copy(right, 0, 0, mx).wait_send()
    attn_copy(right, 1, 1, mx).wait_send()
    attn_copy(right, 0, 2, before_x).wait_send()
    attn_copy(left, 1, 0, mx).wait_send()
    attn_copy(left, 0, 1, mx).wait_send()
    attn_copy(left, 1, 2, after_x).wait_send()
    for d in range(2):
        for t in range(ZN - 1):
            ring_copy(d, t).wait_send()


def layer(*args):
    vmem = pl.BlockSpec(memory_space=pltpu.VMEM)
    dma = pltpu.SemaphoreType.DMA
    wide = HEADS * HD
    flat = jax.ShapeDtypeStruct((TOK * HEADS, HD), BF16)

    def half(*shape):
        return pltpu.VMEM(shape, BF16)

    def full(*shape):
        return pltpu.VMEM(shape, F32)

    return pl.pallas_call(
        layer_kernel,
        out_shape=(
            jax.ShapeDtypeStruct((ROW, D), BF16), flat, flat, flat,
            jax.ShapeDtypeStruct((128, wide), BF16),
        ),
        in_specs=[vmem] * 2 + [pl.BlockSpec(memory_space=pl.ANY)] * 5,
        out_specs=(vmem,) * 5,
        scratch_shapes=[
            half(D, wide), half(3, TOK * HEADS, HD), full(3, TOK * HEADS, HD), half(HEADS, TOK, 3 * HD),
            half(HEADS, GROUP, TOK), half(HEADS, TOK, GROUP),
            half(SEQ, MSG, 3 * HD), pltpu.VMEM((SEQ, 1, 128), jnp.int32),
            half(SEQ, MSG, HD), half(SEQ, MSG, HD), half(SEQ, MSG, 3 * HD),
            half(SEQ, MSG, 3 * HD), pltpu.VMEM((SEQ, 1, 128), jnp.int32),
            half(SEQ, MSG, HD), half(SEQ, MSG, HD), half(SEQ, MSG, 3 * HD),
            full(TOK, wide), half(N_HEAD, ROW, D),
            half(XN, ZN, ROW, 128), half(XN, ZN, ROW, 128), half(N_HEAD, XN, ZN, ROW, 128),
            half(HEADS, ROWS, GROUP), half(HEADS, GROUP, ROWS),
            full(ROWS, 3 * HD), full(ROWS, HD), full(ROWS, 128), full(BLOCKS, 8, CAP),
            half(ROWS, 3 * HD), half(ROWS, HD), half(BLOCKS, 2 * CAP, 2 * HD),
            full(BLOCKS, CAP, 2 * CAP), full(ROWS, 2 * HD), half(ROWS, 2 * HD),
            half(ROWS, HD), half(ROWS, 3 * HD),
            half(N_HEAD, ROW, wide), half(N_HEAD, XN, ROW, wide), half(wide, XN * TOK),
            half(N_HEAD, ROW, D), half(N_HEAD, ROW, D),
            half(2, wide // 2, 128), half(2, ZN - 1, wide // 2, 128),
            dma((5,)), dma((5, SEQ)), dma((5, SEQ)), dma((2, 4)), dma((2, 4)), dma((2, 4)), dma((2, 4)),
            dma((XN,)), dma((XN,)), dma((2, 3)), dma((2, 3)),
            dma((N_HEAD,)), dma((N_HEAD,)), dma((2, ZN - 1)), dma((2, ZN - 1)),
        ],
        compiler_params=pltpu.CompilerParams(
            collective_id=0, has_side_effects=True, vmem_limit_bytes=VMEM_LIMIT
        ),
        name="layer",
    )(*args)


def deliver_kernel(*refs):
    count = len(refs) // 2
    sems = refs[-1]
    copies = [pltpu.make_async_copy(refs[n], refs[count + n], sems.at[n]) for n in range(count)]
    for copy in copies:
        copy.start()
    for copy in copies:
        copy.wait()


def deliver(*arrays):
    anywhere = pl.BlockSpec(memory_space=pl.ANY)
    return pl.pallas_call(
        deliver_kernel,
        out_shape=tuple(jax.ShapeDtypeStruct(a.shape, a.dtype) for a in arrays),
        in_specs=[anywhere] * len(arrays),
        out_specs=(anywhere,) * len(arrays),
        scratch_shapes=[pltpu.SemaphoreType.DMA((len(arrays),))],
        compiler_params=pltpu.CompilerParams(vmem_limit_bytes=VMEM_LIMIT),
        name="deliver",
    )(*arrays)


def shards(queries, keys_in, values, out_proj, out_grad, slot_index, partner_block):
    flat = (TOK * HEADS, HD)
    mixed, dq, dk, dv, gp = deliver(
        *layer(
            slot_index, partner_block,
            queries.reshape(flat), keys_in.reshape(flat), values.reshape(flat),
            out_grad, out_proj,
        )
    )
    shape = (TOK, HEADS, HD)
    return mixed, dq.reshape(shape), dk.reshape(shape), dv.reshape(shape), gp


def solution(mesh):
    placed = (
        P("seq", "head", None),
        P("seq", "head", None),
        P("seq", "head", None),
        P(None, "head"),
        P(("seq", "head"), None),
        P("head", "seq"),
        P("head", "seq"),
    )
    return jax.shard_map(
        shards,
        mesh=mesh,
        in_specs=placed,
        out_specs=(
            P(("seq", "head"), None),
            P("seq", "head", None),
            P("seq", "head", None),
            P("seq", "head", None),
            P("seq", "head"),
        ),
        check_vma=False,
    )
```

```python
import functools

import jax
import jax.numpy as jnp
from jax import lax
from jax.experimental import pallas as pl
from jax.experimental.pallas import tpu as pltpu
from jax.sharding import PartitionSpec as P

MESH = pl.DeviceIdType.MESH
CAP = 128
HD = 128
HEADS = 4
TOK = 256
SEQ = 32
N_HEAD = 8
OWNED = 384
PER = 12
MSG = HEADS * PER
QUADS = 8
ROWS = SEQ * MSG
BLOCKS = ROWS // CAP
D = 4096
XN = 4
ZN = 8
VMEM_LIMIT = 56 * 1024 * 1024
F32 = jnp.float32
BF16 = jnp.bfloat16


def iota(shape, dim):
    return lax.broadcasted_iota(jnp.int32, shape, dim)


def greet(peers):
    barrier = pltpu.get_barrier_semaphore()
    for peer in peers:
        pl.semaphore_signal(barrier, inc=1, device_id=peer, device_id_type=MESH)


def greeted(count):
    pl.semaphore_wait(pltpu.get_barrier_semaphore(), count)


def remote(src, dst, send_sem, recv_sem, peer):
    return pltpu.make_async_remote_copy(
        src_ref=src,
        dst_ref=dst,
        send_sem=send_sem,
        recv_sem=recv_sem,
        device_id=peer,
        device_id_type=MESH,
    )

NT = (((1,), (1,)), ((), ()))
TN = (((0,), (0,)), ((), ()))
ID, QKV, GA, ATT, BACK = range(5)
ROW = TOK // N_HEAD
GROUP = QUADS * MSG


def dot(a, b):
    return jnp.dot(a, b, preferred_element_type=F32)


def dot_general(a, b, dims):
    return lax.dot_general(a, b, dims, preferred_element_type=F32)


def hot(condition):
    return jnp.where(condition, 1.0, 0.0).astype(BF16)


def layer_kernel(
    slot_ref, partner_ref, q_hbm, k_hbm, v_hbm, grad_hbm, proj_hbm,
    mixed_ref, dq_ref, dk_ref, dv_ref, gp_ref,
    proj, raw, xf, x, pack, pack_t, sx, sid, sga, satt, sback, rx, rid, rga, ratt, rback,
    ga_scr, up, gs, gx, gall, put, take, acc, acc_g, fill_col, fill_row,
    placed, placed_g, key_set, probs_scr, own, far, res, res_g,
    attn, attn_all, attn_t, part, mixed_in, gp_part, gp_in,
    in_sem, t_send, t_recv, up_send, up_recv, core_send, core_recv,
    gx_send, gx_recv, a_send, a_recv, m_send, m_recv, p_send, p_recv,
):
    me = lax.axis_index("seq")
    hm = lax.axis_index("head")
    mx = lax.rem(me, XN)
    mz = me // XN
    first = me // QUADS
    quad = lax.rem(me, QUADS)
    core = lax.rem(hm, 2)
    my = hm // 2
    sibling = {"head": my * 2 + 1 - core}
    loads = [
        pltpu.make_async_copy(source, target, in_sem.at[n])
        for n, (source, target) in enumerate(
            (
                (q_hbm, raw.at[0]), (k_hbm, raw.at[1]), (v_hbm, raw.at[2]),
                (grad_hbm, up.at[hm]), (proj_hbm, proj),
            )
        )
    ]
    for load in loads:
        load.start()

    def x_peer(k):
        to = lax.rem(mx + k, XN)
        return to, {"seq": mz * XN + to}

    def y_peer(k):
        to = lax.rem(my + k, 4)
        return to, {"head": to * 2 + core}

    def h_peer(k):
        to = lax.rem(hm + k, N_HEAD)
        return to, {"head": to}

    greet(
        [{"seq": lax.rem(me + k, SEQ)} for k in range(1, SEQ)]
        + [h_peer(k)[1] for k in range(1, N_HEAD)]
    )

    def gather_start(kind, src, out):
        for k in (1, 3, 2):
            _, who = y_peer(k)
            remote(src, out.at[hm], up_send.at[kind, k], up_recv.at[kind, my], who).start()
        remote(src, out.at[hm], core_send.at[kind, 0], core_recv.at[kind, my], sibling).start()

    def gather_forward(kind, src, out):
        for k in (1, 3, 2):
            y, who = y_peer(k)
            block = out.at[y * 2 + core]
            remote(src, block, up_send.at[kind, k], up_recv.at[kind, y], who).wait_recv()
            remote(block, block, core_send.at[kind, k], core_recv.at[kind, y], sibling).start()

    def gather_end(kind, src, out):
        for k in range(4):
            y, who = y_peer(k)
            block = out.at[y * 2 + 1 - core]
            remote(src, block, core_send.at[kind, k], core_recv.at[kind, y], sibling).wait()
            if k:
                remote(src, block, up_send.at[kind, k], up_recv.at[kind, y], who).wait_send()

    def send(kind, src, out, to):
        remote(src.at[to], out.at[me], t_send.at[kind, to], t_recv.at[kind, me], {"seq": to}).start()

    def message(kind, src, out, peer):
        return remote(
            src.at[peer], out.at[peer], t_send.at[kind, peer], t_recv.at[kind, peer], {"seq": peer}
        )

    def members(group, i):
        for k in range(QUADS):
            yield group * QUADS + lax.rem(quad + k, QUADS), i == 0 and k == 0

    def send_group(kind, src, out, group, i):
        for to, mine in members(group, i):
            if mine:
                out[me] = src[me]
            else:
                send(kind, src, out, to)

    def wait_group(kind, src, out, group, i):
        for peer, mine in members(group, i):
            if not mine:
                message(kind, src, out, peer).wait_recv()

    for n in range(3):
        loads[n].wait()
        xf[n] = raw[n].astype(F32)
    for h in range(HEADS):
        for n in range(3):
            x[h, :, n * HD : (n + 1) * HD] = xf[n, pl.ds(h, TOK, stride=HEADS), :].astype(BF16)

    owner_col = iota((SEQ, TOK), 0)
    before_mask = hot(iota((TOK, TOK), 0) < iota((TOK, TOK), 1))
    lane = iota((QUADS, 128), 1)
    lane_row = iota((1, 128), 1)
    quad_col = iota((QUADS, TOK), 0).astype(F32)
    row_col = iota((128, TOK), 0).astype(F32)
    base = ((owner_col % QUADS) * MSG + (owner_col // QUADS) * PER).astype(F32)
    for i in range(HEADS):
        h = lax.rem(first + i, HEADS)
        slots = slot_ref[pl.ds(h, 1), :]
        member = (slots >= owner_col * OWNED) & (slots < (owner_col + 1) * OWNED)
        one = jnp.where(member, 1.0, 0.0)
        before = dot(one.astype(BF16), before_mask)
        rank = jnp.sum(one * before, axis=0, keepdims=True)
        owner = jnp.sum(jnp.where(member, owner_col.astype(F32), 0.0), axis=0, keepdims=True)
        spot = jnp.sum(jnp.where(member, base, 0.0), axis=0, keepdims=True) + rank
        within = slots.astype(F32) - owner * OWNED
        block = jnp.where(within >= CAP, 1.0, 0.0) + jnp.where(within >= 2 * CAP, 1.0, 0.0)
        place = within - block * CAP
        row_part = jnp.floor(owner / QUADS)
        row = row_part * PER + rank
        here = quad_col == owner - row_part * QUADS
        at_row = hot(row_col == row)
        high = dot_general(jnp.where(here, block + 1.0, 0.0).astype(BF16), at_row, NT)
        low = dot_general(jnp.where(here, place, 0.0).astype(BF16), at_row, NT)
        ids = (lane // PER) * OWNED + ((high - 1.0) * CAP + low).astype(jnp.int32)
        ids = jnp.where(high > 0.5, ids, -1)
        pairs = partner_ref[pl.ds(h, 1), :]
        for b in range(3):
            ids = jnp.where(lane == 64 + b, pairs[:, b : b + 1], ids)
        for d in range(QUADS):
            sid[h * QUADS + d] = ids[d : d + 1]
        packing = hot(iota((GROUP, TOK), 0).astype(F32) == spot)
        pack[h] = packing
        sx[pl.ds(h * QUADS, QUADS)] = dot(packing, x[h]).astype(BF16).reshape(QUADS, MSG, 3 * HD)
        if i == 0:
            greeted(SEQ + N_HEAD - 2)
        send_group(ID, sid, rid, h, i)
        send_group(QKV, sx, rx, h, i)
        if i == 0:
            loads[3].wait()
            gather_start(0, up.at[hm], up)

    for xx in range(XN):
        for zz in range(ZN):
            chunk = zz * XN + xx
            gs[xx, zz] = up[hm, :, chunk * 128 : (chunk + 1) * 128]
    for k in range(1, XN):
        to, who = x_peer(k)
        remote(gs.at[to], gx.at[mx], gx_send.at[k], gx_recv.at[mx], who).start()
    gx[mx] = gs[mx]
    gather_forward(0, up.at[hm], up)
    for k in range(1, XN):
        xx, who = x_peer(k)
        remote(gs.at[xx], gx.at[xx], gx_send.at[k], gx_recv.at[xx], who).wait()
    gather_start(1, gx, gall)
    gall[hm] = gx[...]
    gather_end(0, up.at[hm], up)
    loads[4].wait()
    step = 512
    for n in range(D // step):
        cols = slice(n * step, (n + 1) * step)
        term = dot(up[:, :, cols].reshape(TOK, step), proj[cols, :])
        if n == 0:
            ga_scr[...] = term
        else:
            ga_scr[...] += term
    for i in range(HEADS):
        h = lax.rem(first + i, HEADS)
        mine = ga_scr[:, pl.ds(pl.multiple_of(h * HD, HD), HD)].astype(BF16)
        sga[pl.ds(h * QUADS, QUADS)] = dot(pack[h], mine).astype(BF16).reshape(QUADS, MSG, HD)
        send_group(GA, sga, rga, h, i)
    gather_forward(1, gx, gall)

    spread = hot(iota((128, GROUP), 0) == iota((128, GROUP), 1) % MSG)
    src_row = iota((QUADS, GROUP), 0) == iota((QUADS, GROUP), 1) // MSG
    pick = hot(iota((GROUP, QUADS), 0) // MSG == iota((GROUP, QUADS), 1))
    own_lane = iota((GROUP, 128), 1) == iota((GROUP, 128), 0) % MSG
    sub = iota((QUADS, 128), 0)
    for i in range(HEADS):
        c = lax.rem(first + HEADS - i, HEADS)
        wait_group(ID, sid, rid, c, i)
        ids = jnp.zeros((QUADS, 128), jnp.int32)
        for d in range(QUADS):
            ids = jnp.where(sub == d, rid[c * QUADS + d], ids)
        high = (ids >> 7).astype(F32).astype(BF16)
        low = (ids & 127).astype(F32).astype(BF16)
        wide = dot(high, spread) * CAP + dot(low, spread)
        ids_row = jnp.sum(jnp.where(src_row, wide, 0.0), axis=0, keepdims=True)
        tall = dot(pick, high) * CAP + dot(pick, low)
        ids_col = jnp.sum(jnp.where(own_lane, tall, 0.0), axis=1, keepdims=True)
        put[c] = hot(iota((ROWS, GROUP), 0).astype(F32) == ids_row)
        take[c] = hot(iota((GROUP, ROWS), 1).astype(F32) == ids_col)
        col = dot(put[c], jnp.ones((GROUP, 128), BF16))
        row = dot(jnp.ones((8, GROUP), BF16), take[c])
        if i == 0:
            fill_col[...] = col
        else:
            fill_col[...] += col
        for b in range(BLOCKS):
            piece = row[:, b * CAP : (b + 1) * CAP]
            if i == 0:
                fill_row[b] = piece
            else:
                fill_row[b] += piece
    for h in range(HEADS):
        pack_t[h] = pack[h].T
    for i in range(HEADS):
        c = lax.rem(first + HEADS - i, HEADS)
        wait_group(QKV, sx, rx, c, i)
        term = dot(put[c], rx[pl.ds(c * QUADS, QUADS)].reshape(GROUP, 3 * HD))
        if i == 0:
            acc[...] = term
        elif i < HEADS - 1:
            acc[...] += term
        else:
            placed[...] = (acc[...] + term).astype(BF16)

    scale = HD**-0.5

    def rows_of(b):
        return pl.ds(pl.multiple_of(b * CAP, CAP), CAP)

    def pairing(j, b):
        owner = quad + QUADS * j
        partner = rid[owner][:, 64 + b : 65 + b]
        away = lax.rem(j + 2, 4)
        chosen = [
            jnp.where(partner == (quad + QUADS * away) * 3 + m, 1.0, 0.0) for m in range(3)
        ]
        return away, chosen

    @pl.loop(0, HEADS)
    def _(j):
        for b in range(3):
            near = rows_of(j * 3 + b)
            away, chosen = pairing(j, b)
            other = jnp.zeros((CAP, 2 * HD), F32)
            other_fill = jnp.zeros((1, CAP), F32)
            for m in range(3):
                other += placed[rows_of(away * 3 + m), HD:].astype(F32) * chosen[m]
                other_fill += fill_row[away * 3 + m][:1] * chosen[m]
            both = jnp.concatenate([placed[near, HD:], other.astype(BF16)], axis=0)
            key_set[j * 3 + b] = both
            live = jnp.concatenate([fill_row[j * 3 + b][:1], other_fill], axis=1)
            filled = fill_col[near, :1]
            scores = dot_general(placed[near, :HD], both[:, :HD], NT) * scale
            scores = jnp.where(live > 0, scores, -1e30)
            top = jnp.max(scores, axis=1, keepdims=True)
            weights = jnp.exp(scores - top) * live
            total = jnp.sum(weights, axis=1, keepdims=True) + (1.0 - filled)
            probs = weights * (filled / total)
            probs_scr[j * 3 + b] = probs
            res[near, :] = dot(probs.astype(BF16), both[:, HD:]).astype(BF16)

    for i in range(HEADS):
        c = lax.rem(first + i, HEADS)
        rows = dot(take[c], res[...]).astype(BF16)
        satt[pl.ds(c * QUADS, QUADS)] = rows.reshape(QUADS, MSG, HD)
        send_group(ATT, satt, ratt, c, i)

    for i in range(HEADS):
        c = lax.rem(first + HEADS - i, HEADS)
        wait_group(GA, sga, rga, c, i)
        term = dot(put[c], rga[pl.ds(c * QUADS, QUADS)].reshape(GROUP, HD))
        if i == 0:
            acc_g[...] = term
        elif i < HEADS - 1:
            acc_g[...] += term
        else:
            placed_g[...] = (acc_g[...] + term).astype(BF16)

    @pl.loop(0, HEADS)
    def _(j):
        for b in range(3):
            near = rows_of(j * 3 + b)
            both = key_set[j * 3 + b]
            probs = probs_scr[j * 3 + b]
            grad = placed_g[near, :]
            prob_grad = dot_general(grad, both[:, HD:], NT)
            inner = jnp.sum(probs * prob_grad, axis=1, keepdims=True)
            score_grad = (probs * (prob_grad - inner)).astype(BF16)
            res_g[near, :HD] = (dot(score_grad, both[:, :HD]) * scale).astype(BF16)
            key_grad = dot_general(score_grad, placed[near, :HD], TN) * scale
            val_grad = dot_general(probs.astype(BF16), grad, TN)
            own[near, :HD] = key_grad[:CAP]
            own[near, HD:] = val_grad[:CAP]
            far[near, :HD] = key_grad[CAP:].astype(BF16)
            far[near, HD:] = val_grad[CAP:].astype(BF16)

    @pl.loop(0, HEADS)
    def _(j):
        for b in range(3):
            near = rows_of(j * 3 + b)
            away, chosen = pairing(j, b)
            total = own[near, :]
            for m in range(3):
                total += far[rows_of(away * 3 + m), :].astype(F32) * chosen[m]
            res_g[near, HD:] = total.astype(BF16)

    for i in range(HEADS):
        c = lax.rem(first + i, HEADS)
        rows = dot(take[c], res_g[...]).astype(BF16)
        sback[pl.ds(c * QUADS, QUADS)] = rows.reshape(QUADS, MSG, 3 * HD)
        send_group(BACK, sback, rback, c, i)

    for i in range(HEADS):
        wait_group(ATT, satt, ratt, lax.rem(first + HEADS - i, HEADS), i)
    for h in range(HEADS):
        rows = ratt[h * QUADS : (h + 1) * QUADS].reshape(GROUP, HD)
        home = dot(pack_t[h], rows).astype(BF16)
        attn[:, :, h * HD : (h + 1) * HD] = home.reshape(N_HEAD, ROW, HD)

    def attn_half(n):
        return pl.ds(n * (N_HEAD // 2), N_HEAD // 2)

    def attn_copy(k, n, slot, source):
        _, who = x_peer(k)
        half = attn_half(n)
        block = attn_all.at[half, source]
        mine = attn.at[half] if slot < 2 else block
        return remote(mine, block, a_send.at[k // 2, slot], a_recv.at[k // 2, slot], who)

    right, left = 1, XN - 1
    attn_copy(right, 0, 0, mx).start()
    attn_copy(left, 1, 0, mx).start()
    attn_copy(right, 1, 1, mx).start()
    attn_copy(left, 0, 1, mx).start()
    attn_all[:, mx] = attn[...]
    before_x = lax.rem(mx + XN - 1, XN)
    after_x = lax.rem(mx + 1, XN)
    across_x = lax.rem(mx + 2, XN)
    mixed_rows = attn[...].reshape(TOK, HEADS * HD)
    for n in range(D // step):
        cols = slice(n * step, (n + 1) * step)
        term = dot_general(mixed_rows, proj[cols, :], NT)
        part[:, :, cols] = term.astype(BF16).reshape(N_HEAD, ROW, step)
    for k in range(1, N_HEAD):
        h, who = h_peer(k)
        remote(part.at[h], mixed_in.at[hm], m_send.at[h], m_recv.at[hm], who).start()
    mixed_in[hm] = part[hm]
    attn_copy(right, 0, 0, before_x).wait_recv()
    attn_copy(right, 0, 2, before_x).start()
    attn_copy(left, 1, 0, after_x).wait_recv()
    attn_copy(left, 1, 2, after_x).start()
    gather_end(1, gx, gall)
    attn_copy(right, 1, 1, before_x).wait_recv()
    attn_copy(left, 0, 1, after_x).wait_recv()
    attn_copy(right, 0, 2, across_x).wait_recv()
    attn_copy(left, 1, 2, across_x).wait_recv()
    for n in range(XN):
        group = attn_all[2 * n : 2 * n + 2].reshape(TOK, HEADS * HD)
        attn_t[:, n * TOK : (n + 1) * TOK] = group.T

    tall_half = HEADS * HD // 2

    def at_z(offset):
        return lax.rem(mz + ZN + offset, ZN)

    def partial_of(offset):
        grads = gall[:, :, pl.ds(at_z(offset), 1)].reshape(XN * TOK, 128)
        return dot(attn_t[...], grads)

    hops = {0: -2, 1: -1, 2: 1, 3: -2, 4: -1, 5: 2, 6: 1}

    def tree_copy(d, slot):
        sign = 1 if d == 0 else -1
        who = {"seq": at_z(sign * hops[slot]) * XN + mx}
        return remote(
            gp_part.at[d, slot], gp_in.at[d, slot], p_send.at[d, slot], p_recv.at[d, slot], who
        )

    def tree_sends(offset, slots):
        chunk = partial_of(offset).astype(BF16)
        for d in range(2):
            gp_part[d, slots[d]] = chunk[d * tall_half : (d + 1) * tall_half]
            tree_copy(d, slots[d]).start()

    for offset, slots in ((4, (0, 0)), (-3, (1, 2)), (3, (2, 1)), (-1, (4, 6)), (1, (6, 4))):
        tree_sends(offset, slots)
    behind, ahead, mine = partial_of(-2), partial_of(2), partial_of(0)
    for d, slot, chunk in ((0, 5, ahead), (1, 5, behind), (0, 3, behind), (1, 3, ahead)):
        total = chunk[d * tall_half : (d + 1) * tall_half]
        for n in (0, 1) if slot == 3 else (2,):
            tree_copy(d, n).wait_recv()
            total += gp_in[d, n].astype(F32)
        gp_part[d, slot] = total.astype(BF16)
        tree_copy(d, slot).start()

    for k in range(1, N_HEAD):
        h, who = h_peer(k)
        remote(part.at[h], mixed_in.at[h], m_send.at[h], m_recv.at[h], who).wait()
    total = mixed_in[0].astype(F32)
    for h in range(1, N_HEAD):
        total += mixed_in[h].astype(F32)
    mixed_ref[...] = total.astype(BF16)

    for i in range(HEADS):
        wait_group(BACK, sback, rback, lax.rem(first + HEADS - i, HEADS), i)
    for h in range(HEADS):
        rows = rback[h * QUADS : (h + 1) * QUADS].reshape(GROUP, 3 * HD)
        home = dot(pack_t[h], rows)
        for n in range(3):
            xf[n, pl.ds(h, TOK, stride=HEADS), :] = home[:, n * HD : (n + 1) * HD]
    for n, ref in enumerate((dq_ref, dk_ref, dv_ref)):
        ref[...] = xf[n].astype(BF16)

    for d in range(2):
        total = mine[d * tall_half : (d + 1) * tall_half]
        for slot in (3, 4, 5, 6):
            tree_copy(d, slot).wait_recv()
            total += gp_in[d, slot].astype(F32)
        gp_ref[:, d * tall_half : (d + 1) * tall_half] = total.T.astype(BF16)

    @pl.loop(1, SEQ)
    def _(k):
        peer = lax.rem(me + k, SEQ)
        message(ID, sid, rid, peer).wait_send()
        message(QKV, sx, rx, peer).wait_send()
        message(GA, sga, rga, peer).wait_send()
        message(ATT, satt, ratt, peer).wait_send()
        message(BACK, sback, rback, peer).wait_send()

    attn_copy(right, 0, 0, mx).wait_send()
    attn_copy(right, 1, 1, mx).wait_send()
    attn_copy(right, 0, 2, before_x).wait_send()
    attn_copy(left, 1, 0, mx).wait_send()
    attn_copy(left, 0, 1, mx).wait_send()
    attn_copy(left, 1, 2, after_x).wait_send()
    for d in range(2):
        for slot in range(7):
            tree_copy(d, slot).wait_send()


def layer(*args):
    vmem = pl.BlockSpec(memory_space=pltpu.VMEM)
    dma = pltpu.SemaphoreType.DMA
    wide = HEADS * HD
    flat = jax.ShapeDtypeStruct((TOK * HEADS, HD), BF16)

    def half(*shape):
        return pltpu.VMEM(shape, BF16)

    def full(*shape):
        return pltpu.VMEM(shape, F32)

    return pl.pallas_call(
        layer_kernel,
        out_shape=(
            jax.ShapeDtypeStruct((ROW, D), BF16), flat, flat, flat,
            jax.ShapeDtypeStruct((128, wide), BF16),
        ),
        in_specs=[vmem] * 2 + [pl.BlockSpec(memory_space=pl.ANY)] * 5,
        out_specs=(vmem,) * 5,
        scratch_shapes=[
            half(D, wide), half(3, TOK * HEADS, HD), full(3, TOK * HEADS, HD), half(HEADS, TOK, 3 * HD),
            half(HEADS, GROUP, TOK), half(HEADS, TOK, GROUP),
            half(SEQ, MSG, 3 * HD), pltpu.VMEM((SEQ, 1, 128), jnp.int32),
            half(SEQ, MSG, HD), half(SEQ, MSG, HD), half(SEQ, MSG, 3 * HD),
            half(SEQ, MSG, 3 * HD), pltpu.VMEM((SEQ, 1, 128), jnp.int32),
            half(SEQ, MSG, HD), half(SEQ, MSG, HD), half(SEQ, MSG, 3 * HD),
            full(TOK, wide), half(N_HEAD, ROW, D),
            half(XN, ZN, ROW, 128), half(XN, ZN, ROW, 128), half(N_HEAD, XN, ZN, ROW, 128),
            half(HEADS, ROWS, GROUP), half(HEADS, GROUP, ROWS),
            full(ROWS, 3 * HD), full(ROWS, HD), full(ROWS, 128), full(BLOCKS, 8, CAP),
            half(ROWS, 3 * HD), half(ROWS, HD), half(BLOCKS, 2 * CAP, 2 * HD),
            full(BLOCKS, CAP, 2 * CAP), full(ROWS, 2 * HD), half(ROWS, 2 * HD),
            half(ROWS, HD), half(ROWS, 3 * HD),
            half(N_HEAD, ROW, wide), half(N_HEAD, XN, ROW, wide), half(wide, XN * TOK),
            half(N_HEAD, ROW, D), half(N_HEAD, ROW, D),
            half(2, 7, wide // 2, 128), half(2, 7, wide // 2, 128),
            dma((5,)), dma((5, SEQ)), dma((5, SEQ)), dma((2, 4)), dma((2, 4)), dma((2, 4)), dma((2, 4)),
            dma((XN,)), dma((XN,)), dma((2, 3)), dma((2, 3)),
            dma((N_HEAD,)), dma((N_HEAD,)), dma((2, 7)), dma((2, 7)),
        ],
        compiler_params=pltpu.CompilerParams(
            collective_id=0, has_side_effects=True, vmem_limit_bytes=VMEM_LIMIT
        ),
        name="layer",
    )(*args)


def deliver_kernel(*refs):
    count = len(refs) // 2
    for n in range(count):
        refs[count + n][...] = refs[n][...]


def deliver(*arrays):
    vmem = pl.BlockSpec(memory_space=pltpu.VMEM)
    return pl.pallas_call(
        deliver_kernel,
        out_shape=tuple(jax.ShapeDtypeStruct(a.shape, a.dtype) for a in arrays),
        in_specs=[vmem] * len(arrays),
        out_specs=(vmem,) * len(arrays),
        compiler_params=pltpu.CompilerParams(vmem_limit_bytes=VMEM_LIMIT),
        name="deliver",
    )(*arrays)


def shards(queries, keys_in, values, out_proj, out_grad, slot_index, partner_block):
    flat = (TOK * HEADS, HD)
    mixed, dq, dk, dv, gp = deliver(
        *layer(
            slot_index, partner_block,
            queries.reshape(flat), keys_in.reshape(flat), values.reshape(flat),
            out_grad, out_proj,
        )
    )
    shape = (TOK, HEADS, HD)
    return mixed, dq.reshape(shape), dk.reshape(shape), dv.reshape(shape), gp


def solution(mesh):
    placed = (
        P("seq", "head", None),
        P("seq", "head", None),
        P("seq", "head", None),
        P(None, "head"),
        P(("seq", "head"), None),
        P("head", "seq"),
        P("head", "seq"),
    )
    return jax.shard_map(
        shards,
        mesh=mesh,
        in_specs=placed,
        out_specs=(
            P(("seq", "head"), None),
            P("seq", "head", None),
            P("seq", "head", None),
            P("seq", "head", None),
            P("seq", "head"),
        ),
        check_vma=False,
    )
```

```python
import functools

import jax
import jax.numpy as jnp
from jax import lax
from jax.experimental import pallas as pl
from jax.experimental.pallas import tpu as pltpu
from jax.sharding import PartitionSpec as P

MESH = pl.DeviceIdType.MESH
CAP = 128
HD = 128
HEADS = 4
TOK = 256
SEQ = 32
N_HEAD = 8
OWNED = 384
PER = 12
MSG = HEADS * PER
QUADS = 8
ROWS = SEQ * MSG
BLOCKS = ROWS // CAP
D = 4096
XN = 4
ZN = 8
VMEM_LIMIT = 56 * 1024 * 1024
F32 = jnp.float32
BF16 = jnp.bfloat16


def iota(shape, dim):
    return lax.broadcasted_iota(jnp.int32, shape, dim)


def greet(peers):
    barrier = pltpu.get_barrier_semaphore()
    for peer in peers:
        pl.semaphore_signal(barrier, inc=1, device_id=peer, device_id_type=MESH)


def greeted(count):
    pl.semaphore_wait(pltpu.get_barrier_semaphore(), count)


def remote(src, dst, send_sem, recv_sem, peer):
    return pltpu.make_async_remote_copy(
        src_ref=src,
        dst_ref=dst,
        send_sem=send_sem,
        recv_sem=recv_sem,
        device_id=peer,
        device_id_type=MESH,
    )

NT = (((1,), (1,)), ((), ()))
TN = (((0,), (0,)), ((), ()))
ID, QKV, GA, ATT, BACK = range(5)
ROW = TOK // N_HEAD
GROUP = QUADS * MSG


def dot(a, b):
    return jnp.dot(a, b, preferred_element_type=F32)


def dot_general(a, b, dims):
    return lax.dot_general(a, b, dims, preferred_element_type=F32)


def hot(condition):
    return jnp.where(condition, 1.0, 0.0).astype(BF16)


def layer_kernel(
    slot_ref, partner_ref, q_hbm, k_hbm, v_hbm, grad_hbm, proj_hbm,
    mixed_ref, dq_ref, dk_ref, dv_ref, gp_ref,
    proj, raw, xf, x, pack, pack_t, sx, sid, sga, satt, sback, rx, rid, rga, ratt, rback,
    ga_scr, up, gs, gx, gall, put, take, acc, acc_g, fill_col, fill_row,
    placed, placed_g, key_set, probs_scr, own, far, res, res_g,
    attn, attn_all, attn_t, part, mixed_in, gp_part, gp_in,
    in_sem, t_send, t_recv, up_send, up_recv, core_send, core_recv,
    gx_send, gx_recv, a_send, a_recv, m_send, m_recv, p_send, p_recv,
):
    me = lax.axis_index("seq")
    hm = lax.axis_index("head")
    mx = lax.rem(me, XN)
    mz = me // XN
    first = me // QUADS
    quad = lax.rem(me, QUADS)
    core = lax.rem(hm, 2)
    my = hm // 2
    sibling = {"head": my * 2 + 1 - core}
    loads = [
        pltpu.make_async_copy(source, target, in_sem.at[n])
        for n, (source, target) in enumerate(
            (
                (q_hbm, raw.at[0]), (k_hbm, raw.at[1]), (v_hbm, raw.at[2]),
                (grad_hbm, up.at[hm]), (proj_hbm, proj),
            )
        )
    ]
    for load in loads:
        load.start()

    def x_peer(k):
        to = lax.rem(mx + k, XN)
        return to, {"seq": mz * XN + to}

    def y_peer(k):
        to = lax.rem(my + k, 4)
        return to, {"head": to * 2 + core}

    def h_peer(k):
        to = lax.rem(hm + k, N_HEAD)
        return to, {"head": to}

    greet(
        [{"seq": lax.rem(me + k, SEQ)} for k in range(1, SEQ)]
        + [h_peer(k)[1] for k in range(1, N_HEAD)]
    )

    def gather_start(kind, src, out):
        for k in (1, 3, 2):
            _, who = y_peer(k)
            remote(src, out.at[hm], up_send.at[kind, k], up_recv.at[kind, my], who).start()
        remote(src, out.at[hm], core_send.at[kind, 0], core_recv.at[kind, my], sibling).start()

    def gather_forward(kind, src, out):
        for k in (1, 3, 2):
            y, who = y_peer(k)
            block = out.at[y * 2 + core]
            remote(src, block, up_send.at[kind, k], up_recv.at[kind, y], who).wait_recv()
            remote(block, block, core_send.at[kind, k], core_recv.at[kind, y], sibling).start()

    def gather_end(kind, src, out):
        for k in range(4):
            y, who = y_peer(k)
            block = out.at[y * 2 + 1 - core]
            remote(src, block, core_send.at[kind, k], core_recv.at[kind, y], sibling).wait()
            if k:
                remote(src, block, up_send.at[kind, k], up_recv.at[kind, y], who).wait_send()

    def send(kind, src, out, to):
        remote(
            src.at[to], out.at[me], t_send.at[kind], t_recv.at[kind, first], {"seq": to}
        ).start()

    def arrivals(kind, src, out, begin, count, group):
        part = pl.ds(begin, count)
        who = {"seq": lax.rem(me + 1, SEQ)}
        return remote(src.at[part], out.at[part], t_send.at[kind], t_recv.at[kind, group], who)

    def members(group, i):
        for k in range(QUADS):
            yield group * QUADS + lax.rem(quad + k, QUADS), i == 0 and k == 0

    def send_group(kind, src, out, group, i):
        for to, mine in members(group, i):
            if mine:
                out[me] = src[me]
            else:
                send(kind, src, out, to)

    def wait_group(kind, src, out, group, i):
        count = QUADS - 1 if i == 0 else QUADS
        arrivals(kind, src, out, group * QUADS, count, group).wait_recv()

    for n in range(3):
        loads[n].wait()
        xf[n] = raw[n].astype(F32)
    for h in range(HEADS):
        for n in range(3):
            x[h, :, n * HD : (n + 1) * HD] = xf[n, pl.ds(h, TOK, stride=HEADS), :].astype(BF16)

    owner_col = iota((SEQ, TOK), 0)
    before_mask = hot(iota((TOK, TOK), 0) < iota((TOK, TOK), 1))
    lane = iota((QUADS, 128), 1)
    lane_row = iota((1, 128), 1)
    quad_col = iota((QUADS, TOK), 0).astype(F32)
    row_col = iota((128, TOK), 0).astype(F32)
    base = ((owner_col % QUADS) * MSG + (owner_col // QUADS) * PER).astype(F32)
    for i in range(HEADS):
        h = lax.rem(first + i, HEADS)
        slots = slot_ref[pl.ds(h, 1), :]
        member = (slots >= owner_col * OWNED) & (slots < (owner_col + 1) * OWNED)
        one = jnp.where(member, 1.0, 0.0)
        before = dot(one.astype(BF16), before_mask)
        rank = jnp.sum(one * before, axis=0, keepdims=True)
        owner = jnp.sum(jnp.where(member, owner_col.astype(F32), 0.0), axis=0, keepdims=True)
        spot = jnp.sum(jnp.where(member, base, 0.0), axis=0, keepdims=True) + rank
        within = slots.astype(F32) - owner * OWNED
        block = jnp.where(within >= CAP, 1.0, 0.0) + jnp.where(within >= 2 * CAP, 1.0, 0.0)
        place = within - block * CAP
        row_part = jnp.floor(owner / QUADS)
        row = row_part * PER + rank
        here = quad_col == owner - row_part * QUADS
        at_row = hot(row_col == row)
        high = dot_general(jnp.where(here, block + 1.0, 0.0).astype(BF16), at_row, NT)
        low = dot_general(jnp.where(here, place, 0.0).astype(BF16), at_row, NT)
        ids = (lane // PER) * OWNED + ((high - 1.0) * CAP + low).astype(jnp.int32)
        ids = jnp.where(high > 0.5, ids, -1)
        pairs = partner_ref[pl.ds(h, 1), :]
        for b in range(3):
            ids = jnp.where(lane == 64 + b, pairs[:, b : b + 1], ids)
        for d in range(QUADS):
            sid[h * QUADS + d] = ids[d : d + 1]
        packing = hot(iota((GROUP, TOK), 0).astype(F32) == spot)
        pack[h] = packing
        sx[pl.ds(h * QUADS, QUADS)] = dot(packing, x[h]).astype(BF16).reshape(QUADS, MSG, 3 * HD)
        if i == 0:
            greeted(SEQ + N_HEAD - 2)
        send_group(QKV, sx, rx, h, i)
        send_group(ID, sid, rid, h, i)
        if i == 0:
            loads[3].wait()
            gather_start(0, up.at[hm], up)

    for xx in range(XN):
        for zz in range(ZN):
            chunk = zz * XN + xx
            gs[xx, zz] = up[hm, :, chunk * 128 : (chunk + 1) * 128]
    for k in range(1, XN):
        to, who = x_peer(k)
        remote(gs.at[to], gx.at[mx], gx_send.at[k], gx_recv.at[mx], who).start()
    gx[mx] = gs[mx]
    gather_forward(0, up.at[hm], up)
    for k in range(1, XN):
        xx, who = x_peer(k)
        remote(gs.at[xx], gx.at[xx], gx_send.at[k], gx_recv.at[xx], who).wait()
    gather_start(1, gx, gall)
    gall[hm] = gx[...]
    gather_end(0, up.at[hm], up)
    loads[4].wait()
    step = 512
    for n in range(D // step):
        cols = slice(n * step, (n + 1) * step)
        term = dot(up[:, :, cols].reshape(TOK, step), proj[cols, :])
        if n == 0:
            ga_scr[...] = term
        else:
            ga_scr[...] += term
    for i in range(HEADS):
        h = lax.rem(first + i, HEADS)
        mine = ga_scr[:, pl.ds(pl.multiple_of(h * HD, HD), HD)].astype(BF16)
        sga[pl.ds(h * QUADS, QUADS)] = dot(pack[h], mine).astype(BF16).reshape(QUADS, MSG, HD)
        send_group(GA, sga, rga, h, i)
    gather_forward(1, gx, gall)

    spread = hot(iota((128, GROUP), 0) == iota((128, GROUP), 1) % MSG)
    src_row = iota((QUADS, GROUP), 0) == iota((QUADS, GROUP), 1) // MSG
    pick = hot(iota((GROUP, QUADS), 0) // MSG == iota((GROUP, QUADS), 1))
    own_lane = iota((GROUP, 128), 1) == iota((GROUP, 128), 0) % MSG
    sub = iota((QUADS, 128), 0)
    for i in range(HEADS):
        c = lax.rem(first + HEADS - i, HEADS)
        wait_group(ID, sid, rid, c, i)
        ids = jnp.zeros((QUADS, 128), jnp.int32)
        for d in range(QUADS):
            ids = jnp.where(sub == d, rid[c * QUADS + d], ids)
        high = (ids >> 7).astype(F32).astype(BF16)
        low = (ids & 127).astype(F32).astype(BF16)
        wide = dot(high, spread) * CAP + dot(low, spread)
        ids_row = jnp.sum(jnp.where(src_row, wide, 0.0), axis=0, keepdims=True)
        tall = dot(pick, high) * CAP + dot(pick, low)
        ids_col = jnp.sum(jnp.where(own_lane, tall, 0.0), axis=1, keepdims=True)
        put[c] = hot(iota((ROWS, GROUP), 0).astype(F32) == ids_row)
        take[c] = hot(iota((GROUP, ROWS), 1).astype(F32) == ids_col)
        col = dot(put[c], jnp.ones((GROUP, 128), BF16))
        row = dot(jnp.ones((8, GROUP), BF16), take[c])
        if i == 0:
            fill_col[...] = col
        else:
            fill_col[...] += col
        for b in range(BLOCKS):
            piece = row[:, b * CAP : (b + 1) * CAP]
            if i == 0:
                fill_row[b] = piece
            else:
                fill_row[b] += piece
    for h in range(HEADS):
        pack_t[h] = pack[h].T
    for i in range(HEADS):
        c = lax.rem(first + HEADS - i, HEADS)
        wait_group(QKV, sx, rx, c, i)
        term = dot(put[c], rx[pl.ds(c * QUADS, QUADS)].reshape(GROUP, 3 * HD))
        if i == 0:
            acc[...] = term
        elif i < HEADS - 1:
            acc[...] += term
        else:
            placed[...] = (acc[...] + term).astype(BF16)

    scale = HD**-0.5

    def rows_of(b):
        return pl.ds(b * CAP, CAP)

    def pairing(j, b):
        owner = quad + QUADS * j
        partner = rid[owner][:, 64 + b : 65 + b]
        away = (j + 2) % 4
        chosen = [
            jnp.where(partner == (quad + QUADS * away) * 3 + m, 1.0, 0.0) for m in range(3)
        ]
        return away, chosen

    for j in range(HEADS):
        for b in range(3):
            near = rows_of(j * 3 + b)
            away, chosen = pairing(j, b)
            other = jnp.zeros((CAP, 2 * HD), F32)
            other_fill = jnp.zeros((1, CAP), F32)
            for m in range(3):
                other += placed[rows_of(away * 3 + m), HD:].astype(F32) * chosen[m]
                other_fill += fill_row[away * 3 + m][:1] * chosen[m]
            both = jnp.concatenate([placed[near, HD:], other.astype(BF16)], axis=0)
            key_set[j * 3 + b] = both
            live = jnp.concatenate([fill_row[j * 3 + b][:1], other_fill], axis=1)
            filled = fill_col[near, :1]
            scores = dot_general(placed[near, :HD], both[:, :HD], NT) * scale
            scores = jnp.where(live > 0, scores, -1e30)
            top = jnp.max(scores, axis=1, keepdims=True)
            weights = jnp.exp(scores - top) * live
            total = jnp.sum(weights, axis=1, keepdims=True) + (1.0 - filled)
            probs = weights * (filled / total)
            probs_scr[j * 3 + b] = probs
            res[near, :] = dot(probs.astype(BF16), both[:, HD:]).astype(BF16)

    for i in range(HEADS):
        c = lax.rem(first + i, HEADS)
        rows = dot(take[c], res[...]).astype(BF16)
        satt[pl.ds(c * QUADS, QUADS)] = rows.reshape(QUADS, MSG, HD)
        send_group(ATT, satt, ratt, c, i)

    for i in range(HEADS):
        c = lax.rem(first + HEADS - i, HEADS)
        wait_group(GA, sga, rga, c, i)
        term = dot(put[c], rga[pl.ds(c * QUADS, QUADS)].reshape(GROUP, HD))
        if i == 0:
            acc_g[...] = term
        elif i < HEADS - 1:
            acc_g[...] += term
        else:
            placed_g[...] = (acc_g[...] + term).astype(BF16)

    for j in range(HEADS):
        for b in range(3):
            near = rows_of(j * 3 + b)
            both = key_set[j * 3 + b]
            probs = probs_scr[j * 3 + b]
            grad = placed_g[near, :]
            prob_grad = dot_general(grad, both[:, HD:], NT)
            inner = jnp.sum(probs * prob_grad, axis=1, keepdims=True)
            score_grad = (probs * (prob_grad - inner)).astype(BF16)
            res_g[near, :HD] = (dot(score_grad, both[:, :HD]) * scale).astype(BF16)
            key_grad = dot_general(score_grad, placed[near, :HD], TN) * scale
            val_grad = dot_general(probs.astype(BF16), grad, TN)
            own[near, :HD] = key_grad[:CAP]
            own[near, HD:] = val_grad[:CAP]
            far[near, :HD] = key_grad[CAP:].astype(BF16)
            far[near, HD:] = val_grad[CAP:].astype(BF16)

    for j in range(HEADS):
        for b in range(3):
            near = rows_of(j * 3 + b)
            away, chosen = pairing(j, b)
            total = own[near, :]
            for m in range(3):
                total += far[rows_of(away * 3 + m), :].astype(F32) * chosen[m]
            res_g[near, HD:] = total.astype(BF16)

    for i in range(HEADS):
        c = lax.rem(first + i, HEADS)
        rows = dot(take[c], res_g[...]).astype(BF16)
        sback[pl.ds(c * QUADS, QUADS)] = rows.reshape(QUADS, MSG, 3 * HD)
        send_group(BACK, sback, rback, c, i)

    for i in range(HEADS):
        wait_group(ATT, satt, ratt, lax.rem(first + HEADS - i, HEADS), i)
    for h in range(HEADS):
        rows = ratt[h * QUADS : (h + 1) * QUADS].reshape(GROUP, HD)
        home = dot(pack_t[h], rows).astype(BF16)
        attn[:, :, h * HD : (h + 1) * HD] = home.reshape(N_HEAD, ROW, HD)

    def attn_half(n):
        return pl.ds(n * (N_HEAD // 2), N_HEAD // 2)

    def attn_copy(k, n, slot, source):
        _, who = x_peer(k)
        half = attn_half(n)
        block = attn_all.at[half, source]
        mine = attn.at[half] if slot < 2 else block
        return remote(mine, block, a_send.at[k // 2, slot], a_recv.at[k // 2, slot], who)

    right, left = 1, XN - 1
    attn_copy(right, 0, 0, mx).start()
    attn_copy(left, 1, 0, mx).start()
    attn_copy(right, 1, 1, mx).start()
    attn_copy(left, 0, 1, mx).start()
    attn_all[:, mx] = attn[...]
    before_x = lax.rem(mx + XN - 1, XN)
    after_x = lax.rem(mx + 1, XN)
    across_x = lax.rem(mx + 2, XN)
    mixed_rows = attn[...].reshape(TOK, HEADS * HD)
    for n in range(D // step):
        cols = slice(n * step, (n + 1) * step)
        term = dot_general(mixed_rows, proj[cols, :], NT)
        part[:, :, cols] = term.astype(BF16).reshape(N_HEAD, ROW, step)
    for k in range(1, N_HEAD):
        h, who = h_peer(k)
        remote(part.at[h], mixed_in.at[hm], m_send.at[h], m_recv.at[hm], who).start()
    mixed_in[hm] = part[hm]
    attn_copy(right, 0, 0, before_x).wait_recv()
    attn_copy(right, 0, 2, before_x).start()
    attn_copy(left, 1, 0, after_x).wait_recv()
    attn_copy(left, 1, 2, after_x).start()
    gather_end(1, gx, gall)
    attn_copy(right, 1, 1, before_x).wait_recv()
    attn_copy(left, 0, 1, after_x).wait_recv()
    attn_copy(right, 0, 2, across_x).wait_recv()
    attn_copy(left, 1, 2, across_x).wait_recv()
    for n in range(XN):
        group = attn_all[2 * n : 2 * n + 2].reshape(TOK, HEADS * HD)
        attn_t[:, n * TOK : (n + 1) * TOK] = group.T

    tall_half = HEADS * HD // 2

    def at_z(offset):
        return lax.rem(mz + ZN + offset, ZN)

    def partial_of(offset):
        grads = gall[:, :, pl.ds(at_z(offset), 1)].reshape(XN * TOK, 128)
        return dot(attn_t[...], grads)

    hops = {0: -2, 1: -1, 2: 1, 3: -2, 4: -1, 5: 2, 6: 1}

    def tree_copy(d, slot):
        sign = 1 if d == 0 else -1
        who = {"seq": at_z(sign * hops[slot]) * XN + mx}
        return remote(
            gp_part.at[d, slot], gp_in.at[d, slot], p_send.at[d, slot], p_recv.at[d, slot], who
        )

    def tree_sends(offset, slots):
        chunk = partial_of(offset).astype(BF16)
        for d in range(2):
            gp_part[d, slots[d]] = chunk[d * tall_half : (d + 1) * tall_half]
            tree_copy(d, slots[d]).start()

    for offset, slots in ((4, (0, 0)), (-3, (1, 2)), (3, (2, 1)), (-1, (4, 6)), (1, (6, 4))):
        tree_sends(offset, slots)
    behind, ahead, mine = partial_of(-2), partial_of(2), partial_of(0)
    for d, slot, chunk in ((0, 5, ahead), (1, 5, behind), (0, 3, behind), (1, 3, ahead)):
        total = chunk[d * tall_half : (d + 1) * tall_half]
        for n in (0, 1) if slot == 3 else (2,):
            tree_copy(d, n).wait_recv()
            total += gp_in[d, n].astype(F32)
        gp_part[d, slot] = total.astype(BF16)
        tree_copy(d, slot).start()

    for k in range(1, N_HEAD):
        h, who = h_peer(k)
        remote(part.at[h], mixed_in.at[h], m_send.at[h], m_recv.at[h], who).wait()
    total = mixed_in[0].astype(F32)
    for h in range(1, N_HEAD):
        total += mixed_in[h].astype(F32)
    mixed_ref[...] = total.astype(BF16)

    for i in range(HEADS):
        wait_group(BACK, sback, rback, lax.rem(first + HEADS - i, HEADS), i)
    for h in range(HEADS):
        rows = rback[h * QUADS : (h + 1) * QUADS].reshape(GROUP, 3 * HD)
        home = dot(pack_t[h], rows)
        for n in range(3):
            xf[n, pl.ds(h, TOK, stride=HEADS), :] = home[:, n * HD : (n + 1) * HD]
    for n, ref in enumerate((dq_ref, dk_ref, dv_ref)):
        ref[...] = xf[n].astype(BF16)

    for d in range(2):
        total = mine[d * tall_half : (d + 1) * tall_half]
        for slot in (3, 4, 5, 6):
            tree_copy(d, slot).wait_recv()
            total += gp_in[d, slot].astype(F32)
        gp_ref[:, d * tall_half : (d + 1) * tall_half] = total.T.astype(BF16)

    for kind, src, out in (
        (ID, sid, rid), (QKV, sx, rx), (GA, sga, rga), (ATT, satt, ratt), (BACK, sback, rback)
    ):
        arrivals(kind, src, out, 0, SEQ - 1, first).wait_send()

    attn_copy(right, 0, 0, mx).wait_send()
    attn_copy(right, 1, 1, mx).wait_send()
    attn_copy(right, 0, 2, before_x).wait_send()
    attn_copy(left, 1, 0, mx).wait_send()
    attn_copy(left, 0, 1, mx).wait_send()
    attn_copy(left, 1, 2, after_x).wait_send()
    for d in range(2):
        for slot in range(7):
            tree_copy(d, slot).wait_send()


def layer(*args):
    vmem = pl.BlockSpec(memory_space=pltpu.VMEM)
    dma = pltpu.SemaphoreType.DMA
    wide = HEADS * HD
    flat = jax.ShapeDtypeStruct((TOK * HEADS, HD), BF16)

    def half(*shape):
        return pltpu.VMEM(shape, BF16)

    def full(*shape):
        return pltpu.VMEM(shape, F32)

    return pl.pallas_call(
        layer_kernel,
        out_shape=(
            jax.ShapeDtypeStruct((ROW, D), BF16), flat, flat, flat,
            jax.ShapeDtypeStruct((128, wide), BF16),
        ),
        in_specs=[vmem] * 2 + [pl.BlockSpec(memory_space=pl.ANY)] * 5,
        out_specs=(vmem,) * 5,
        scratch_shapes=[
            half(D, wide), half(3, TOK * HEADS, HD), full(3, TOK * HEADS, HD), half(HEADS, TOK, 3 * HD),
            half(HEADS, GROUP, TOK), half(HEADS, TOK, GROUP),
            half(SEQ, MSG, 3 * HD), pltpu.VMEM((SEQ, 1, 128), jnp.int32),
            half(SEQ, MSG, HD), half(SEQ, MSG, HD), half(SEQ, MSG, 3 * HD),
            half(SEQ, MSG, 3 * HD), pltpu.VMEM((SEQ, 1, 128), jnp.int32),
            half(SEQ, MSG, HD), half(SEQ, MSG, HD), half(SEQ, MSG, 3 * HD),
            full(TOK, wide), half(N_HEAD, ROW, D),
            half(XN, ZN, ROW, 128), half(XN, ZN, ROW, 128), half(N_HEAD, XN, ZN, ROW, 128),
            half(HEADS, ROWS, GROUP), half(HEADS, GROUP, ROWS),
            full(ROWS, 3 * HD), full(ROWS, HD), full(ROWS, 128), full(BLOCKS, 8, CAP),
            half(ROWS, 3 * HD), half(ROWS, HD), half(BLOCKS, 2 * CAP, 2 * HD),
            full(BLOCKS, CAP, 2 * CAP), full(ROWS, 2 * HD), half(ROWS, 2 * HD),
            half(ROWS, HD), half(ROWS, 3 * HD),
            half(N_HEAD, ROW, wide), half(N_HEAD, XN, ROW, wide), half(wide, XN * TOK),
            half(N_HEAD, ROW, D), half(N_HEAD, ROW, D),
            half(2, 7, wide // 2, 128), half(2, 7, wide // 2, 128),
            dma((5,)), dma((5,)), dma((5, HEADS)), dma((2, 4)), dma((2, 4)), dma((2, 4)), dma((2, 4)),
            dma((XN,)), dma((XN,)), dma((2, 3)), dma((2, 3)),
            dma((N_HEAD,)), dma((N_HEAD,)), dma((2, 7)), dma((2, 7)),
        ],
        compiler_params=pltpu.CompilerParams(
            collective_id=0, has_side_effects=True, vmem_limit_bytes=VMEM_LIMIT
        ),
        name="layer",
    )(*args)


def deliver_kernel(*refs):
    count = len(refs) // 2
    for n in range(count):
        refs[count + n][...] = refs[n][...]


def deliver(*arrays):
    vmem = pl.BlockSpec(memory_space=pltpu.VMEM)
    return pl.pallas_call(
        deliver_kernel,
        out_shape=tuple(jax.ShapeDtypeStruct(a.shape, a.dtype) for a in arrays),
        in_specs=[vmem] * len(arrays),
        out_specs=(vmem,) * len(arrays),
        compiler_params=pltpu.CompilerParams(vmem_limit_bytes=VMEM_LIMIT),
        name="deliver",
    )(*arrays)


def shards(queries, keys_in, values, out_proj, out_grad, slot_index, partner_block):
    flat = (TOK * HEADS, HD)
    mixed, dq, dk, dv, gp = deliver(
        *layer(
            slot_index, partner_block,
            queries.reshape(flat), keys_in.reshape(flat), values.reshape(flat),
            out_grad, out_proj,
        )
    )
    shape = (TOK, HEADS, HD)
    return mixed, dq.reshape(shape), dk.reshape(shape), dv.reshape(shape), gp


def solution(mesh):
    placed = (
        P("seq", "head", None),
        P("seq", "head", None),
        P("seq", "head", None),
        P(None, "head"),
        P(("seq", "head"), None),
        P("head", "seq"),
        P("head", "seq"),
    )
    return jax.shard_map(
        shards,
        mesh=mesh,
        in_specs=placed,
        out_specs=(
            P(("seq", "head"), None),
            P("seq", "head", None),
            P("seq", "head", None),
            P("seq", "head", None),
            P("seq", "head"),
        ),
        check_vma=False,
    )
```

```python
import functools

import jax
import jax.numpy as jnp
from jax import lax
from jax.experimental import pallas as pl
from jax.experimental.pallas import tpu as pltpu
from jax.sharding import PartitionSpec as P

MESH = pl.DeviceIdType.MESH
CAP = 128
HD = 128
HEADS = 4
TOK = 256
SEQ = 32
N_HEAD = 8
OWNED = 384
PER = 12
MSG = HEADS * PER
QUADS = 8
ROWS = SEQ * MSG
BLOCKS = ROWS // CAP
D = 4096
XN = 4
ZN = 8
VMEM_LIMIT = 56 * 1024 * 1024
F32 = jnp.float32
BF16 = jnp.bfloat16


def iota(shape, dim):
    return lax.broadcasted_iota(jnp.int32, shape, dim)


def greet(peers):
    barrier = pltpu.get_barrier_semaphore()
    for peer in peers:
        pl.semaphore_signal(barrier, inc=1, device_id=peer, device_id_type=MESH)


def greeted(count):
    pl.semaphore_wait(pltpu.get_barrier_semaphore(), count)


def remote(src, dst, send_sem, recv_sem, peer):
    return pltpu.make_async_remote_copy(
        src_ref=src,
        dst_ref=dst,
        send_sem=send_sem,
        recv_sem=recv_sem,
        device_id=peer,
        device_id_type=MESH,
    )

NT = (((1,), (1,)), ((), ()))
TN = (((0,), (0,)), ((), ()))
ID, QKV, GA, ATT, BACK = range(5)
ROW = TOK // N_HEAD
GROUP = QUADS * MSG


def dot(a, b):
    return jnp.dot(a, b, preferred_element_type=F32)


def dot_general(a, b, dims):
    return lax.dot_general(a, b, dims, preferred_element_type=F32)


def hot(condition):
    return jnp.where(condition, 1.0, 0.0).astype(BF16)


def layer_kernel(
    slot_ref, partner_ref, q_hbm, k_hbm, v_hbm, grad_hbm, proj_hbm,
    mixed_hbm, dq_hbm, dk_hbm, dv_hbm, gp_hbm,
    mixed_ref, gp_ref, out_sem, proj, raw, xf, x, pack, pack_t, sx, sid, sga, satt, sback, rx, rid, rga, ratt, rback,
    ga_scr, up, gs, gx, gall, put, take, acc, acc_g, fill_col, fill_row,
    placed, placed_g, key_set, probs_scr, own, far, res, res_g,
    attn, attn_all, attn_t, part, mixed_in, gp_part, gp_in,
    in_sem, t_send, t_recv, up_send, up_recv, core_send, core_recv,
    gx_send, gx_recv, a_send, a_recv, m_send, m_recv, p_send, p_recv,
):
    me = lax.axis_index("seq")
    hm = lax.axis_index("head")
    mx = lax.rem(me, XN)
    mz = me // XN
    first = me // QUADS
    quad = lax.rem(me, QUADS)
    core = lax.rem(hm, 2)
    my = hm // 2
    sibling = {"head": my * 2 + 1 - core}
    loads = [
        pltpu.make_async_copy(source, target, in_sem.at[n])
        for n, (source, target) in enumerate(
            (
                (q_hbm, raw.at[0]), (k_hbm, raw.at[1]), (v_hbm, raw.at[2]),
                (grad_hbm, up.at[hm]), (proj_hbm, proj),
            )
        )
    ]
    for load in loads:
        load.start()

    def x_peer(k):
        to = lax.rem(mx + k, XN)
        return to, {"seq": mz * XN + to}

    def y_peer(k):
        to = lax.rem(my + k, 4)
        return to, {"head": to * 2 + core}

    def h_peer(k):
        to = lax.rem(hm + k, N_HEAD)
        return to, {"head": to}

    greet(
        [{"seq": lax.rem(me + k, SEQ)} for k in range(1, SEQ)]
        + [h_peer(k)[1] for k in range(1, N_HEAD)]
    )

    def gather_start(kind, src, out):
        for k in (1, 3, 2):
            _, who = y_peer(k)
            remote(src, out.at[hm], up_send.at[kind, k], up_recv.at[kind, my], who).start()
        remote(src, out.at[hm], core_send.at[kind, 0], core_recv.at[kind, my], sibling).start()

    def gather_forward(kind, src, out):
        for k in (1, 3, 2):
            y, who = y_peer(k)
            block = out.at[y * 2 + core]
            remote(src, block, up_send.at[kind, k], up_recv.at[kind, y], who).wait_recv()
            remote(block, block, core_send.at[kind, k], core_recv.at[kind, y], sibling).start()

    def gather_end(kind, src, out):
        for k in range(4):
            y, who = y_peer(k)
            block = out.at[y * 2 + 1 - core]
            remote(src, block, core_send.at[kind, k], core_recv.at[kind, y], sibling).wait()
            if k:
                remote(src, block, up_send.at[kind, k], up_recv.at[kind, y], who).wait_send()

    def send(kind, src, out, to):
        remote(
            src.at[to], out.at[me], t_send.at[kind], t_recv.at[kind, first], {"seq": to}
        ).start()

    def arrivals(kind, src, out, begin, count, group):
        part = pl.ds(begin, count)
        who = {"seq": lax.rem(me + 1, SEQ)}
        return remote(src.at[part], out.at[part], t_send.at[kind], t_recv.at[kind, group], who)

    def members(group, i):
        for k in range(QUADS):
            yield group * QUADS + lax.rem(quad + k, QUADS), i == 0 and k == 0

    def send_group(kind, src, out, group, i):
        for to, mine in members(group, i):
            if mine:
                out[me] = src[me]
            else:
                send(kind, src, out, to)

    def wait_group(kind, src, out, group, i):
        count = QUADS - 1 if i == 0 else QUADS
        arrivals(kind, src, out, group * QUADS, count, group).wait_recv()

    for n in range(3):
        loads[n].wait()
        xf[n] = raw[n].astype(F32)
    for h in range(HEADS):
        for n in range(3):
            x[h, :, n * HD : (n + 1) * HD] = xf[n, pl.ds(h, TOK, stride=HEADS), :].astype(BF16)

    owner_col = iota((SEQ, TOK), 0)
    before_mask = hot(iota((TOK, TOK), 0) < iota((TOK, TOK), 1))
    lane = iota((QUADS, 128), 1)
    lane_row = iota((1, 128), 1)
    quad_col = iota((QUADS, TOK), 0).astype(F32)
    row_col = iota((128, TOK), 0).astype(F32)
    base = ((owner_col % QUADS) * MSG + (owner_col // QUADS) * PER).astype(F32)
    for i in range(HEADS):
        h = lax.rem(first + i, HEADS)
        slots = slot_ref[pl.ds(h, 1), :]
        member = (slots >= owner_col * OWNED) & (slots < (owner_col + 1) * OWNED)
        one = jnp.where(member, 1.0, 0.0)
        before = dot(one.astype(BF16), before_mask)
        rank = jnp.sum(one * before, axis=0, keepdims=True)
        owner = jnp.sum(jnp.where(member, owner_col.astype(F32), 0.0), axis=0, keepdims=True)
        spot = jnp.sum(jnp.where(member, base, 0.0), axis=0, keepdims=True) + rank
        within = slots.astype(F32) - owner * OWNED
        block = jnp.where(within >= CAP, 1.0, 0.0) + jnp.where(within >= 2 * CAP, 1.0, 0.0)
        place = within - block * CAP
        row_part = jnp.floor(owner / QUADS)
        row = row_part * PER + rank
        here = quad_col == owner - row_part * QUADS
        at_row = hot(row_col == row)
        high = dot_general(jnp.where(here, block + 1.0, 0.0).astype(BF16), at_row, NT)
        low = dot_general(jnp.where(here, place, 0.0).astype(BF16), at_row, NT)
        ids = (lane // PER) * OWNED + ((high - 1.0) * CAP + low).astype(jnp.int32)
        ids = jnp.where(high > 0.5, ids, -1)
        pairs = partner_ref[pl.ds(h, 1), :]
        for b in range(3):
            ids = jnp.where(lane == 64 + b, pairs[:, b : b + 1], ids)
        for d in range(QUADS):
            sid[h * QUADS + d] = ids[d : d + 1]
        packing = hot(iota((GROUP, TOK), 0).astype(F32) == spot)
        pack[h] = packing
        sx[pl.ds(h * QUADS, QUADS)] = dot(packing, x[h]).astype(BF16).reshape(QUADS, MSG, 3 * HD)
        if i == 0:
            greeted(SEQ + N_HEAD - 2)
        send_group(QKV, sx, rx, h, i)
        send_group(ID, sid, rid, h, i)
        if i == 0:
            loads[3].wait()
            gather_start(0, up.at[hm], up)

    for xx in range(XN):
        for zz in range(ZN):
            chunk = zz * XN + xx
            gs[xx, zz] = up[hm, :, chunk * 128 : (chunk + 1) * 128]
    for k in range(1, XN):
        to, who = x_peer(k)
        remote(gs.at[to], gx.at[mx], gx_send.at[k], gx_recv.at[mx], who).start()
    gx[mx] = gs[mx]
    gather_forward(0, up.at[hm], up)
    for k in range(1, XN):
        xx, who = x_peer(k)
        remote(gs.at[xx], gx.at[xx], gx_send.at[k], gx_recv.at[xx], who).wait()
    gather_start(1, gx, gall)
    gall[hm] = gx[...]
    gather_end(0, up.at[hm], up)
    loads[4].wait()
    step = 512
    for n in range(D // step):
        cols = slice(n * step, (n + 1) * step)
        term = dot(up[:, :, cols].reshape(TOK, step), proj[cols, :])
        if n == 0:
            ga_scr[...] = term
        else:
            ga_scr[...] += term
    for i in range(HEADS):
        h = lax.rem(first + i, HEADS)
        mine = ga_scr[:, pl.ds(pl.multiple_of(h * HD, HD), HD)].astype(BF16)
        sga[pl.ds(h * QUADS, QUADS)] = dot(pack[h], mine).astype(BF16).reshape(QUADS, MSG, HD)
        send_group(GA, sga, rga, h, i)
    gather_forward(1, gx, gall)

    spread = hot(iota((128, GROUP), 0) == iota((128, GROUP), 1) % MSG)
    src_row = iota((QUADS, GROUP), 0) == iota((QUADS, GROUP), 1) // MSG
    pick = hot(iota((GROUP, QUADS), 0) // MSG == iota((GROUP, QUADS), 1))
    own_lane = iota((GROUP, 128), 1) == iota((GROUP, 128), 0) % MSG
    sub = iota((QUADS, 128), 0)
    for i in range(HEADS):
        c = lax.rem(first + HEADS - i, HEADS)
        wait_group(ID, sid, rid, c, i)
        ids = jnp.zeros((QUADS, 128), jnp.int32)
        for d in range(QUADS):
            ids = jnp.where(sub == d, rid[c * QUADS + d], ids)
        high = (ids >> 7).astype(F32).astype(BF16)
        low = (ids & 127).astype(F32).astype(BF16)
        wide = dot(high, spread) * CAP + dot(low, spread)
        ids_row = jnp.sum(jnp.where(src_row, wide, 0.0), axis=0, keepdims=True)
        tall = dot(pick, high) * CAP + dot(pick, low)
        ids_col = jnp.sum(jnp.where(own_lane, tall, 0.0), axis=1, keepdims=True)
        put[c] = hot(iota((ROWS, GROUP), 0).astype(F32) == ids_row)
        take[c] = hot(iota((GROUP, ROWS), 1).astype(F32) == ids_col)
        col = dot(put[c], jnp.ones((GROUP, 128), BF16))
        row = dot(jnp.ones((8, GROUP), BF16), take[c])
        if i == 0:
            fill_col[...] = col
        else:
            fill_col[...] += col
        for b in range(BLOCKS):
            piece = row[:, b * CAP : (b + 1) * CAP]
            if i == 0:
                fill_row[b] = piece
            else:
                fill_row[b] += piece
    for h in range(HEADS):
        pack_t[h] = pack[h].T
    for i in range(HEADS):
        c = lax.rem(first + HEADS - i, HEADS)
        wait_group(QKV, sx, rx, c, i)
        term = dot(put[c], rx[pl.ds(c * QUADS, QUADS)].reshape(GROUP, 3 * HD))
        if i == 0:
            acc[...] = term
        elif i < HEADS - 1:
            acc[...] += term
        else:
            placed[...] = (acc[...] + term).astype(BF16)

    scale = HD**-0.5

    def rows_of(b):
        return pl.ds(b * CAP, CAP)

    def pairing(j, b):
        owner = quad + QUADS * j
        partner = rid[owner][:, 64 + b : 65 + b]
        away = (j + 2) % 4
        chosen = [
            jnp.where(partner == (quad + QUADS * away) * 3 + m, 1.0, 0.0) for m in range(3)
        ]
        return away, chosen

    for j in range(HEADS):
        for b in range(3):
            near = rows_of(j * 3 + b)
            away, chosen = pairing(j, b)
            other = jnp.zeros((CAP, 2 * HD), BF16)
            other_fill = jnp.zeros((1, CAP), F32)
            for m in range(3):
                mask = jnp.broadcast_to(chosen[m], (CAP, 2 * HD)).astype(BF16)
                other += placed[rows_of(away * 3 + m), HD:] * mask
                other_fill += fill_row[away * 3 + m][:1] * chosen[m]
            both = jnp.concatenate([placed[near, HD:], other], axis=0)
            key_set[j * 3 + b] = both
            live = jnp.concatenate([fill_row[j * 3 + b][:1], other_fill], axis=1)
            filled = fill_col[near, :1]
            scores = dot_general(placed[near, :HD], both[:, :HD], NT) * scale
            scores = jnp.where(live > 0, scores, -1e30)
            top = jnp.max(scores, axis=1, keepdims=True)
            weights = jnp.exp(scores - top) * live
            total = jnp.sum(weights, axis=1, keepdims=True) + (1.0 - filled)
            probs = weights * (filled / total)
            probs_scr[j * 3 + b] = probs
            res[near, :] = dot(probs.astype(BF16), both[:, HD:]).astype(BF16)

    for i in range(HEADS):
        c = lax.rem(first + i, HEADS)
        rows = dot(take[c], res[...]).astype(BF16)
        satt[pl.ds(c * QUADS, QUADS)] = rows.reshape(QUADS, MSG, HD)
        send_group(ATT, satt, ratt, c, i)

    for i in range(HEADS):
        c = lax.rem(first + HEADS - i, HEADS)
        wait_group(GA, sga, rga, c, i)
        term = dot(put[c], rga[pl.ds(c * QUADS, QUADS)].reshape(GROUP, HD))
        if i == 0:
            acc_g[...] = term
        elif i < HEADS - 1:
            acc_g[...] += term
        else:
            placed_g[...] = (acc_g[...] + term).astype(BF16)

    for j in range(HEADS):
        for b in range(3):
            near = rows_of(j * 3 + b)
            both = key_set[j * 3 + b]
            probs = probs_scr[j * 3 + b]
            grad = placed_g[near, :]
            prob_grad = dot_general(grad, both[:, HD:], NT)
            inner = jnp.sum(probs * prob_grad, axis=1, keepdims=True)
            score_grad = (probs * (prob_grad - inner)).astype(BF16)
            res_g[near, :HD] = (dot(score_grad, both[:, :HD]) * scale).astype(BF16)
            key_grad = dot_general(score_grad, placed[near, :HD], TN) * scale
            val_grad = dot_general(probs.astype(BF16), grad, TN)
            own[near, :HD] = key_grad[:CAP]
            own[near, HD:] = val_grad[:CAP]
            far[near, :HD] = key_grad[CAP:].astype(BF16)
            far[near, HD:] = val_grad[CAP:].astype(BF16)

    for j in range(HEADS):
        for b in range(3):
            near = rows_of(j * 3 + b)
            away, chosen = pairing(j, b)
            total = own[near, :]
            for m in range(3):
                total += far[rows_of(away * 3 + m), :].astype(F32) * chosen[m]
            res_g[near, HD:] = total.astype(BF16)

    for i in range(HEADS):
        c = lax.rem(first + i, HEADS)
        rows = dot(take[c], res_g[...]).astype(BF16)
        sback[pl.ds(c * QUADS, QUADS)] = rows.reshape(QUADS, MSG, 3 * HD)
        send_group(BACK, sback, rback, c, i)

    for i in range(HEADS):
        wait_group(ATT, satt, ratt, lax.rem(first + HEADS - i, HEADS), i)
    for h in range(HEADS):
        rows = ratt[h * QUADS : (h + 1) * QUADS].reshape(GROUP, HD)
        home = dot(pack_t[h], rows).astype(BF16)
        attn[:, :, h * HD : (h + 1) * HD] = home.reshape(N_HEAD, ROW, HD)

    def attn_half(n):
        return pl.ds(n * (N_HEAD // 2), N_HEAD // 2)

    side = HEADS * HD // 2

    def attn_copy(f, k, n, slot, source):
        _, who = x_peer(k)
        half = attn_half(n)
        cols = pl.ds(f * side, side)
        block = attn_all.at[half, source, :, cols]
        mine = attn.at[half, :, cols] if slot < 2 else block
        return remote(mine, block, a_send.at[f, k // 2, slot], a_recv.at[f, k // 2, slot], who)

    right, left = 1, XN - 1
    for f in range(2):
        attn_copy(f, right, 0, 0, mx).start()
        attn_copy(f, left, 1, 0, mx).start()
        attn_copy(f, right, 1, 1, mx).start()
        attn_copy(f, left, 0, 1, mx).start()
    attn_all[:, mx] = attn[...]
    before_x = lax.rem(mx + XN - 1, XN)
    after_x = lax.rem(mx + 1, XN)
    across_x = lax.rem(mx + 2, XN)
    mixed_rows = attn[...].reshape(TOK, HEADS * HD)
    for n in range(D // step):
        cols = slice(n * step, (n + 1) * step)
        term = dot_general(mixed_rows, proj[cols, :], NT)
        part[:, :, cols] = term.astype(BF16).reshape(N_HEAD, ROW, step)
    for f in range(2):
        attn_copy(f, right, 0, 0, before_x).wait_recv()
        attn_copy(f, right, 0, 2, before_x).start()
        attn_copy(f, left, 1, 0, after_x).wait_recv()
        attn_copy(f, left, 1, 2, after_x).start()
    for k in range(1, N_HEAD):
        h, who = h_peer(k)
        remote(part.at[h], mixed_in.at[hm], m_send.at[h], m_recv.at[hm], who).start()
    mixed_in[hm] = part[hm]
    gather_end(1, gx, gall)

    def at_z(offset):
        return lax.rem(mz + ZN + offset, ZN)

    def partial_of(offset, d):
        grads = gall[:, :, pl.ds(at_z(offset), 1)].reshape(XN * TOK, 128)
        return dot(attn_t[d * side : (d + 1) * side, :], grads)

    hops = {0: -2, 1: -1, 2: 1, 3: -2, 4: -1, 5: 2, 6: 1}

    def tree_copy(d, slot):
        sign = 1 if d == 0 else -1
        who = {"seq": at_z(sign * hops[slot]) * XN + mx}
        return remote(
            gp_part.at[d, slot], gp_in.at[d, slot], p_send.at[d, slot], p_recv.at[d, slot], who
        )

    def tree_send(d, slot, total):
        gp_part[d, slot] = total.astype(BF16)
        tree_copy(d, slot).start()

    for d in range(2):
        sign = 1 if d == 0 else -1
        attn_copy(d, right, 1, 1, before_x).wait_recv()
        attn_copy(d, left, 0, 1, after_x).wait_recv()
        attn_copy(d, right, 0, 2, across_x).wait_recv()
        attn_copy(d, left, 1, 2, across_x).wait_recv()
        cols = slice(d * side, (d + 1) * side)
        for n in range(XN):
            group = attn_all[2 * n : 2 * n + 2, :, :, cols].reshape(TOK, side)
            attn_t[cols, n * TOK : (n + 1) * TOK] = group.T
        for slot, offset in ((0, 4), (1, -3 * sign), (2, 3 * sign)):
            tree_send(d, slot, partial_of(offset, d))
    late = [(d, 1 if d == 0 else -1) for d in range(2)]
    behind = [partial_of(-2 * sign, d) for d, sign in late]
    ahead = [partial_of(2 * sign, d) for d, sign in late]
    mine = [partial_of(0, d) for d, _ in late]
    for d, sign in late:
        tree_copy(d, 2).wait_recv()
        tree_send(d, 5, ahead[d] + gp_in[d, 2].astype(F32))
        tree_copy(d, 0).wait_recv()
        tree_copy(d, 1).wait_recv()
        tree_send(d, 3, behind[d] + gp_in[d, 0].astype(F32) + gp_in[d, 1].astype(F32))
    for d, sign in late:
        tree_send(d, 4, partial_of(-sign, d))
        tree_send(d, 6, partial_of(sign, d))

    for k in range(1, N_HEAD):
        h, who = h_peer(k)
        remote(part.at[h], mixed_in.at[h], m_send.at[h], m_recv.at[h], who).wait()
    total = mixed_in[0].astype(F32)
    for h in range(1, N_HEAD):
        total += mixed_in[h].astype(F32)
    mixed_ref[...] = total.astype(BF16)
    stores = [pltpu.make_async_copy(mixed_ref, mixed_hbm, out_sem.at[0])]
    stores[0].start()

    for i in range(HEADS):
        wait_group(BACK, sback, rback, lax.rem(first + HEADS - i, HEADS), i)
    for h in range(HEADS):
        rows = rback[h * QUADS : (h + 1) * QUADS].reshape(GROUP, 3 * HD)
        home = dot(pack_t[h], rows)
        for n in range(3):
            xf[n, pl.ds(h, TOK, stride=HEADS), :] = home[:, n * HD : (n + 1) * HD]
    for n, out in enumerate((dq_hbm, dk_hbm, dv_hbm)):
        raw[n] = xf[n].astype(BF16)
        stores.append(pltpu.make_async_copy(raw.at[n], out, out_sem.at[n + 1]))
        stores[-1].start()

    for d in range(2):
        total = mine[d]
        for slot in (3, 4, 5, 6):
            tree_copy(d, slot).wait_recv()
            total += gp_in[d, slot].astype(F32)
        gp_ref[:, d * side : (d + 1) * side] = total.T.astype(BF16)
    stores.append(pltpu.make_async_copy(gp_ref, gp_hbm, out_sem.at[4]))
    stores[-1].start()

    for kind, src, out in (
        (ID, sid, rid), (QKV, sx, rx), (GA, sga, rga), (ATT, satt, ratt), (BACK, sback, rback)
    ):
        arrivals(kind, src, out, 0, SEQ - 1, first).wait_send()

    for f in range(2):
        attn_copy(f, right, 0, 0, mx).wait_send()
        attn_copy(f, right, 1, 1, mx).wait_send()
        attn_copy(f, right, 0, 2, before_x).wait_send()
        attn_copy(f, left, 1, 0, mx).wait_send()
        attn_copy(f, left, 0, 1, mx).wait_send()
        attn_copy(f, left, 1, 2, after_x).wait_send()
    for d in range(2):
        for slot in range(7):
            tree_copy(d, slot).wait_send()
    for store in stores:
        store.wait()


def layer(*args):
    vmem = pl.BlockSpec(memory_space=pltpu.VMEM)
    dma = pltpu.SemaphoreType.DMA
    wide = HEADS * HD
    flat = jax.ShapeDtypeStruct((TOK * HEADS, HD), BF16)

    def half(*shape):
        return pltpu.VMEM(shape, BF16)

    def full(*shape):
        return pltpu.VMEM(shape, F32)

    return pl.pallas_call(
        layer_kernel,
        out_shape=(
            jax.ShapeDtypeStruct((ROW, D), BF16), flat, flat, flat,
            jax.ShapeDtypeStruct((128, wide), BF16),
        ),
        in_specs=[vmem] * 2 + [pl.BlockSpec(memory_space=pl.ANY)] * 5,
        out_specs=(pl.BlockSpec(memory_space=pl.ANY),) * 5,
        scratch_shapes=[
            half(ROW, D), half(128, wide), dma((5,)),
            half(D, wide), half(3, TOK * HEADS, HD), full(3, TOK * HEADS, HD), half(HEADS, TOK, 3 * HD),
            half(HEADS, GROUP, TOK), half(HEADS, TOK, GROUP),
            half(SEQ, MSG, 3 * HD), pltpu.VMEM((SEQ, 1, 128), jnp.int32),
            half(SEQ, MSG, HD), half(SEQ, MSG, HD), half(SEQ, MSG, 3 * HD),
            half(SEQ, MSG, 3 * HD), pltpu.VMEM((SEQ, 1, 128), jnp.int32),
            half(SEQ, MSG, HD), half(SEQ, MSG, HD), half(SEQ, MSG, 3 * HD),
            full(TOK, wide), half(N_HEAD, ROW, D),
            half(XN, ZN, ROW, 128), half(XN, ZN, ROW, 128), half(N_HEAD, XN, ZN, ROW, 128),
            half(HEADS, ROWS, GROUP), half(HEADS, GROUP, ROWS),
            full(ROWS, 3 * HD), full(ROWS, HD), full(ROWS, 128), full(BLOCKS, 8, CAP),
            half(ROWS, 3 * HD), half(ROWS, HD), half(BLOCKS, 2 * CAP, 2 * HD),
            full(BLOCKS, CAP, 2 * CAP), full(ROWS, 2 * HD), half(ROWS, 2 * HD),
            half(ROWS, HD), half(ROWS, 3 * HD),
            half(N_HEAD, ROW, wide), half(N_HEAD, XN, ROW, wide), half(wide, XN * TOK),
            half(N_HEAD, ROW, D), half(N_HEAD, ROW, D),
            half(2, 7, wide // 2, 128), half(2, 7, wide // 2, 128),
            dma((5,)), dma((5,)), dma((5, HEADS)), dma((2, 4)), dma((2, 4)), dma((2, 4)), dma((2, 4)),
            dma((XN,)), dma((XN,)), dma((2, 2, 3)), dma((2, 2, 3)),
            dma((N_HEAD,)), dma((N_HEAD,)), dma((2, 7)), dma((2, 7)),
        ],
        compiler_params=pltpu.CompilerParams(
            collective_id=0, has_side_effects=True, vmem_limit_bytes=VMEM_LIMIT
        ),
        name="layer",
    )(*args)


def deliver_kernel(*refs):
    count = len(refs) // 2
    for n in range(count):
        refs[count + n][...] = refs[n][...]


def deliver(*arrays):
    vmem = pl.BlockSpec(memory_space=pltpu.VMEM)
    return pl.pallas_call(
        deliver_kernel,
        out_shape=tuple(jax.ShapeDtypeStruct(a.shape, a.dtype) for a in arrays),
        in_specs=[vmem] * len(arrays),
        out_specs=(vmem,) * len(arrays),
        compiler_params=pltpu.CompilerParams(vmem_limit_bytes=VMEM_LIMIT),
        name="deliver",
    )(*arrays)


def shards(queries, keys_in, values, out_proj, out_grad, slot_index, partner_block):
    flat = (TOK * HEADS, HD)
    mixed, dq, dk, dv, gp = deliver(
        *layer(
            slot_index, partner_block,
            queries.reshape(flat), keys_in.reshape(flat), values.reshape(flat),
            out_grad, out_proj,
        )
    )
    shape = (TOK, HEADS, HD)
    return mixed, dq.reshape(shape), dk.reshape(shape), dv.reshape(shape), gp


def solution(mesh):
    placed = (
        P("seq", "head", None),
        P("seq", "head", None),
        P("seq", "head", None),
        P(None, "head"),
        P(("seq", "head"), None),
        P("head", "seq"),
        P("head", "seq"),
    )
    return jax.shard_map(
        shards,
        mesh=mesh,
        in_specs=placed,
        out_specs=(
            P(("seq", "head"), None),
            P("seq", "head", None),
            P("seq", "head", None),
            P("seq", "head", None),
            P("seq", "head"),
        ),
        check_vma=False,
    )
```

```python
import functools

import jax
import jax.numpy as jnp
from jax import lax
from jax.experimental import pallas as pl
from jax.experimental.pallas import tpu as pltpu
from jax.sharding import PartitionSpec as P

MESH = pl.DeviceIdType.MESH
CAP = 128
HD = 128
HEADS = 4
TOK = 256
SEQ = 32
N_HEAD = 8
OWNED = 384
PER = 12
MSG = HEADS * PER
QUADS = 8
ROWS = SEQ * MSG
BLOCKS = ROWS // CAP
D = 4096
XN = 4
ZN = 8
VMEM_LIMIT = 56 * 1024 * 1024
F32 = jnp.float32
BF16 = jnp.bfloat16


def iota(shape, dim):
    return lax.broadcasted_iota(jnp.int32, shape, dim)


def greet(peers):
    barrier = pltpu.get_barrier_semaphore()
    for peer in peers:
        pl.semaphore_signal(barrier, inc=1, device_id=peer, device_id_type=MESH)


def greeted(count):
    pl.semaphore_wait(pltpu.get_barrier_semaphore(), count)


def remote(src, dst, send_sem, recv_sem, peer):
    return pltpu.make_async_remote_copy(
        src_ref=src,
        dst_ref=dst,
        send_sem=send_sem,
        recv_sem=recv_sem,
        device_id=peer,
        device_id_type=MESH,
    )

NT = (((1,), (1,)), ((), ()))
LOG2_E = 1.4426950408889634
TN = (((0,), (0,)), ((), ()))
ID, QK, VAL, GA, ATT, BACK = range(6)
ROW = TOK // N_HEAD
GROUP = QUADS * MSG


def dot(a, b):
    return jnp.dot(a, b, preferred_element_type=F32)


def dot_general(a, b, dims):
    return lax.dot_general(a, b, dims, preferred_element_type=F32)


def hot(condition):
    return jnp.where(condition, 1.0, 0.0).astype(BF16)


def layer_kernel(
    slot_ref, partner_ref, q_hbm, k_hbm, v_hbm, grad_hbm, proj_hbm,
    mixed_hbm, dq_hbm, dk_hbm, dv_hbm, gp_hbm,
    mixed_ref, gp_ref, out_sem, proj, raw, xf, x, pack, pack_t, sqk, sv, sid, sga, satt, sback, rqk, rv, rid, rga, ratt, rback,
    ga_scr, up, gs, gx, gall, put, take, acc, fill_col, fill_row,
    placed, placed_v, placed_g, key_set, val_set, probs_scr, own, far, res, res_g,
    attn, attn_all, attn_t, part, mixed_in, gp_part, gp_in,
    in_sem, t_send, t_recv, up_send, up_recv, core_send, core_recv,
    gx_send, gx_recv, a_send, a_recv, m_send, m_recv, p_send, p_recv,
):
    me = lax.axis_index("seq")
    hm = lax.axis_index("head")
    mx = lax.rem(me, XN)
    mz = me // XN
    first = me // QUADS
    quad = lax.rem(me, QUADS)
    core = lax.rem(hm, 2)
    my = hm // 2
    sibling = {"head": my * 2 + 1 - core}
    loads = [
        pltpu.make_async_copy(source, target, in_sem.at[n])
        for n, (source, target) in enumerate(
            (
                (q_hbm, raw.at[0]), (k_hbm, raw.at[1]), (v_hbm, raw.at[2]),
                (grad_hbm, up.at[hm]), (proj_hbm, proj),
            )
        )
    ]
    for load in loads:
        load.start()

    def x_peer(k):
        to = lax.rem(mx + k, XN)
        return to, {"seq": mz * XN + to}

    def y_peer(k):
        to = lax.rem(my + k, 4)
        return to, {"head": to * 2 + core}

    def h_peer(k):
        to = lax.rem(hm + k, N_HEAD)
        return to, {"head": to}

    greet(
        [{"seq": lax.rem(me + k, SEQ)} for k in range(1, SEQ)]
        + [h_peer(k)[1] for k in range(1, N_HEAD)]
    )

    def gather_start(kind, src, out):
        for k in (1, 3, 2):
            _, who = y_peer(k)
            remote(src, out.at[hm], up_send.at[kind, k], up_recv.at[kind, my], who).start()
        remote(src, out.at[hm], core_send.at[kind, 0], core_recv.at[kind, my], sibling).start()

    def gather_forward(kind, src, out):
        for k in (1, 3, 2):
            y, who = y_peer(k)
            block = out.at[y * 2 + core]
            remote(src, block, up_send.at[kind, k], up_recv.at[kind, y], who).wait_recv()
            remote(block, block, core_send.at[kind, k], core_recv.at[kind, y], sibling).start()

    def gather_end(kind, src, out):
        for k in range(4):
            y, who = y_peer(k)
            block = out.at[y * 2 + 1 - core]
            remote(src, block, core_send.at[kind, k], core_recv.at[kind, y], sibling).wait()
            if k:
                remote(src, block, up_send.at[kind, k], up_recv.at[kind, y], who).wait_send()

    def send(kind, src, out, to):
        remote(
            src.at[to], out.at[me], t_send.at[kind], t_recv.at[kind, first], {"seq": to}
        ).start()

    def arrivals(kind, src, out, begin, count, group):
        part = pl.ds(begin, count)
        who = {"seq": lax.rem(me + 1, SEQ)}
        return remote(src.at[part], out.at[part], t_send.at[kind], t_recv.at[kind, group], who)

    def members(group, i):
        for k in range(QUADS):
            yield group * QUADS + lax.rem(quad + k, QUADS), i == 0 and k == 0

    def send_group(kind, src, out, group, i):
        for to, mine in members(group, i):
            if mine:
                out[me] = src[me]
            else:
                send(kind, src, out, to)

    def wait_group(kind, src, out, group, i):
        count = QUADS - 1 if i == 0 else QUADS
        arrivals(kind, src, out, group * QUADS, count, group).wait_recv()

    for n in range(3):
        loads[n].wait()
        xf[n] = raw[n].astype(F32)
    for h in range(HEADS):
        for n in range(3):
            x[h, :, n * HD : (n + 1) * HD] = xf[n, pl.ds(h, TOK, stride=HEADS), :].astype(BF16)

    owner_col = iota((SEQ, TOK), 0)
    before_mask = hot(iota((TOK, TOK), 0) < iota((TOK, TOK), 1))
    lane = iota((QUADS, 128), 1)
    lane_row = iota((1, 128), 1)
    quad_col = iota((QUADS, TOK), 0).astype(F32)
    row_col = iota((128, TOK), 0).astype(F32)
    base = ((owner_col % QUADS) * MSG + (owner_col // QUADS) * PER).astype(F32)
    for i in range(HEADS):
        h = lax.rem(first + i, HEADS)
        slots = slot_ref[pl.ds(h, 1), :]
        member = (slots >= owner_col * OWNED) & (slots < (owner_col + 1) * OWNED)
        one = jnp.where(member, 1.0, 0.0)
        before = dot(one.astype(BF16), before_mask)
        rank = jnp.sum(one * before, axis=0, keepdims=True)
        owner = jnp.sum(jnp.where(member, owner_col.astype(F32), 0.0), axis=0, keepdims=True)
        spot = jnp.sum(jnp.where(member, base, 0.0), axis=0, keepdims=True) + rank
        within = slots.astype(F32) - owner * OWNED
        block = jnp.where(within >= CAP, 1.0, 0.0) + jnp.where(within >= 2 * CAP, 1.0, 0.0)
        place = within - block * CAP
        row_part = jnp.floor(owner / QUADS)
        row = row_part * PER + rank
        here = quad_col == owner - row_part * QUADS
        at_row = hot(row_col == row)
        high = dot_general(jnp.where(here, block + 1.0, 0.0).astype(BF16), at_row, NT)
        low = dot_general(jnp.where(here, place, 0.0).astype(BF16), at_row, NT)
        ids = (lane // PER) * OWNED + ((high - 1.0) * CAP + low).astype(jnp.int32)
        ids = jnp.where(high > 0.5, ids, -1)
        pairs = partner_ref[pl.ds(h, 1), :]
        for b in range(3):
            ids = jnp.where(lane == 64 + b, pairs[:, b : b + 1], ids)
        for d in range(QUADS):
            sid[h * QUADS + d] = ids[d : d + 1]
        packing = hot(iota((GROUP, TOK), 0).astype(F32) == spot)
        pack[h] = packing
        packed = dot(packing, x[h]).astype(BF16)
        sqk[pl.ds(h * QUADS, QUADS)] = packed[:, : 2 * HD].reshape(QUADS, MSG, 2 * HD)
        sv[pl.ds(h * QUADS, QUADS)] = packed[:, 2 * HD :].reshape(QUADS, MSG, HD)
        if i == 0:
            greeted(SEQ + N_HEAD - 2)
        send_group(QK, sqk, rqk, h, i)
        send_group(ID, sid, rid, h, i)
        if i == 0:
            loads[3].wait()
            gather_start(0, up.at[hm], up)
    for i in range(HEADS):
        send_group(VAL, sv, rv, lax.rem(first + i, HEADS), i)

    for xx in range(XN):
        for zz in range(ZN):
            chunk = zz * XN + xx
            gs[xx, zz] = up[hm, :, chunk * 128 : (chunk + 1) * 128]
    for k in range(1, XN):
        to, who = x_peer(k)
        remote(gs.at[to], gx.at[mx], gx_send.at[k], gx_recv.at[mx], who).start()
    gx[mx] = gs[mx]
    gather_forward(0, up.at[hm], up)
    for k in range(1, XN):
        xx, who = x_peer(k)
        remote(gs.at[xx], gx.at[xx], gx_send.at[k], gx_recv.at[xx], who).wait()
    gather_start(1, gx, gall)
    gall[hm] = gx[...]
    gather_end(0, up.at[hm], up)
    loads[4].wait()
    step = 512
    for n in range(D // step):
        cols = slice(n * step, (n + 1) * step)
        term = dot(up[:, :, cols].reshape(TOK, step), proj[cols, :])
        if n == 0:
            ga_scr[...] = term
        else:
            ga_scr[...] += term
    for i in range(HEADS):
        h = lax.rem(first + i, HEADS)
        mine = ga_scr[:, pl.ds(pl.multiple_of(h * HD, HD), HD)].astype(BF16)
        sga[pl.ds(h * QUADS, QUADS)] = dot(pack[h], mine).astype(BF16).reshape(QUADS, MSG, HD)
        send_group(GA, sga, rga, h, i)
    gather_forward(1, gx, gall)

    spread = hot(iota((128, GROUP), 0) == iota((128, GROUP), 1) % MSG)
    src_row = iota((QUADS, GROUP), 0) == iota((QUADS, GROUP), 1) // MSG
    pick = hot(iota((GROUP, QUADS), 0) // MSG == iota((GROUP, QUADS), 1))
    own_lane = iota((GROUP, 128), 1) == iota((GROUP, 128), 0) % MSG
    sub = iota((QUADS, 128), 0)
    for i in range(HEADS):
        c = lax.rem(first + HEADS - i, HEADS)
        wait_group(ID, sid, rid, c, i)
        ids = jnp.zeros((QUADS, 128), jnp.int32)
        for d in range(QUADS):
            ids = jnp.where(sub == d, rid[c * QUADS + d], ids)
        high = (ids >> 7).astype(F32).astype(BF16)
        low = (ids & 127).astype(F32).astype(BF16)
        wide = dot(high, spread) * CAP + dot(low, spread)
        ids_row = jnp.sum(jnp.where(src_row, wide, 0.0), axis=0, keepdims=True)
        tall = dot(pick, high) * CAP + dot(pick, low)
        ids_col = jnp.sum(jnp.where(own_lane, tall, 0.0), axis=1, keepdims=True)
        put[c] = hot(iota((ROWS, GROUP), 0).astype(F32) == ids_row)
        take[c] = hot(iota((GROUP, ROWS), 1).astype(F32) == ids_col)
        col = dot(put[c], jnp.ones((GROUP, 128), BF16))
        row = dot(jnp.ones((8, GROUP), BF16), take[c])
        if i == 0:
            fill_col[...] = col
        else:
            fill_col[...] += col
        for b in range(BLOCKS):
            piece = row[:, b * CAP : (b + 1) * CAP]
            if i == 0:
                fill_row[b] = piece
            else:
                fill_row[b] += piece
    for h in range(HEADS):
        pack_t[h] = pack[h].T
    for i in range(HEADS):
        c = lax.rem(first + HEADS - i, HEADS)
        wait_group(QK, sqk, rqk, c, i)
        term = dot(put[c], rqk[pl.ds(c * QUADS, QUADS)].reshape(GROUP, 2 * HD))
        if i == 0:
            acc[...] = term
        elif i < HEADS - 1:
            acc[...] += term
        else:
            placed[...] = (acc[...] + term).astype(BF16)

    scale = HD**-0.5

    def rows_of(b):
        return pl.ds(b * CAP, CAP)

    def pairing(j, b):
        owner = quad + QUADS * j
        partner = rid[owner][:, 64 + b : 65 + b]
        away = (j + 2) % 4
        chosen = [
            jnp.where(partner == (quad + QUADS * away) * 3 + m, 1.0, 0.0) for m in range(3)
        ]
        return away, chosen

    def key_side(source, lanes, j, b, chosen, away):
        other = jnp.zeros((CAP, HD), BF16)
        for m in range(3):
            mask = jnp.broadcast_to(chosen[m], (CAP, HD)).astype(BF16)
            other += source[rows_of(away * 3 + m), lanes] * mask
        return jnp.concatenate([source[rows_of(j * 3 + b), lanes], other], axis=0)

    for j in range(HEADS):
        for b in range(3):
            near = rows_of(j * 3 + b)
            away, chosen = pairing(j, b)
            other_fill = jnp.zeros((1, CAP), F32)
            for m in range(3):
                other_fill += fill_row[away * 3 + m][:1] * chosen[m]
            keys = key_side(placed, slice(HD, 2 * HD), j, b, chosen, away)
            key_set[j * 3 + b] = keys
            live = jnp.concatenate([fill_row[j * 3 + b][:1], other_fill], axis=1)
            filled = fill_col[near, :1]
            scores = dot_general(placed[near, :HD], keys, NT)
            scores = jnp.where(live > 0, scores, -1e30)
            top = jnp.max(scores, axis=1, keepdims=True)
            weights = jnp.exp2((scores - top) * (scale * LOG2_E))
            total = jnp.sum(weights, axis=1, keepdims=True) + (1.0 - filled)
            probs_scr[j * 3 + b] = weights * (filled / total)

    def place(kind, src, out, target):
        for i in range(HEADS):
            wait_group(kind, src, out, lax.rem(first + HEADS - i, HEADS), i)
        total = jnp.zeros((ROWS, HD), F32)
        for c in range(HEADS):
            total += dot(put[c], out[c * QUADS : (c + 1) * QUADS].reshape(GROUP, HD))
        target[...] = total.astype(BF16)

    place(VAL, sv, rv, placed_v)
    for j in range(HEADS):
        for b in range(3):
            away, chosen = pairing(j, b)
            vals = key_side(placed_v, slice(0, HD), j, b, chosen, away)
            val_set[j * 3 + b] = vals
            res[rows_of(j * 3 + b), :] = dot(probs_scr[j * 3 + b].astype(BF16), vals).astype(BF16)

    for i in range(HEADS):
        c = lax.rem(first + i, HEADS)
        rows = dot(take[c], res[...]).astype(BF16)
        satt[pl.ds(c * QUADS, QUADS)] = rows.reshape(QUADS, MSG, HD)
        send_group(ATT, satt, ratt, c, i)

    place(GA, sga, rga, placed_g)

    for j in range(HEADS):
        for b in range(3):
            near = rows_of(j * 3 + b)
            keys, vals = key_set[j * 3 + b], val_set[j * 3 + b]
            probs = probs_scr[j * 3 + b]
            grad = placed_g[near, :]
            prob_grad = dot_general(grad, vals, NT)
            inner = jnp.sum(probs * prob_grad, axis=1, keepdims=True)
            score_grad = (probs * (prob_grad - inner)).astype(BF16)
            res_g[near, :HD] = (dot(score_grad, keys) * scale).astype(BF16)
            key_grad = dot_general(score_grad, placed[near, :HD], TN) * scale
            val_grad = dot_general(probs.astype(BF16), grad, TN)
            own[near, :HD] = key_grad[:CAP]
            own[near, HD:] = val_grad[:CAP]
            far[near, :HD] = key_grad[CAP:].astype(BF16)
            far[near, HD:] = val_grad[CAP:].astype(BF16)

    for j in range(HEADS):
        for b in range(3):
            near = rows_of(j * 3 + b)
            away, chosen = pairing(j, b)
            total = own[near, :]
            for m in range(3):
                total += far[rows_of(away * 3 + m), :].astype(F32) * chosen[m]
            res_g[near, HD:] = total.astype(BF16)

    for i in range(HEADS):
        c = lax.rem(first + i, HEADS)
        rows = dot(take[c], res_g[...]).astype(BF16)
        sback[pl.ds(c * QUADS, QUADS)] = rows.reshape(QUADS, MSG, 3 * HD)
        send_group(BACK, sback, rback, c, i)

    for i in range(HEADS):
        wait_group(ATT, satt, ratt, lax.rem(first + HEADS - i, HEADS), i)
    for h in range(HEADS):
        rows = ratt[h * QUADS : (h + 1) * QUADS].reshape(GROUP, HD)
        home = dot(pack_t[h], rows).astype(BF16)
        attn[:, :, h * HD : (h + 1) * HD] = home.reshape(N_HEAD, ROW, HD)

    def attn_half(n):
        return pl.ds(n * (N_HEAD // 2), N_HEAD // 2)

    side = HEADS * HD // 2

    def attn_copy(f, k, n, slot, source):
        _, who = x_peer(k)
        half = attn_half(n)
        cols = pl.ds(f * side, side)
        block = attn_all.at[half, source, :, cols]
        mine = attn.at[half, :, cols] if slot < 2 else block
        return remote(mine, block, a_send.at[f, k // 2, slot], a_recv.at[f, k // 2, slot], who)

    right, left = 1, XN - 1
    for f in range(2):
        attn_copy(f, right, 0, 0, mx).start()
        attn_copy(f, left, 1, 0, mx).start()
        attn_copy(f, right, 1, 1, mx).start()
        attn_copy(f, left, 0, 1, mx).start()
    attn_all[:, mx] = attn[...]
    before_x = lax.rem(mx + XN - 1, XN)
    after_x = lax.rem(mx + 1, XN)
    across_x = lax.rem(mx + 2, XN)
    mixed_rows = attn[...].reshape(TOK, HEADS * HD)
    for n in range(D // step):
        cols = slice(n * step, (n + 1) * step)
        term = dot_general(mixed_rows, proj[cols, :], NT)
        part[:, :, cols] = term.astype(BF16).reshape(N_HEAD, ROW, step)
    for f in range(2):
        attn_copy(f, right, 0, 0, before_x).wait_recv()
        attn_copy(f, right, 0, 2, before_x).start()
        attn_copy(f, left, 1, 0, after_x).wait_recv()
        attn_copy(f, left, 1, 2, after_x).start()
    for k in range(1, N_HEAD):
        h, who = h_peer(k)
        remote(part.at[h], mixed_in.at[hm], m_send.at[h], m_recv.at[hm], who).start()
    mixed_in[hm] = part[hm]
    gather_end(1, gx, gall)

    def at_z(offset):
        return lax.rem(mz + ZN + offset, ZN)

    def partial_of(offset, d):
        grads = gall[:, :, pl.ds(at_z(offset), 1)].reshape(XN * TOK, 128)
        return dot(attn_t[d * side : (d + 1) * side, :], grads)

    hops = {0: -2, 1: -1, 2: 1, 3: -2, 4: -1, 5: 2, 6: 1}

    def tree_copy(d, slot):
        sign = 1 if d == 0 else -1
        who = {"seq": at_z(sign * hops[slot]) * XN + mx}
        return remote(
            gp_part.at[d, slot], gp_in.at[d, slot], p_send.at[d, slot], p_recv.at[d, slot], who
        )

    def tree_send(d, slot, total):
        gp_part[d, slot] = total.astype(BF16)
        tree_copy(d, slot).start()

    for d in range(2):
        sign = 1 if d == 0 else -1
        attn_copy(d, right, 1, 1, before_x).wait_recv()
        attn_copy(d, left, 0, 1, after_x).wait_recv()
        attn_copy(d, right, 0, 2, across_x).wait_recv()
        attn_copy(d, left, 1, 2, across_x).wait_recv()
        cols = slice(d * side, (d + 1) * side)
        for n in range(XN):
            group = attn_all[2 * n : 2 * n + 2, :, :, cols].reshape(TOK, side)
            attn_t[cols, n * TOK : (n + 1) * TOK] = group.T
        for slot, offset in ((0, 4), (1, -3 * sign), (2, 3 * sign)):
            tree_send(d, slot, partial_of(offset, d))
    late = [(d, 1 if d == 0 else -1) for d in range(2)]
    behind = [partial_of(-2 * sign, d) for d, sign in late]
    ahead = [partial_of(2 * sign, d) for d, sign in late]
    mine = [partial_of(0, d) for d, _ in late]
    for d, sign in late:
        tree_copy(d, 2).wait_recv()
        tree_send(d, 5, ahead[d] + gp_in[d, 2].astype(F32))
        tree_copy(d, 0).wait_recv()
        tree_copy(d, 1).wait_recv()
        tree_send(d, 3, behind[d] + gp_in[d, 0].astype(F32) + gp_in[d, 1].astype(F32))
    for d, sign in late:
        tree_send(d, 4, partial_of(-sign, d))
        tree_send(d, 6, partial_of(sign, d))

    for k in range(1, N_HEAD):
        h, who = h_peer(k)
        remote(part.at[h], mixed_in.at[h], m_send.at[h], m_recv.at[h], who).wait()
    total = mixed_in[0].astype(F32)
    for h in range(1, N_HEAD):
        total += mixed_in[h].astype(F32)
    mixed_ref[...] = total.astype(BF16)
    stores = [pltpu.make_async_copy(mixed_ref, mixed_hbm, out_sem.at[0])]
    stores[0].start()

    for i in range(HEADS):
        wait_group(BACK, sback, rback, lax.rem(first + HEADS - i, HEADS), i)
    for h in range(HEADS):
        rows = rback[h * QUADS : (h + 1) * QUADS].reshape(GROUP, 3 * HD)
        home = dot(pack_t[h], rows)
        for n in range(3):
            xf[n, pl.ds(h, TOK, stride=HEADS), :] = home[:, n * HD : (n + 1) * HD]
    for n, out in enumerate((dq_hbm, dk_hbm, dv_hbm)):
        raw[n] = xf[n].astype(BF16)
        stores.append(pltpu.make_async_copy(raw.at[n], out, out_sem.at[n + 1]))
        stores[-1].start()

    for d in range(2):
        total = mine[d]
        for slot in (3, 4, 5, 6):
            tree_copy(d, slot).wait_recv()
            total += gp_in[d, slot].astype(F32)
        gp_ref[:, d * side : (d + 1) * side] = total.T.astype(BF16)
    stores.append(pltpu.make_async_copy(gp_ref, gp_hbm, out_sem.at[4]))
    stores[-1].start()

    for kind, src, out in (
        (ID, sid, rid), (QK, sqk, rqk), (VAL, sv, rv),
        (GA, sga, rga), (ATT, satt, ratt), (BACK, sback, rback),
    ):
        arrivals(kind, src, out, 0, SEQ - 1, first).wait_send()

    for f in range(2):
        attn_copy(f, right, 0, 0, mx).wait_send()
        attn_copy(f, right, 1, 1, mx).wait_send()
        attn_copy(f, right, 0, 2, before_x).wait_send()
        attn_copy(f, left, 1, 0, mx).wait_send()
        attn_copy(f, left, 0, 1, mx).wait_send()
        attn_copy(f, left, 1, 2, after_x).wait_send()
    for d in range(2):
        for slot in range(7):
            tree_copy(d, slot).wait_send()
    for store in stores:
        store.wait()


def layer(*args):
    vmem = pl.BlockSpec(memory_space=pltpu.VMEM)
    dma = pltpu.SemaphoreType.DMA
    wide = HEADS * HD
    flat = jax.ShapeDtypeStruct((TOK * HEADS, HD), BF16)

    def half(*shape):
        return pltpu.VMEM(shape, BF16)

    def full(*shape):
        return pltpu.VMEM(shape, F32)

    return pl.pallas_call(
        layer_kernel,
        out_shape=(
            jax.ShapeDtypeStruct((ROW, D), BF16), flat, flat, flat,
            jax.ShapeDtypeStruct((128, wide), BF16),
        ),
        in_specs=[vmem] * 2 + [pl.BlockSpec(memory_space=pl.ANY)] * 5,
        out_specs=(pl.BlockSpec(memory_space=pl.ANY),) * 5,
        scratch_shapes=[
            half(ROW, D), half(128, wide), dma((5,)),
            half(D, wide), half(3, TOK * HEADS, HD), full(3, TOK * HEADS, HD), half(HEADS, TOK, 3 * HD),
            half(HEADS, GROUP, TOK), half(HEADS, TOK, GROUP),
            half(SEQ, MSG, 2 * HD), half(SEQ, MSG, HD), pltpu.VMEM((SEQ, 1, 128), jnp.int32),
            half(SEQ, MSG, HD), half(SEQ, MSG, HD), half(SEQ, MSG, 3 * HD),
            half(SEQ, MSG, 2 * HD), half(SEQ, MSG, HD), pltpu.VMEM((SEQ, 1, 128), jnp.int32),
            half(SEQ, MSG, HD), half(SEQ, MSG, HD), half(SEQ, MSG, 3 * HD),
            full(TOK, wide), half(N_HEAD, ROW, D),
            half(XN, ZN, ROW, 128), half(XN, ZN, ROW, 128), half(N_HEAD, XN, ZN, ROW, 128),
            half(HEADS, ROWS, GROUP), half(HEADS, GROUP, ROWS),
            full(ROWS, 2 * HD), full(ROWS, 128), full(BLOCKS, 8, CAP),
            half(ROWS, 2 * HD), half(ROWS, HD), half(ROWS, HD),
            half(BLOCKS, 2 * CAP, HD), half(BLOCKS, 2 * CAP, HD),
            full(BLOCKS, CAP, 2 * CAP), full(ROWS, 2 * HD), half(ROWS, 2 * HD),
            half(ROWS, HD), half(ROWS, 3 * HD),
            half(N_HEAD, ROW, wide), half(N_HEAD, XN, ROW, wide), half(wide, XN * TOK),
            half(N_HEAD, ROW, D), half(N_HEAD, ROW, D),
            half(2, 7, wide // 2, 128), half(2, 7, wide // 2, 128),
            dma((5,)), dma((6,)), dma((6, HEADS)), dma((2, 4)), dma((2, 4)), dma((2, 4)), dma((2, 4)),
            dma((XN,)), dma((XN,)), dma((2, 2, 3)), dma((2, 2, 3)),
            dma((N_HEAD,)), dma((N_HEAD,)), dma((2, 7)), dma((2, 7)),
        ],
        compiler_params=pltpu.CompilerParams(
            collective_id=0, has_side_effects=True, vmem_limit_bytes=VMEM_LIMIT
        ),
        name="layer",
    )(*args)


def deliver_kernel(*refs):
    count = len(refs) // 2
    for n in range(count):
        refs[count + n][...] = refs[n][...]


def deliver(*arrays):
    vmem = pl.BlockSpec(memory_space=pltpu.VMEM)
    return pl.pallas_call(
        deliver_kernel,
        out_shape=tuple(jax.ShapeDtypeStruct(a.shape, a.dtype) for a in arrays),
        in_specs=[vmem] * len(arrays),
        out_specs=(vmem,) * len(arrays),
        compiler_params=pltpu.CompilerParams(vmem_limit_bytes=VMEM_LIMIT),
        name="deliver",
    )(*arrays)


def shards(queries, keys_in, values, out_proj, out_grad, slot_index, partner_block):
    flat = (TOK * HEADS, HD)
    mixed, dq, dk, dv, gp = deliver(
        *layer(
            slot_index, partner_block,
            queries.reshape(flat), keys_in.reshape(flat), values.reshape(flat),
            out_grad, out_proj,
        )
    )
    shape = (TOK, HEADS, HD)
    return mixed, dq.reshape(shape), dk.reshape(shape), dv.reshape(shape), gp


def solution(mesh):
    placed = (
        P("seq", "head", None),
        P("seq", "head", None),
        P("seq", "head", None),
        P(None, "head"),
        P(("seq", "head"), None),
        P("head", "seq"),
        P("head", "seq"),
    )
    return jax.shard_map(
        shards,
        mesh=mesh,
        in_specs=placed,
        out_specs=(
            P(("seq", "head"), None),
            P("seq", "head", None),
            P("seq", "head", None),
            P("seq", "head", None),
            P("seq", "head"),
        ),
        check_vma=False,
    )
```

```python
import functools

import jax
import jax.numpy as jnp
from jax import lax
from jax.experimental import pallas as pl
from jax.experimental.pallas import tpu as pltpu
from jax.sharding import PartitionSpec as P

MESH = pl.DeviceIdType.MESH
CAP = 128
HD = 128
HEADS = 4
TOK = 256
SEQ = 32
N_HEAD = 8
OWNED = 384
PER = 12
MSG = HEADS * PER
QUADS = 8
ROWS = SEQ * MSG
BLOCKS = ROWS // CAP
D = 4096
XN = 4
ZN = 8
VMEM_LIMIT = 56 * 1024 * 1024
F32 = jnp.float32
BF16 = jnp.bfloat16


def iota(shape, dim):
    return lax.broadcasted_iota(jnp.int32, shape, dim)


def greet(peers):
    barrier = pltpu.get_barrier_semaphore()
    for peer in peers:
        pl.semaphore_signal(barrier, inc=1, device_id=peer, device_id_type=MESH)


def greeted(count):
    pl.semaphore_wait(pltpu.get_barrier_semaphore(), count)


def remote(src, dst, send_sem, recv_sem, peer):
    return pltpu.make_async_remote_copy(
        src_ref=src,
        dst_ref=dst,
        send_sem=send_sem,
        recv_sem=recv_sem,
        device_id=peer,
        device_id_type=MESH,
    )

NT = (((1,), (1,)), ((), ()))
LOG2_E = 1.4426950408889634
TN = (((0,), (0,)), ((), ()))
ID, QK, VAL, GA, ATT, BACK = range(6)
ROW = TOK // N_HEAD
GROUP = QUADS * MSG


def dot(a, b):
    return jnp.dot(a, b, preferred_element_type=F32)


def dot_general(a, b, dims):
    return lax.dot_general(a, b, dims, preferred_element_type=F32)


def hot(condition):
    return jnp.where(condition, 1.0, 0.0).astype(BF16)


def layer_kernel(
    slot_ref, partner_ref, q_hbm, k_hbm, v_hbm, grad_hbm, proj_hbm,
    mixed_hbm, dq_hbm, dk_hbm, dv_hbm, gp_hbm,
    mixed_ref, gp_ref, out_sem, proj, raw, xf, x, pack, pack_t, sqk, sv, sid, sga, satt, sback, rqk, rv, rid, rga, ratt, rback,
    ga_scr, up, gs, gx, gall, put, take, acc, fill_col, fill_row,
    placed, placed_v, placed_g, key_set, val_set, probs_scr, own, far, res, res_g,
    attn, attn_all, attn_t, part, mixed_in, gp_part, gp_in,
    in_sem, t_send, t_recv, up_send, up_recv, core_send, core_recv,
    gx_send, gx_recv, a_send, a_recv, m_send, m_recv, p_send, p_recv,
):
    me = lax.axis_index("seq")
    hm = lax.axis_index("head")
    mx = lax.rem(me, XN)
    mz = me // XN
    first = me // QUADS
    quad = lax.rem(me, QUADS)
    core = lax.rem(hm, 2)
    my = hm // 2
    sibling = {"head": my * 2 + 1 - core}
    loads = [
        pltpu.make_async_copy(source, target, in_sem.at[n])
        for n, (source, target) in enumerate(
            (
                (q_hbm, raw.at[0]), (k_hbm, raw.at[1]), (v_hbm, raw.at[2]),
                (grad_hbm, up.at[hm]), (proj_hbm, proj),
            )
        )
    ]
    for load in loads:
        load.start()

    def x_peer(k):
        to = lax.rem(mx + k, XN)
        return to, {"seq": mz * XN + to}

    def y_peer(k):
        to = lax.rem(my + k, 4)
        return to, {"head": to * 2 + core}

    def h_peer(k):
        to = lax.rem(hm + k, N_HEAD)
        return to, {"head": to}

    greet(
        [{"seq": lax.rem(me + k, SEQ)} for k in range(1, SEQ)]
        + [h_peer(k)[1] for k in range(1, N_HEAD)]
    )

    def gather_start(kind, src, out):
        for k in (1, 3, 2):
            _, who = y_peer(k)
            remote(src, out.at[hm], up_send.at[kind, k], up_recv.at[kind, my], who).start()
        remote(src, out.at[hm], core_send.at[kind, 0], core_recv.at[kind, my], sibling).start()

    def gather_forward(kind, src, out):
        for k in (1, 3, 2):
            y, who = y_peer(k)
            block = out.at[y * 2 + core]
            remote(src, block, up_send.at[kind, k], up_recv.at[kind, y], who).wait_recv()
            remote(block, block, core_send.at[kind, k], core_recv.at[kind, y], sibling).start()

    def gather_end(kind, src, out):
        for k in range(4):
            y, who = y_peer(k)
            block = out.at[y * 2 + 1 - core]
            remote(src, block, core_send.at[kind, k], core_recv.at[kind, y], sibling).wait()
            if k:
                remote(src, block, up_send.at[kind, k], up_recv.at[kind, y], who).wait_send()

    def send(kind, src, out, to):
        remote(
            src.at[to], out.at[me], t_send.at[kind], t_recv.at[kind, first], {"seq": to}
        ).start()

    def arrivals(kind, src, out, begin, count, group):
        part = pl.ds(begin, count)
        who = {"seq": lax.rem(me + 1, SEQ)}
        return remote(src.at[part], out.at[part], t_send.at[kind], t_recv.at[kind, group], who)

    def members(group, i):
        for k in range(QUADS):
            yield group * QUADS + lax.rem(quad + k, QUADS), i == 0 and k == 0

    def send_group(kind, src, out, group, i):
        for to, mine in members(group, i):
            if mine:
                out[me] = src[me]
            else:
                send(kind, src, out, to)

    def wait_group(kind, src, out, group, i):
        count = QUADS - 1 if i == 0 else QUADS
        arrivals(kind, src, out, group * QUADS, count, group).wait_recv()

    for n in range(3):
        loads[n].wait()
        xf[n] = raw[n].astype(F32)
    for h in range(HEADS):
        for n in range(3):
            x[h, :, n * HD : (n + 1) * HD] = xf[n, pl.ds(h, TOK, stride=HEADS), :].astype(BF16)

    owner_col = iota((SEQ, TOK), 0)
    before_mask = hot(iota((TOK, TOK), 0) < iota((TOK, TOK), 1))
    lane = iota((QUADS, 128), 1)
    lane_row = iota((1, 128), 1)
    quad_col = iota((QUADS, TOK), 0).astype(F32)
    row_col = iota((128, TOK), 0).astype(F32)
    base = ((owner_col % QUADS) * MSG + (owner_col // QUADS) * PER).astype(F32)
    for i in range(HEADS):
        h = lax.rem(first + i, HEADS)
        slots = slot_ref[pl.ds(h, 1), :]
        member = (slots >= owner_col * OWNED) & (slots < (owner_col + 1) * OWNED)
        one = jnp.where(member, 1.0, 0.0)
        before = dot(one.astype(BF16), before_mask)
        rank = jnp.sum(one * before, axis=0, keepdims=True)
        owner = jnp.sum(jnp.where(member, owner_col.astype(F32), 0.0), axis=0, keepdims=True)
        spot = jnp.sum(jnp.where(member, base, 0.0), axis=0, keepdims=True) + rank
        within = slots.astype(F32) - owner * OWNED
        block = jnp.where(within >= CAP, 1.0, 0.0) + jnp.where(within >= 2 * CAP, 1.0, 0.0)
        place = within - block * CAP
        row_part = jnp.floor(owner / QUADS)
        row = row_part * PER + rank
        here = quad_col == owner - row_part * QUADS
        at_row = hot(row_col == row)
        high = dot_general(jnp.where(here, block + 1.0, 0.0).astype(BF16), at_row, NT)
        low = dot_general(jnp.where(here, place, 0.0).astype(BF16), at_row, NT)
        ids = (lane // PER) * OWNED + ((high - 1.0) * CAP + low).astype(jnp.int32)
        ids = jnp.where(high > 0.5, ids, -1)
        pairs = partner_ref[pl.ds(h, 1), :]
        for b in range(3):
            ids = jnp.where(lane == 64 + b, pairs[:, b : b + 1], ids)
        for d in range(QUADS):
            sid[h * QUADS + d] = ids[d : d + 1]
        packing = hot(iota((GROUP, TOK), 0).astype(F32) == spot)
        pack[h] = packing
        packed = dot(packing, x[h]).astype(BF16)
        sqk[pl.ds(h * QUADS, QUADS)] = packed[:, : 2 * HD].reshape(QUADS, MSG, 2 * HD)
        sv[pl.ds(h * QUADS, QUADS)] = packed[:, 2 * HD :].reshape(QUADS, MSG, HD)
        if i == 0:
            greeted(SEQ + N_HEAD - 2)
        send_group(QK, sqk, rqk, h, i)
        send_group(ID, sid, rid, h, i)
        if i == 0:
            loads[3].wait()
            gather_start(0, up.at[hm], up)
    for i in range(HEADS):
        send_group(VAL, sv, rv, lax.rem(first + i, HEADS), i)

    for xx in range(XN):
        for zz in range(ZN):
            chunk = zz * XN + xx
            gs[xx, zz] = up[hm, :, chunk * 128 : (chunk + 1) * 128]
    for k in range(1, XN):
        to, who = x_peer(k)
        remote(gs.at[to], gx.at[mx], gx_send.at[k], gx_recv.at[mx], who).start()
    gx[mx] = gs[mx]
    gather_forward(0, up.at[hm], up)
    for k in range(1, XN):
        xx, who = x_peer(k)
        remote(gs.at[xx], gx.at[xx], gx_send.at[k], gx_recv.at[xx], who).wait()
    gather_start(1, gx, gall)
    gall[hm] = gx[...]
    gather_end(0, up.at[hm], up)
    loads[4].wait()
    step = 512
    for n in range(D // step):
        cols = slice(n * step, (n + 1) * step)
        term = dot(up[:, :, cols].reshape(TOK, step), proj[cols, :])
        if n == 0:
            ga_scr[...] = term
        else:
            ga_scr[...] += term
    for i in range(HEADS):
        h = lax.rem(first + i, HEADS)
        mine = ga_scr[:, pl.ds(pl.multiple_of(h * HD, HD), HD)].astype(BF16)
        sga[pl.ds(h * QUADS, QUADS)] = dot(pack[h], mine).astype(BF16).reshape(QUADS, MSG, HD)
        send_group(GA, sga, rga, h, i)
    gather_forward(1, gx, gall)

    spread = hot(iota((128, GROUP), 0) == iota((128, GROUP), 1) % MSG)
    src_row = iota((QUADS, GROUP), 0) == iota((QUADS, GROUP), 1) // MSG
    pick = hot(iota((GROUP, QUADS), 0) // MSG == iota((GROUP, QUADS), 1))
    own_lane = iota((GROUP, 128), 1) == iota((GROUP, 128), 0) % MSG
    sub = iota((QUADS, 128), 0)
    for i in range(HEADS):
        c = lax.rem(first + HEADS - i, HEADS)
        wait_group(ID, sid, rid, c, i)
        ids = jnp.zeros((QUADS, 128), jnp.int32)
        for d in range(QUADS):
            ids = jnp.where(sub == d, rid[c * QUADS + d], ids)
        high = (ids >> 7).astype(F32).astype(BF16)
        low = (ids & 127).astype(F32).astype(BF16)
        wide = dot(high, spread) * CAP + dot(low, spread)
        ids_row = jnp.sum(jnp.where(src_row, wide, 0.0), axis=0, keepdims=True)
        tall = dot(pick, high) * CAP + dot(pick, low)
        ids_col = jnp.sum(jnp.where(own_lane, tall, 0.0), axis=1, keepdims=True)
        put[c] = hot(iota((ROWS, GROUP), 0).astype(F32) == ids_row)
        take[c] = hot(iota((GROUP, ROWS), 1).astype(F32) == ids_col)
        col = dot(put[c], jnp.ones((GROUP, 128), BF16))
        row = dot(jnp.ones((8, GROUP), BF16), take[c])
        if i == 0:
            fill_col[...] = col
        else:
            fill_col[...] += col
        for b in range(BLOCKS):
            piece = row[:, b * CAP : (b + 1) * CAP]
            if i == 0:
                fill_row[b] = piece
            else:
                fill_row[b] += piece
    for h in range(HEADS):
        pack_t[h] = pack[h].T
    for i in range(HEADS):
        c = lax.rem(first + HEADS - i, HEADS)
        wait_group(QK, sqk, rqk, c, i)
        term = dot(put[c], rqk[pl.ds(c * QUADS, QUADS)].reshape(GROUP, 2 * HD))
        if i == 0:
            acc[...] = term
        elif i < HEADS - 1:
            acc[...] += term
        else:
            placed[...] = (acc[...] + term).astype(BF16)

    scale = HD**-0.5

    def rows_of(b):
        return pl.ds(b * CAP, CAP)

    def pairing(j, b):
        owner = quad + QUADS * j
        partner = rid[owner][:, 64 + b : 65 + b]
        away = (j + 2) % 4
        chosen = [
            jnp.where(partner == (quad + QUADS * away) * 3 + m, 1.0, 0.0) for m in range(3)
        ]
        return away, chosen

    def key_side(source, lanes, j, b, chosen, away):
        other = jnp.zeros((CAP, HD), BF16)
        for m in range(3):
            mask = jnp.broadcast_to(chosen[m], (CAP, HD)).astype(BF16)
            other += source[rows_of(away * 3 + m), lanes] * mask
        return jnp.concatenate([source[rows_of(j * 3 + b), lanes], other], axis=0)

    for j in range(HEADS):
        for b in range(3):
            near = rows_of(j * 3 + b)
            away, chosen = pairing(j, b)
            other_fill = jnp.zeros((1, CAP), F32)
            for m in range(3):
                other_fill += fill_row[away * 3 + m][:1] * chosen[m]
            keys = key_side(placed, slice(HD, 2 * HD), j, b, chosen, away)
            key_set[j * 3 + b] = keys
            live = jnp.concatenate([fill_row[j * 3 + b][:1], other_fill], axis=1)
            filled = fill_col[near, :1]
            scores = dot_general(placed[near, :HD], keys, NT)
            scores = jnp.where(live > 0, scores, -1e30)
            top = jnp.max(scores, axis=1, keepdims=True)
            weights = jnp.exp2((scores - top) * (scale * LOG2_E))
            total = jnp.sum(weights, axis=1, keepdims=True) + (1.0 - filled)
            probs_scr[j * 3 + b] = weights * (filled / total)

    def place(kind, src, out, target):
        for i in range(HEADS):
            wait_group(kind, src, out, lax.rem(first + HEADS - i, HEADS), i)
        total = jnp.zeros((ROWS, HD), F32)
        for c in range(HEADS):
            total += dot(put[c], out[c * QUADS : (c + 1) * QUADS].reshape(GROUP, HD))
        target[...] = total.astype(BF16)

    place(VAL, sv, rv, placed_v)
    for j in range(HEADS):
        for b in range(3):
            away, chosen = pairing(j, b)
            vals = key_side(placed_v, slice(0, HD), j, b, chosen, away)
            val_set[j * 3 + b] = vals
            res[rows_of(j * 3 + b), :] = dot(probs_scr[j * 3 + b].astype(BF16), vals).astype(BF16)

    for i in range(HEADS):
        c = lax.rem(first + i, HEADS)
        rows = dot(take[c], res[...]).astype(BF16)
        satt[pl.ds(c * QUADS, QUADS)] = rows.reshape(QUADS, MSG, HD)
        send_group(ATT, satt, ratt, c, i)

    place(GA, sga, rga, placed_g)

    for j in range(HEADS):
        for b in range(3):
            near = rows_of(j * 3 + b)
            keys, vals = key_set[j * 3 + b], val_set[j * 3 + b]
            probs = probs_scr[j * 3 + b]
            grad = placed_g[near, :]
            prob_grad = dot_general(grad, vals, NT)
            inner = jnp.sum(probs * prob_grad, axis=1, keepdims=True)
            score_grad = (probs * (prob_grad - inner)).astype(BF16)
            res_g[near, :HD] = (dot(score_grad, keys) * scale).astype(BF16)
            key_grad = dot_general(score_grad, placed[near, :HD], TN) * scale
            val_grad = dot_general(probs.astype(BF16), grad, TN)
            own[near, :HD] = key_grad[:CAP]
            own[near, HD:] = val_grad[:CAP]
            far[near, :HD] = key_grad[CAP:].astype(BF16)
            far[near, HD:] = val_grad[CAP:].astype(BF16)

    for j in range(HEADS):
        for b in range(3):
            near = rows_of(j * 3 + b)
            away, chosen = pairing(j, b)
            total = own[near, :]
            for m in range(3):
                total += far[rows_of(away * 3 + m), :].astype(F32) * chosen[m]
            res_g[near, HD:] = total.astype(BF16)

    for i in range(HEADS):
        c = lax.rem(first + i, HEADS)
        rows = dot(take[c], res_g[...]).astype(BF16)
        sback[pl.ds(c * QUADS, QUADS)] = rows.reshape(QUADS, MSG, 3 * HD)
        send_group(BACK, sback, rback, c, i)

    for i in range(HEADS):
        wait_group(ATT, satt, ratt, lax.rem(first + HEADS - i, HEADS), i)
    for h in range(HEADS):
        rows = ratt[h * QUADS : (h + 1) * QUADS].reshape(GROUP, HD)
        home = dot(pack_t[h], rows).astype(BF16)
        attn[:, :, h * HD : (h + 1) * HD] = home.reshape(N_HEAD, ROW, HD)

    def attn_half(n):
        return pl.ds(n * (N_HEAD // 2), N_HEAD // 2)

    side = HEADS * HD // 2

    def attn_copy(f, k, n, slot, source):
        _, who = x_peer(k)
        half = attn_half(n)
        cols = pl.ds(f * side, side)
        block = attn_all.at[half, source, :, cols]
        mine = attn.at[half, :, cols] if slot < 2 else block
        return remote(mine, block, a_send.at[f, k // 2, slot], a_recv.at[f, k // 2, slot], who)

    right, left = 1, XN - 1
    for f in range(2):
        attn_copy(f, right, 0, 0, mx).start()
        attn_copy(f, left, 1, 0, mx).start()
        attn_copy(f, right, 1, 1, mx).start()
        attn_copy(f, left, 0, 1, mx).start()
    attn_all[:, mx] = attn[...]
    before_x = lax.rem(mx + XN - 1, XN)
    after_x = lax.rem(mx + 1, XN)
    across_x = lax.rem(mx + 2, XN)
    mixed_rows = attn[...].reshape(TOK, HEADS * HD)
    for n in range(D // step):
        cols = slice(n * step, (n + 1) * step)
        term = dot_general(mixed_rows, proj[cols, :], NT)
        part[:, :, cols] = term.astype(BF16).reshape(N_HEAD, ROW, step)
    for f in range(2):
        attn_copy(f, right, 0, 0, before_x).wait_recv()
        attn_copy(f, right, 0, 2, before_x).start()
        attn_copy(f, left, 1, 0, after_x).wait_recv()
        attn_copy(f, left, 1, 2, after_x).start()
    for k in range(1, N_HEAD):
        h, who = h_peer(k)
        remote(part.at[h], mixed_in.at[hm], m_send.at[h], m_recv.at[hm], who).start()
    mixed_in[hm] = part[hm]
    gather_end(1, gx, gall)

    def at_z(offset):
        return lax.rem(mz + ZN + offset, ZN)

    def partial_of(offset, d):
        grads = gall[:, :, pl.ds(at_z(offset), 1)].reshape(XN * TOK, 128)
        return dot(attn_t[d * side : (d + 1) * side, :], grads)

    hops = {0: -1, 1: -1, 2: 1, 3: -2, 4: 1, 5: -1, 6: 1}

    def tree_copy(d, slot):
        sign = 1 if d == 0 else -1
        who = {"seq": at_z(sign * hops[slot]) * XN + mx}
        return remote(
            gp_part.at[d, slot], gp_in.at[d, slot], p_send.at[d, slot], p_recv.at[d, slot], who
        )

    def tree_send(d, slot, total):
        gp_part[d, slot] = total.astype(BF16)
        tree_copy(d, slot).start()

    for d in range(2):
        sign = 1 if d == 0 else -1
        attn_copy(d, right, 1, 1, before_x).wait_recv()
        attn_copy(d, left, 0, 1, after_x).wait_recv()
        attn_copy(d, right, 0, 2, across_x).wait_recv()
        attn_copy(d, left, 1, 2, across_x).wait_recv()
        cols = slice(d * side, (d + 1) * side)
        for n in range(XN):
            group = attn_all[2 * n : 2 * n + 2, :, :, cols].reshape(TOK, side)
            attn_t[cols, n * TOK : (n + 1) * TOK] = group.T
        for slot, offset in ((0, 4), (2, 3 * sign), (1, -2 * sign)):
            tree_send(d, slot, partial_of(offset, d))
    late = [(d, 1 if d == 0 else -1) for d in range(2)]
    mine = [partial_of(0, d) for d, _ in late]
    for joins in (((3, -3, (0,)), (4, 2, (2,))), ((5, -1, (1, 3)), (6, 1, (4,)))):
        terms = [[partial_of(offset * sign, d) for _, offset, _ in joins] for d, sign in late]
        for d, sign in late:
            for (slot, _, inputs), total in zip(joins, terms[d]):
                for n in inputs:
                    tree_copy(d, n).wait_recv()
                    total += gp_in[d, n].astype(F32)
                tree_send(d, slot, total)

    for k in range(1, N_HEAD):
        h, who = h_peer(k)
        remote(part.at[h], mixed_in.at[h], m_send.at[h], m_recv.at[h], who).wait()
    total = mixed_in[0].astype(F32)
    for h in range(1, N_HEAD):
        total += mixed_in[h].astype(F32)
    mixed_ref[...] = total.astype(BF16)
    stores = [pltpu.make_async_copy(mixed_ref, mixed_hbm, out_sem.at[0])]
    stores[0].start()

    for i in range(HEADS):
        wait_group(BACK, sback, rback, lax.rem(first + HEADS - i, HEADS), i)
    for h in range(HEADS):
        rows = rback[h * QUADS : (h + 1) * QUADS].reshape(GROUP, 3 * HD)
        home = dot(pack_t[h], rows)
        for n in range(3):
            xf[n, pl.ds(h, TOK, stride=HEADS), :] = home[:, n * HD : (n + 1) * HD]
    for n, out in enumerate((dq_hbm, dk_hbm, dv_hbm)):
        raw[n] = xf[n].astype(BF16)
        stores.append(pltpu.make_async_copy(raw.at[n], out, out_sem.at[n + 1]))
        stores[-1].start()

    for d in range(2):
        total = mine[d]
        for slot in (5, 6):
            tree_copy(d, slot).wait_recv()
            total += gp_in[d, slot].astype(F32)
        gp_ref[:, d * side : (d + 1) * side] = total.T.astype(BF16)
    stores.append(pltpu.make_async_copy(gp_ref, gp_hbm, out_sem.at[4]))
    stores[-1].start()

    for kind, src, out in (
        (ID, sid, rid), (QK, sqk, rqk), (VAL, sv, rv),
        (GA, sga, rga), (ATT, satt, ratt), (BACK, sback, rback),
    ):
        arrivals(kind, src, out, 0, SEQ - 1, first).wait_send()

    for f in range(2):
        attn_copy(f, right, 0, 0, mx).wait_send()
        attn_copy(f, right, 1, 1, mx).wait_send()
        attn_copy(f, right, 0, 2, before_x).wait_send()
        attn_copy(f, left, 1, 0, mx).wait_send()
        attn_copy(f, left, 0, 1, mx).wait_send()
        attn_copy(f, left, 1, 2, after_x).wait_send()
    for d in range(2):
        for slot in range(7):
            tree_copy(d, slot).wait_send()
    for store in stores:
        store.wait()


def layer(*args):
    vmem = pl.BlockSpec(memory_space=pltpu.VMEM)
    dma = pltpu.SemaphoreType.DMA
    wide = HEADS * HD
    flat = jax.ShapeDtypeStruct((TOK * HEADS, HD), BF16)

    def half(*shape):
        return pltpu.VMEM(shape, BF16)

    def full(*shape):
        return pltpu.VMEM(shape, F32)

    return pl.pallas_call(
        layer_kernel,
        out_shape=(
            jax.ShapeDtypeStruct((ROW, D), BF16), flat, flat, flat,
            jax.ShapeDtypeStruct((128, wide), BF16),
        ),
        in_specs=[vmem] * 2 + [pl.BlockSpec(memory_space=pl.ANY)] * 5,
        out_specs=(pl.BlockSpec(memory_space=pl.ANY),) * 5,
        scratch_shapes=[
            half(ROW, D), half(128, wide), dma((5,)),
            half(D, wide), half(3, TOK * HEADS, HD), full(3, TOK * HEADS, HD), half(HEADS, TOK, 3 * HD),
            half(HEADS, GROUP, TOK), half(HEADS, TOK, GROUP),
            half(SEQ, MSG, 2 * HD), half(SEQ, MSG, HD), pltpu.VMEM((SEQ, 1, 128), jnp.int32),
            half(SEQ, MSG, HD), half(SEQ, MSG, HD), half(SEQ, MSG, 3 * HD),
            half(SEQ, MSG, 2 * HD), half(SEQ, MSG, HD), pltpu.VMEM((SEQ, 1, 128), jnp.int32),
            half(SEQ, MSG, HD), half(SEQ, MSG, HD), half(SEQ, MSG, 3 * HD),
            full(TOK, wide), half(N_HEAD, ROW, D),
            half(XN, ZN, ROW, 128), half(XN, ZN, ROW, 128), half(N_HEAD, XN, ZN, ROW, 128),
            half(HEADS, ROWS, GROUP), half(HEADS, GROUP, ROWS),
            full(ROWS, 2 * HD), full(ROWS, 128), full(BLOCKS, 8, CAP),
            half(ROWS, 2 * HD), half(ROWS, HD), half(ROWS, HD),
            half(BLOCKS, 2 * CAP, HD), half(BLOCKS, 2 * CAP, HD),
            full(BLOCKS, CAP, 2 * CAP), full(ROWS, 2 * HD), half(ROWS, 2 * HD),
            half(ROWS, HD), half(ROWS, 3 * HD),
            half(N_HEAD, ROW, wide), half(N_HEAD, XN, ROW, wide), half(wide, XN * TOK),
            half(N_HEAD, ROW, D), half(N_HEAD, ROW, D),
            half(2, 7, wide // 2, 128), half(2, 7, wide // 2, 128),
            dma((5,)), dma((6,)), dma((6, HEADS)), dma((2, 4)), dma((2, 4)), dma((2, 4)), dma((2, 4)),
            dma((XN,)), dma((XN,)), dma((2, 2, 3)), dma((2, 2, 3)),
            dma((N_HEAD,)), dma((N_HEAD,)), dma((2, 7)), dma((2, 7)),
        ],
        compiler_params=pltpu.CompilerParams(
            collective_id=0, has_side_effects=True, vmem_limit_bytes=VMEM_LIMIT
        ),
        name="layer",
    )(*args)


def deliver_kernel(*refs):
    count = len(refs) // 2
    for n in range(count):
        refs[count + n][...] = refs[n][...]


def deliver(*arrays):
    vmem = pl.BlockSpec(memory_space=pltpu.VMEM)
    return pl.pallas_call(
        deliver_kernel,
        out_shape=tuple(jax.ShapeDtypeStruct(a.shape, a.dtype) for a in arrays),
        in_specs=[vmem] * len(arrays),
        out_specs=(vmem,) * len(arrays),
        compiler_params=pltpu.CompilerParams(vmem_limit_bytes=VMEM_LIMIT),
        name="deliver",
    )(*arrays)


def shards(queries, keys_in, values, out_proj, out_grad, slot_index, partner_block):
    flat = (TOK * HEADS, HD)
    mixed, dq, dk, dv, gp = deliver(
        *layer(
            slot_index, partner_block,
            queries.reshape(flat), keys_in.reshape(flat), values.reshape(flat),
            out_grad, out_proj,
        )
    )
    shape = (TOK, HEADS, HD)
    return mixed, dq.reshape(shape), dk.reshape(shape), dv.reshape(shape), gp


def solution(mesh):
    placed = (
        P("seq", "head", None),
        P("seq", "head", None),
        P("seq", "head", None),
        P(None, "head"),
        P(("seq", "head"), None),
        P("head", "seq"),
        P("head", "seq"),
    )
    return jax.shard_map(
        shards,
        mesh=mesh,
        in_specs=placed,
        out_specs=(
            P(("seq", "head"), None),
            P("seq", "head", None),
            P("seq", "head", None),
            P("seq", "head", None),
            P("seq", "head"),
        ),
        check_vma=False,
    )
```
